32 devices in a mesh: blk: 16 (over z, y, x), mp: 2 (over core).
Axes of the slice: x: 2, y: 2, z: 4, core: 2. Of those that a mesh axis runs over, the one named last changes fastest.
Arguments:
- hidden: bfloat16 [144, 3584], replicated, may hold values from -6 to 6
- medusa_w: bfloat16 [2, 3584, 3584], P(None, 'blk', 'mp'), may hold values from -0.09375 to 0.09375
- embedding: bfloat16 [131072, 3584], P(('blk', 'mp')), may hold values from -0.5 to 0.5
- cand_ids: int32 [2, 144, 10], replicated, may hold values from 0 to 131071
- tree_q: bfloat16 [12, 48, 4096], P(None, None, 'mp'), may hold values from -6 to 6
- tree_key_value: bfloat16 [2, 12, 48, 2048], P(None, None, None, 'mp'), may hold values from -6 to 6
- prompt_key_value: bfloat16 [2, 16, 2048, 2048], P(None, 'blk', None, 'mp'), may hold values from -6 to 6
- block_group: int32 [16], P('blk'), may hold values from 0 to 11, as said below
- block_len: int32 [16], P('blk'), may hold values from 1 to 2048
- block_empty: int32 [16], P('blk'), may hold values 0 or 1
- parents: int32 [12, 48], replicated, may hold values from 0 to 46, as said below
- out_weight: bfloat16 [4096, 3584], P('mp'), may hold values from -0.09375 to 0.09375
- post_gain: float32 [3584], replicated, may hold values from 0.5 to 1.5
- resid: bfloat16 [576, 3584], P('blk'), may hold values from -6 to 6
Outputs:
- draft_logprob: float32 [2, 144, 10], replicated
- layer_out: bfloat16 [576, 3584], P('blk')
The draws below stay inside these ranges and needn't reach their ends.
Inputs may be any that keep to these rules, and one draw needn't show every extreme that they name: `block_group`: every group number from 0 to min(12, 16) - 1 owns at least one block. `parents`: entry 0 of each row is 0; entry i for i >= 1 is below i; some group's last token has parent 48 - 2.
All inputs are finite; a program needn't handle non-finite values. No bound on the sum of `block_empty` on one device may be relied on, other than what follows from the above.
Results may differ from the reference program's by a relative error of at most 0.005.
Values may be sent and summed in bfloat16 or wider, within the bound.
No kernel may reach another device: no remote copies, remote signals or barrier semaphores. Data moves between devices by JAX's collectives and lax.ppermute only.
A program may use at most 192 MiB of HBM per device.

```python
import jax
import jax.numpy as jnp
from jax import lax

D = 3584
HQ = 16
KEY_VALUE_HEADS = 8
HEAD_SIZE = 256
VOC = 131072
MEDUSA = 2
TOPC = 10
ROWS = 144
PROMPT_GROUPS = 12
TREE_TOKENS = 48
BLOCK_SLOTS = 2048
PROMPT_BLOCKS = 16
TOKENS = 576


def draw_block_group(key, part):
    column = jnp.arange(PROMPT_BLOCKS, dtype=jnp.int32)
    random_groups = jax.random.randint(key, (PROMPT_BLOCKS,), 0, PROMPT_GROUPS, dtype=jnp.int32)
    groups = jnp.where(column < PROMPT_GROUPS, column, random_groups)
    return jax.random.permutation(jax.random.fold_in(key, 1), groups)


def draw_block_len(key, part):
    lengths = jax.random.randint(key, (PROMPT_BLOCKS,), 1, BLOCK_SLOTS + 1, dtype=jnp.int32)
    lengths = lengths.at[0].set(BLOCK_SLOTS).at[1].set(1)
    return jax.random.permutation(jax.random.fold_in(key, 1), lengths)


def draw_parents(key, part):
    column = jnp.arange(TREE_TOKENS, dtype=jnp.int32)
    upper = jnp.maximum(column, 1)
    picks = jax.random.randint(key, (PROMPT_GROUPS, TREE_TOKENS), 0, upper[None, :], dtype=jnp.int32)
    picks = jnp.where(column[None, :] == 0, 0, picks).astype(jnp.int32)
    return picks.at[0, TREE_TOKENS - 1].set(TREE_TOKENS - 2)


def plant(drawn, own_key, least, largest):
    extent = drawn.shape
    spot = [jax.random.randint(jax.random.fold_in(own_key, axis), (), 0, extent[axis]) for axis in range(len(extent))]
    drawn = drawn.at[tuple(spot)].set(least)
    longest = extent.index(max(extent))
    spot[longest] = (spot[longest] + 1) % extent[longest]
    return drawn.at[tuple(spot)].set(largest)


def levels(stream_key, shape, shards, least, high):
    def one(position, shards_of):
        draws = jax.random.uniform(jax.random.fold_in(jax.random.fold_in(stream_key, 6), position), (shards_of,), jnp.float32, least / len(shards), high / len(shards))
        return jnp.repeat(jnp.exp(draws), shape[position] // shards_of).reshape((-1,) + (1,) * (len(shape) - position - 1))

    level = one(*shards[0])
    for cut in shards[1:]:
        level = level * one(*cut)
    return level


def centred(own_key, extent, scale, most, shards=(), kind=jnp.bfloat16):
    factor_of = levels(own_key, extent, shards, -0.22, 0.18) if shards else 1.0
    entries = jax.random.normal(own_key, extent, jnp.float32) * scale * factor_of
    return jnp.minimum(jnp.maximum(entries, -most), most).astype(kind)


def setup_inputs(seed: int = 0) -> dict:
    key_of = jax.random.split(jax.random.key(seed), 15)
    return {
        "hidden": centred(key_of[0], (ROWS, D), 1.0, 6.0),
        "medusa_w": centred(key_of[1], (MEDUSA, D, D), D ** -0.5, 0.09375, ((1, 16), (2, 2))),
        "embedding": centred(key_of[2], (VOC, D), (D // 25) ** -0.5, 0.5, ((0, 32),)),
        "cand_ids": plant(jax.random.randint(key_of[3], (MEDUSA, ROWS, TOPC), 0, VOC), jax.random.fold_in(key_of[3], 1), 0, VOC - 1).astype(jnp.int32),
        "tree_q": centred(key_of[4], (PROMPT_GROUPS, TREE_TOKENS, HQ * HEAD_SIZE), 1.0, 6.0, ((2, 2),)),
        "tree_key_value": centred(key_of[5], (2, PROMPT_GROUPS, TREE_TOKENS, KEY_VALUE_HEADS * HEAD_SIZE), 1.0, 6.0, ((3, 2),)),
        "prompt_key_value": centred(key_of[6], (2, PROMPT_BLOCKS, BLOCK_SLOTS, KEY_VALUE_HEADS * HEAD_SIZE), 1.0, 6.0, ((1, 16), (3, 2))),
        "block_group": draw_block_group(jax.random.fold_in(key_of[14], 71), 0),
        "block_len": draw_block_len(jax.random.fold_in(key_of[14], 71), 0),
        "block_empty": plant((jax.random.randint(key_of[9], (PROMPT_BLOCKS,), 0, 4) < 1).astype(jnp.int32), jax.random.fold_in(key_of[9], 1), 0, 1),
        "parents": draw_parents(jax.random.fold_in(key_of[14], 71), 0),
        "out_weight": centred(key_of[11], (HQ * HEAD_SIZE, D), (HQ * HEAD_SIZE) ** -0.5, 0.09375, ((0, 2),)),
        "post_gain": jnp.clip(1.0 + 0.1 * jax.random.normal(key_of[12], (D,), jnp.float32), 0.5, 1.5),
        "resid": centred(key_of[13], (TOKENS, D), 1.0, 6.0, ((0, 16),)),
    }


def capped(values, limit):
    return limit * jnp.tanh(values / limit)

def ancestry(parents):
    count = parents.shape[1]
    column = jnp.arange(count, dtype=jnp.int32)
    linked = (parents[:, :, None] == column[None, None, :]) & (column[None, :, None] > 0)
    reach = jnp.eye(count, dtype=jnp.float32)[None] + linked.astype(jnp.float32)
    for sweep in range(count.bit_length()):
        reach = jnp.minimum(jnp.einsum('gij,gjk->gik', reach, reach, precision=lax.Precision.HIGHEST), 1.0)
    return reach

def attend(queries, keys, values, mask):
    rows = queries.shape[0]
    length = keys.shape[0]
    kv_heads = keys.shape[1] // HEAD_SIZE
    repeats = queries.shape[1] // keys.shape[1]
    query_view = queries.astype(jnp.float32).reshape(rows, kv_heads, repeats, HEAD_SIZE)
    key_view = keys.astype(jnp.float32).reshape(length, kv_heads, HEAD_SIZE)
    value_view = values.astype(jnp.float32).reshape(length, kv_heads, HEAD_SIZE)
    scores = jnp.einsum('qhrd,khd->hrqk', query_view, key_view) * HEAD_SIZE ** (-0.5)
    weights = jnp.exp(capped(scores, 50.0)) * mask[None, None]
    denominator = lax.optimization_barrier(jnp.sum(weights, -1)).transpose(2, 0, 1).reshape(rows, kv_heads * repeats)
    rounded = lax.optimization_barrier(weights.astype(jnp.bfloat16)).astype(jnp.float32)
    numerator = jnp.einsum('hrqk,khd->qhrd', rounded, value_view).reshape(rows, kv_heads * repeats * HEAD_SIZE)
    return (numerator, denominator)

def reference(hidden, medusa_w, embedding, cand_ids, tree_q, tree_key_value, prompt_key_value, block_group, block_len, block_empty, parents, out_weight, post_gain, resid):
    results = []
    for head in range(MEDUSA):
        inner = jnp.dot(hidden, medusa_w[head], preferred_element_type=jnp.float32)
        fresh = (hidden.astype(jnp.float32) + jax.nn.silu(inner)).astype(jnp.bfloat16)
        logits = capped(jnp.dot(fresh, embedding.T, preferred_element_type=jnp.float32), 30.0)
        total = lax.optimization_barrier(jnp.sum(jnp.exp(logits), -1))
        picked = jnp.take_along_axis(logits, cand_ids[head], axis=1)
        results.append(picked - jnp.log(total)[:, None])
    draft_logprob = jnp.stack(results)
    positions = jnp.arange(BLOCK_SLOTS, dtype=jnp.int32)
    numer_init = jnp.zeros((PROMPT_GROUPS, TREE_TOKENS, HQ * HEAD_SIZE), jnp.float32)
    denom_init = jnp.zeros((PROMPT_GROUPS, TREE_TOKENS, HQ), jnp.float32)

    def visit(carry, item):
        numer, denom = carry
        keys, values, group, length, empty = item
        queries = lax.dynamic_index_in_dim(tree_q, group, 0, keepdims=False)
        key_ok = ((positions < length) & (empty == 0)).astype(jnp.float32)
        mask = jnp.broadcast_to(key_ok[None, :], (TREE_TOKENS, BLOCK_SLOTS))
        more_numer, more_denom = attend(queries, keys, values, mask)
        numer = lax.dynamic_update_index_in_dim(numer, lax.dynamic_index_in_dim(numer, group, 0, keepdims=False) + more_numer, group, 0)
        denom = lax.dynamic_update_index_in_dim(denom, lax.dynamic_index_in_dim(denom, group, 0, keepdims=False) + more_denom, group, 0)
        return ((numer, denom), None)
    scanned = lax.scan(visit, (numer_init, denom_init), (prompt_key_value[0], prompt_key_value[1], block_group, block_len, block_empty))
    numer, denom = scanned[0]
    reach = ancestry(parents)
    tree_numer, tree_denom = jax.vmap(attend)(tree_q, tree_key_value[0], tree_key_value[1], reach)
    numer = numer + tree_numer
    denom = denom + tree_denom
    heads_out = (numer.reshape(PROMPT_GROUPS, TREE_TOKENS, HQ, HEAD_SIZE) / denom[..., None]).reshape(TOKENS, HQ * HEAD_SIZE).astype(jnp.bfloat16)
    attn = jnp.dot(heads_out, out_weight, preferred_element_type=jnp.float32)
    normed = attn * lax.rsqrt(lax.optimization_barrier(jnp.mean(attn * attn, -1, keepdims=True)) + 1e-06) * post_gain
    layer_out = (normed + resid.astype(jnp.float32)).astype(jnp.bfloat16)
    return (draft_logprob, layer_out)
```

```python
import functools

import jax
import jax.numpy as jnp
from jax import lax
from jax.experimental import pallas as pl
from jax.experimental.pallas import tpu as pltpu
from jax.sharding import PartitionSpec as P

HEAD_SIZE = 256
LANES = 128
MIB = 1 << 20

EXTRA = 16
HIGH, LOW, GROUP = 0, 4, 8


def swap_sum(value, axis, size):
    if size & (size - 1):
        return lax.psum(value, axis)
    step = 1
    while step < size:
        value = value + lax.ppermute(value, axis, [(i, i ^ step) for i in range(size)])
        step *= 2
    return value


def soft_weights(scores):
    return jnp.exp(50.0 * jnp.tanh(scores * (HEAD_SIZE**-0.5 / 50.0)))


def dot_t(left, right):
    return lax.dot_general(left, right, (((1,), (1,)), ((), ())), preferred_element_type=jnp.float32)


def prompt_kernel(tree_size, repeats, width, meta, q_ref, k_ref, v_ref, out_ref):
    group, used, empty = meta[0], meta[1], meta[2]
    limit = jnp.where(empty == 0, used, 0)
    queries = jnp.concatenate(
        [q_ref[0, :, r * HEAD_SIZE : (r + 1) * HEAD_SIZE] for r in range(repeats)], axis=0
    )
    rows = tree_size * repeats
    slots = k_ref.shape[2]
    scores = dot_t(queries, k_ref[0, 0])
    slot = lax.broadcasted_iota(jnp.int32, (rows, slots), 1)
    weights = jnp.where(slot < limit, soft_weights(scores), 0.0)
    denom = jnp.sum(weights, axis=1, keepdims=True)
    numer = jnp.dot(weights.astype(jnp.bfloat16), v_ref[0, 0], preferred_element_type=jnp.float32)
    per_head = HEAD_SIZE // width
    row_id = lax.broadcasted_iota(jnp.int32, (tree_size, width), 0)
    lane_id = lax.broadcasted_iota(jnp.int32, (tree_size, width), 1)
    extra_id = lax.broadcasted_iota(jnp.int32, (EXTRA, width), 0)
    for r in range(repeats):
        mine = jnp.broadcast_to(denom[r * tree_size : (r + 1) * tree_size], (tree_size, width))
        extra = jnp.where(extra_id == GROUP, group.astype(jnp.float32), 0.0)
        for c in range(-(-tree_size // width)):
            line = jnp.sum(
                jnp.where(row_id == lane_id + c * width, mine, 0.0), axis=0, keepdims=True
            )
            high = line.astype(jnp.bfloat16).astype(jnp.float32)
            extra = jnp.where(extra_id == HIGH + c, high, extra)
            extra = jnp.where(extra_id == LOW + c, line - high, extra)
        for part in range(per_head):
            out_ref[r * per_head + part, :tree_size, :] = numer[
                r * tree_size : (r + 1) * tree_size, part * width : (part + 1) * width
            ].astype(jnp.bfloat16)
            out_ref[r * per_head + part, tree_size:, :] = extra.astype(jnp.bfloat16)


def prompt_part(tree_q, prompt_key_value, meta, width, blocks):
    groups, tree_size, features = tree_q.shape
    slots, key_features = prompt_key_value.shape[2:]
    kv_heads = key_features // HEAD_SIZE
    repeats = features // key_features
    per_step = repeats * HEAD_SIZE // width
    return pl.pallas_call(
        functools.partial(prompt_kernel, tree_size, repeats, width),
        out_shape=jax.ShapeDtypeStruct((blocks, tree_size + EXTRA, width), jnp.bfloat16),
        grid_spec=pltpu.PrefetchScalarGridSpec(
            num_scalar_prefetch=1,
            grid=(kv_heads,),
            in_specs=[
                pl.BlockSpec((1, tree_size, repeats * HEAD_SIZE), lambda h, meta: (meta[0], 0, h)),
                pl.BlockSpec((1, 1, slots, HEAD_SIZE), lambda h, meta: (0, 0, 0, h)),
                pl.BlockSpec((1, 1, slots, HEAD_SIZE), lambda h, meta: (1, 0, 0, h)),
            ],
            out_specs=pl.BlockSpec((per_step, tree_size + EXTRA, width), lambda h, meta: (h, 0, 0)),
        ),
        compiler_params=pltpu.CompilerParams(vmem_limit_bytes=24 * MIB),
        cost_estimate=pl.CostEstimate(
            flops=4 * tree_size * features * slots,
            bytes_accessed=4 * slots * key_features,
            transcendentals=2 * tree_size * slots * features // HEAD_SIZE,
        ),
        name="prompt_part",
    )(meta, tree_q, prompt_key_value, prompt_key_value)


def tree_kernel(q_ref, k_ref, v_ref, reach_ref, numer_ref, denom_ref):
    for g in range(q_ref.shape[0]):
        weights = soft_weights(dot_t(q_ref[g], k_ref[g])) * reach_ref[g]
        denom_ref[g] = jnp.broadcast_to(
            jnp.sum(weights, axis=1, keepdims=True), denom_ref.shape[1:]
        )
        numer_ref[g] = jnp.dot(
            weights.astype(jnp.bfloat16), v_ref[g], preferred_element_type=jnp.float32
        )


def tree_part(queries, keys, values, reach):
    shape = values.shape
    return pl.pallas_call(
        tree_kernel,
        out_shape=[jax.ShapeDtypeStruct(shape, jnp.float32)] * 2,
        compiler_params=pltpu.CompilerParams(vmem_limit_bytes=24 * MIB),
        name="tree_part",
    )(queries, keys, values, reach)


def merge_kernel(got_ref, numer_ref, denom_ref, out_ref, hold):
    blocks = got_ref.shape[0]
    groups, tree_size, width = numer_ref.shape
    row_id = lax.broadcasted_iota(jnp.int32, (tree_size, width), 0)
    lane_id = lax.broadcasted_iota(jnp.int32, (tree_size, width), 1)
    lines = -(-tree_size // width)

    @pl.loop(0, groups)
    def _(g):
        def add(b, carry):
            numer, extra = carry
            more = got_ref[b, tree_size:, :].astype(jnp.float32)
            same = more[GROUP : GROUP + 1, :] == g.astype(jnp.float32)
            numer = numer + jnp.where(same, got_ref[b, :tree_size, :].astype(jnp.float32), 0.0)
            extra = extra + jnp.where(same, more, 0.0)
            return numer, extra

        start = (numer_ref[g], jnp.zeros((EXTRA, width), jnp.float32))
        numer, extra = lax.fori_loop(0, blocks, add, start, unroll=True)
        denom = denom_ref[g]
        for c in range(lines):
            line = extra[HIGH + c : HIGH + c + 1, :] + extra[LOW + c : LOW + c + 1, :]
            spread = jnp.where(row_id == lane_id + c * width, line, 0.0)
            denom = denom + jnp.sum(spread, axis=1, keepdims=True)
        hold[pl.ds(pl.multiple_of(g * tree_size, 8), tree_size), :] = numer / denom

    count = out_ref.shape[1]
    for d in range(out_ref.shape[0]):
        out_ref[d] = hold[d * count : (d + 1) * count, :].astype(jnp.bfloat16)


def merge_part(got, numer, denom):
    blocks, _, width = got.shape
    groups, tree_size, _ = numer.shape
    tokens = groups * tree_size
    return pl.pallas_call(
        merge_kernel,
        out_shape=jax.ShapeDtypeStruct((blocks, tokens // blocks, width), jnp.bfloat16),
        scratch_shapes=[pltpu.VMEM((tokens, width), jnp.float32)],
        compiler_params=pltpu.CompilerParams(vmem_limit_bytes=24 * MIB),
        name="merge_part",
    )(got, numer, denom)


def score_kernel(picks, ids_ref, fresh_ref, embed_ref, out_ref, total, picked):
    step = pl.program_id(0)

    @pl.when(step == 0)
    def _():
        total[...] = jnp.zeros_like(total)
        picked[...] = jnp.zeros_like(picked)

    tile = embed_ref.shape[0]
    logits = 30.0 * jnp.tanh(dot_t(fresh_ref[...], embed_ref[...]) * (1.0 / 30.0))
    local = ids_ref[...] - step * tile
    lane = local & (LANES - 1)
    chunk = local >> 7
    sums, found = total[...], picked[...]
    for c in range(tile // LANES):
        part = logits[:, c * LANES : (c + 1) * LANES]
        sums = sums + jnp.exp(part)
        there = jnp.take_along_axis(part, lane, axis=1, mode="promise_in_bounds")
        found = found + jnp.where(chunk == c, there, 0.0)
    total[...] = sums
    picked[...] = found

    @pl.when(step == pl.num_programs(0) - 1)
    def _():
        place = lax.broadcasted_iota(jnp.int32, sums.shape, 1)
        whole = jnp.sum(sums, axis=1, keepdims=True)
        out_ref[...] = jnp.where(place < picks, found, jnp.where(place == picks, whole, 0.0))


def score_part(fresh, embedding, ids, picks):
    rows, depth = fresh.shape
    vocab = embedding.shape[0]
    tile = min(512, vocab)
    return pl.pallas_call(
        functools.partial(score_kernel, picks),
        out_shape=jax.ShapeDtypeStruct((rows, LANES), jnp.float32),
        grid=(vocab // tile,),
        in_specs=[
            pl.BlockSpec((rows, LANES), lambda i: (0, 0)),
            pl.BlockSpec((rows, depth), lambda i: (0, 0)),
            pl.BlockSpec((tile, depth), lambda i: (i, 0)),
        ],
        out_specs=pl.BlockSpec((rows, LANES), lambda i: (0, 0)),
        scratch_shapes=[pltpu.VMEM((rows, LANES), jnp.float32)] * 2,
        compiler_params=pltpu.CompilerParams(vmem_limit_bytes=32 * MIB),
        cost_estimate=pl.CostEstimate(
            flops=2 * rows * depth * vocab,
            bytes_accessed=2 * vocab * depth,
            transcendentals=2 * rows * vocab,
        ),
        name="score_part",
    )(ids, fresh, embedding)


def ancestry(parents):
    count = parents.shape[1]
    column = jnp.arange(count, dtype=jnp.int32)
    linked = (parents[:, :, None] == column[None, None, :]) & (column[None, :, None] > 0)
    reach = jnp.eye(count, dtype=jnp.bfloat16)[None] + linked.astype(jnp.bfloat16)
    for sweep in range(count.bit_length()):
        met = jnp.einsum("gij,gjk->gik", reach, reach, preferred_element_type=jnp.float32)
        reach = jnp.minimum(met, 1.0).astype(jnp.bfloat16)
    return reach.astype(jnp.float32)


def per_device(
    hidden,
    medusa_w,
    embedding,
    cand_ids,
    tree_q,
    tree_key_value,
    prompt_key_value,
    block_group,
    block_len,
    block_empty,
    parents,
    out_weight,
    post_gain,
    resid,
):
    blocks, splits = lax.axis_size("blk"), lax.axis_size("mp")
    blk, mp = lax.axis_index("blk"), lax.axis_index("mp")
    drafts, depth, units = medusa_w.shape
    rows, model = hidden.shape
    lines = drafts * rows
    own = lines // blocks

    hidden_cols = lax.dynamic_slice_in_dim(hidden, blk * depth, depth, 1)
    partial = jnp.einsum("rd,mdu->mru", hidden_cols, medusa_w, preferred_element_type=jnp.float32)
    partial = partial.reshape(blocks, own, units).astype(jnp.bfloat16)
    inner = lax.psum_scatter(partial, "blk", scatter_dimension=0).astype(jnp.float32)
    base = lax.dynamic_slice(hidden, ((blk * own) % rows, mp * units), (own, units))
    fresh = (base.astype(jnp.float32) + jax.nn.silu(inner)).astype(jnp.bfloat16)
    fresh = lax.all_gather(fresh, "blk", axis=0, tiled=True)
    fresh = lax.all_gather(fresh, "mp", axis=1, tiled=True)

    groups, tree_size, features = tree_q.shape
    width = features // blocks
    meta = jnp.concatenate([block_group, block_len, block_empty])
    sent = prompt_part(tree_q, prompt_key_value, meta, width, blocks)
    got = lax.all_to_all(sent, "blk", 0, 0, tiled=True)

    repeats = features // tree_key_value.shape[3]
    column = blk * width
    head = column // HEAD_SIZE
    kv_head = head // repeats
    queries = lax.dynamic_slice_in_dim(tree_q, head * HEAD_SIZE, HEAD_SIZE, 2)
    keys = lax.dynamic_slice_in_dim(tree_key_value[0], kv_head * HEAD_SIZE, HEAD_SIZE, 2)
    values = lax.dynamic_slice_in_dim(
        tree_key_value[1], kv_head * HEAD_SIZE + column % HEAD_SIZE, width, 2
    )
    tree_numer, tree_denom = tree_part(queries, keys, values, ancestry(parents))
    heads_out = merge_part(got, tree_numer, tree_denom)
    heads_out = lax.all_to_all(heads_out, "blk", 0, 0, tiled=True)
    tokens = heads_out.shape[1]
    heads_out = heads_out.transpose(1, 0, 2).reshape(tokens, features)
    attn = swap_sum(jnp.dot(heads_out, out_weight, preferred_element_type=jnp.float32), "mp", splits)
    normed = attn * lax.rsqrt(jnp.mean(attn * attn, -1, keepdims=True) + 1e-06) * post_gain
    layer_out = (normed + resid.astype(jnp.float32)).astype(jnp.bfloat16)

    vocab = embedding.shape[0]
    picks = cand_ids.shape[2]
    ids = cand_ids.reshape(lines, picks) - (blk * splits + mp) * vocab
    ids = jnp.pad(ids, ((0, 0), (0, LANES - picks)), constant_values=-1)
    score = score_part(fresh, embedding, ids, picks)
    payload = score[:, : picks + 1].T.reshape(-1)
    payload = jnp.pad(payload, (0, -payload.shape[0] % 1024)).reshape(-1, LANES)
    spread = jnp.broadcast_to(payload[None], (blocks * splits,) + payload.shape)
    score = jnp.sum(lax.all_to_all(spread, ("blk", "mp"), 0, 0, tiled=True), 0)
    score = score.reshape(-1)[: (picks + 1) * lines].reshape(picks + 1, lines)
    draft_logprob = (score[:picks] - jnp.log(score[picks:])).T.reshape(drafts, rows, picks)
    return (draft_logprob, layer_out)


def solution(mesh):
    placed = (
        P(),
        P(None, "blk", "mp"),
        P(("blk", "mp"), None),
        P(),
        P(None, None, "mp"),
        P(None, None, None, "mp"),
        P(None, "blk", None, "mp"),
        P("blk"),
        P("blk"),
        P("blk"),
        P(),
        P("mp", None),
        P(),
        P("blk", None),
    )
    return jax.shard_map(
        per_device, mesh=mesh, in_specs=placed, out_specs=(P(), P("blk", None)), check_vma=False
    )
```

```python
import functools

import jax
import jax.numpy as jnp
from jax import lax
from jax.experimental import pallas as pl
from jax.experimental.pallas import tpu as pltpu
from jax.sharding import PartitionSpec as P

HEAD_SIZE = 256
LANES = 128
MIB = 1 << 20

EXTRA = 16
HIGH, LOW, GROUP = 0, 4, 8


def soft_weights(scores):
    return jnp.exp(50.0 * jnp.tanh(scores * (HEAD_SIZE**-0.5 / 50.0)))


def dot_t(left, right):
    return lax.dot_general(left, right, (((1,), (1,)), ((), ())), preferred_element_type=jnp.float32)


def prompt_kernel(tree_size, repeats, width, meta, q_ref, k_ref, v_ref, out_ref):
    group, used, empty = meta[0], meta[1], meta[2]
    limit = jnp.where(empty == 0, used, 0)
    queries = jnp.concatenate(
        [q_ref[0, :, r * HEAD_SIZE : (r + 1) * HEAD_SIZE] for r in range(repeats)], axis=0
    )
    rows = tree_size * repeats
    slots = k_ref.shape[2]
    scores = dot_t(queries, k_ref[0, 0])
    slot = lax.broadcasted_iota(jnp.int32, (rows, slots), 1)
    weights = jnp.where(slot < limit, soft_weights(scores), 0.0)
    denom = jnp.sum(weights, axis=1, keepdims=True)
    numer = jnp.dot(weights.astype(jnp.bfloat16), v_ref[0, 0], preferred_element_type=jnp.float32)
    per_head = HEAD_SIZE // width
    row_id = lax.broadcasted_iota(jnp.int32, (tree_size, width), 0)
    lane_id = lax.broadcasted_iota(jnp.int32, (tree_size, width), 1)
    extra_id = lax.broadcasted_iota(jnp.int32, (EXTRA, width), 0)
    for r in range(repeats):
        mine = jnp.broadcast_to(denom[r * tree_size : (r + 1) * tree_size], (tree_size, width))
        extra = jnp.where(extra_id == GROUP, group.astype(jnp.float32), 0.0)
        for c in range(-(-tree_size // width)):
            line = jnp.sum(
                jnp.where(row_id == lane_id + c * width, mine, 0.0), axis=0, keepdims=True
            )
            high = line.astype(jnp.bfloat16).astype(jnp.float32)
            extra = jnp.where(extra_id == HIGH + c, high, extra)
            extra = jnp.where(extra_id == LOW + c, line - high, extra)
        for part in range(per_head):
            out_ref[r * per_head + part, :tree_size, :] = numer[
                r * tree_size : (r + 1) * tree_size, part * width : (part + 1) * width
            ].astype(jnp.bfloat16)
            out_ref[r * per_head + part, tree_size:, :] = extra.astype(jnp.bfloat16)


def prompt_part(tree_q, prompt_key_value, meta, width, blocks):
    groups, tree_size, features = tree_q.shape
    slots, key_features = prompt_key_value.shape[2:]
    kv_heads = key_features // HEAD_SIZE
    repeats = features // key_features
    per_step = repeats * HEAD_SIZE // width
    return pl.pallas_call(
        functools.partial(prompt_kernel, tree_size, repeats, width),
        out_shape=jax.ShapeDtypeStruct((blocks, tree_size + EXTRA, width), jnp.bfloat16),
        grid_spec=pltpu.PrefetchScalarGridSpec(
            num_scalar_prefetch=1,
            grid=(kv_heads,),
            in_specs=[
                pl.BlockSpec((1, tree_size, repeats * HEAD_SIZE), lambda h, meta: (meta[0], 0, h)),
                pl.BlockSpec((1, 1, slots, HEAD_SIZE), lambda h, meta: (0, 0, 0, h)),
                pl.BlockSpec((1, 1, slots, HEAD_SIZE), lambda h, meta: (1, 0, 0, h)),
            ],
            out_specs=pl.BlockSpec((per_step, tree_size + EXTRA, width), lambda h, meta: (h, 0, 0)),
        ),
        compiler_params=pltpu.CompilerParams(vmem_limit_bytes=24 * MIB),
        cost_estimate=pl.CostEstimate(
            flops=4 * tree_size * features * slots,
            bytes_accessed=4 * slots * key_features,
            transcendentals=2 * tree_size * slots * features // HEAD_SIZE,
        ),
        name="prompt_part",
    )(meta, tree_q, prompt_key_value, prompt_key_value)


def tree_kernel(q_ref, k_ref, v_ref, reach_ref, numer_ref, denom_ref):
    for g in range(q_ref.shape[0]):
        weights = soft_weights(dot_t(q_ref[g], k_ref[g])) * reach_ref[g]
        denom_ref[g] = jnp.broadcast_to(
            jnp.sum(weights, axis=1, keepdims=True), denom_ref.shape[1:]
        )
        numer_ref[g] = jnp.dot(
            weights.astype(jnp.bfloat16), v_ref[g], preferred_element_type=jnp.float32
        )


def tree_part(queries, keys, values, reach):
    shape = values.shape
    return pl.pallas_call(
        tree_kernel,
        out_shape=[jax.ShapeDtypeStruct(shape, jnp.float32)] * 2,
        compiler_params=pltpu.CompilerParams(vmem_limit_bytes=24 * MIB),
        name="tree_part",
    )(queries, keys, values, reach)


def merge_kernel(got_ref, numer_ref, denom_ref, out_ref, hold):
    blocks = got_ref.shape[0]
    groups, tree_size, width = numer_ref.shape
    row_id = lax.broadcasted_iota(jnp.int32, (tree_size, width), 0)
    lane_id = lax.broadcasted_iota(jnp.int32, (tree_size, width), 1)
    lines = -(-tree_size // width)

    @pl.loop(0, groups)
    def _(g):
        def add(b, carry):
            numer, extra = carry
            more = got_ref[b, tree_size:, :].astype(jnp.float32)
            same = more[GROUP : GROUP + 1, :] == g.astype(jnp.float32)
            numer = numer + jnp.where(same, got_ref[b, :tree_size, :].astype(jnp.float32), 0.0)
            extra = extra + jnp.where(same, more, 0.0)
            return numer, extra

        start = (numer_ref[g], jnp.zeros((EXTRA, width), jnp.float32))
        numer, extra = lax.fori_loop(0, blocks, add, start, unroll=True)
        denom = denom_ref[g]
        for c in range(lines):
            line = extra[HIGH + c : HIGH + c + 1, :] + extra[LOW + c : LOW + c + 1, :]
            spread = jnp.where(row_id == lane_id + c * width, line, 0.0)
            denom = denom + jnp.sum(spread, axis=1, keepdims=True)
        hold[pl.ds(pl.multiple_of(g * tree_size, 8), tree_size), :] = numer / denom

    count = out_ref.shape[1]
    for d in range(out_ref.shape[0]):
        out_ref[d] = hold[d * count : (d + 1) * count, :].astype(jnp.bfloat16)


def merge_part(got, numer, denom):
    blocks, _, width = got.shape
    groups, tree_size, _ = numer.shape
    tokens = groups * tree_size
    return pl.pallas_call(
        merge_kernel,
        out_shape=jax.ShapeDtypeStruct((blocks, tokens // blocks, width), jnp.bfloat16),
        scratch_shapes=[pltpu.VMEM((tokens, width), jnp.float32)],
        compiler_params=pltpu.CompilerParams(vmem_limit_bytes=24 * MIB),
        name="merge_part",
    )(got, numer, denom)


def score_kernel(picks, count, places, ids_ref, *refs):
    pieces, embed_ref, out_ref = refs[:count], refs[count], refs[count + 1]
    fresh, total, picked = refs[count + 2 :]
    step = pl.program_id(0)

    @pl.when(step == 0)
    def _():
        total[...] = jnp.zeros_like(total)
        picked[...] = jnp.zeros_like(picked)
        for n, piece in enumerate(pieces):
            height, span = piece.shape
            row = pl.multiple_of(places[2 * n] * height, 16)
            col = pl.multiple_of(places[2 * n + 1] * span, LANES)
            fresh[pl.ds(row, height), pl.ds(col, span)] = piece[...]

    tile = embed_ref.shape[0]
    logits = 30.0 * jnp.tanh(dot_t(fresh[...], embed_ref[...]) * (1.0 / 30.0))
    local = ids_ref[...] - step * tile
    lane = local & (LANES - 1)
    chunk = local >> 7
    sums, found = total[...], picked[...]
    for c in range(tile // LANES):
        part = logits[:, c * LANES : (c + 1) * LANES]
        sums = sums + jnp.exp(part)
        there = jnp.take_along_axis(part, lane, axis=1, mode="promise_in_bounds")
        found = found + jnp.where(chunk == c, there, 0.0)
    total[...] = sums
    picked[...] = found

    @pl.when(step == pl.num_programs(0) - 1)
    def _():
        place = lax.broadcasted_iota(jnp.int32, sums.shape, 1)
        whole = jnp.sum(sums, axis=1, keepdims=True)
        both = jnp.where(place < picks, found, jnp.where(place == picks, whole, 0.0))
        out_ref[...] = both.T[: out_ref.shape[0]]


def score_part(pieces, places, embedding, ids, picks):
    rows = ids.shape[0]
    vocab, depth = embedding.shape
    tile = min(512, vocab)
    lines = -(-(picks + 1) // 8) * 8
    return pl.pallas_call(
        functools.partial(score_kernel, picks, len(pieces)),
        out_shape=jax.ShapeDtypeStruct((lines, rows), jnp.float32),
        grid_spec=pltpu.PrefetchScalarGridSpec(
            num_scalar_prefetch=1,
            grid=(vocab // tile,),
            in_specs=[pl.BlockSpec((rows, LANES), lambda i, places: (0, 0))]
            + [pl.BlockSpec(piece.shape, lambda i, places: (0, 0)) for piece in pieces]
            + [pl.BlockSpec((tile, depth), lambda i, places: (i, 0))],
            out_specs=pl.BlockSpec((lines, rows), lambda i, places: (0, 0)),
            scratch_shapes=[pltpu.VMEM((rows, depth), jnp.bfloat16)]
            + [pltpu.VMEM((rows, LANES), jnp.float32)] * 2,
        ),
        compiler_params=pltpu.CompilerParams(vmem_limit_bytes=32 * MIB),
        cost_estimate=pl.CostEstimate(
            flops=2 * rows * depth * vocab,
            bytes_accessed=2 * vocab * depth,
            transcendentals=2 * rows * vocab,
        ),
        name="score_part",
    )(places, ids, *pieces, embedding)


def draft_kernel(meta, hidden_ref, weight_ref, *refs):
    outs, padded = refs[:-1], refs[-1]
    step = pl.program_id(0)
    depth = weight_ref.shape[1]
    window = padded.shape[0]

    @pl.when(step == 0)
    def _():
        padded[...] = jnp.zeros_like(padded)

    padded[pl.ds(pl.multiple_of(meta[1], 16), depth), :] = weight_ref[0]
    columns = hidden_ref[:, pl.ds(pl.multiple_of(meta[0], LANES), window)]
    partial = jnp.dot(columns, padded[...], preferred_element_type=jnp.float32)
    for n, out in enumerate(outs):

        @pl.when(step == n)
        def _():
            out[...] = partial.astype(out.dtype)


def draft_part(hidden, medusa_w, blk):
    rows, model = hidden.shape
    depth, units = medusa_w.shape[1:]
    half = units // 2
    window = -(-depth // LANES) * LANES + LANES
    start = blk * depth
    first = jnp.minimum(start // LANES * LANES, model - window)
    meta = jnp.stack([first, start - first] + [(blk & 3) ^ k for k in range(4)])
    whole = pl.BlockSpec((rows, half), lambda k, meta: (0, 0))
    return pl.pallas_call(
        draft_kernel,
        out_shape=[
            jax.ShapeDtypeStruct((rows, half), jnp.bfloat16 if k else jnp.float32)
            for k in range(4)
        ],
        grid_spec=pltpu.PrefetchScalarGridSpec(
            num_scalar_prefetch=1,
            grid=(4,),
            in_specs=[
                pl.BlockSpec((rows, model), lambda k, meta: (0, 0)),
                pl.BlockSpec(
                    (1, depth, half), lambda k, meta: (meta[2 + k] >> 1, 0, meta[2 + k] & 1)
                ),
            ],
            out_specs=[whole] * 4,
            scratch_shapes=[pltpu.VMEM((window, half), jnp.bfloat16)],
        ),
        compiler_params=pltpu.CompilerParams(vmem_limit_bytes=16 * MIB),
        name="draft_part",
    )(meta, hidden, medusa_w)


def fold_kernel(place, own_ref, *refs):
    got, outs, hold = refs[:3], refs[3:-1], refs[-1]
    total = own_ref[...]
    for one in got:
        total = total + one[...].astype(jnp.float32)
    height = hold.shape[1]
    for j in range(len(outs)):
        hold[j] = total[j * height : (j + 1) * height]
    for k, out in enumerate(outs):
        out[...] = hold[place[0] ^ k].astype(out.dtype)


def fold_part(own, got, place, layers):
    rows, half = own.shape
    height = rows // layers
    spec = pl.BlockSpec(memory_space=pltpu.VMEM)
    return pl.pallas_call(
        fold_kernel,
        out_shape=[
            jax.ShapeDtypeStruct((height, half), jnp.bfloat16 if k else jnp.float32)
            for k in range(layers)
        ],
        in_specs=[pl.BlockSpec(memory_space=pltpu.SMEM)] + [spec] * 4,
        out_specs=[spec] * layers,
        scratch_shapes=[pltpu.VMEM((layers, height, half), jnp.float32)],
        compiler_params=pltpu.CompilerParams(vmem_limit_bytes=16 * MIB),
        name="fold_part",
    )(place, own, *got)


def stack_kernel(place, *refs):
    parts, out_ref, hold, flat = refs[:-3], refs[-3], refs[-2], refs[-1]
    height = hold.shape[1]
    for k, part in enumerate(parts):
        hold[place[0] ^ k] = part[...].astype(jnp.float32)
    for j in range(len(parts)):
        flat[j * height : (j + 1) * height, :] = hold[j]
    out_ref[...] = flat[...].astype(jnp.bfloat16)


def stack_part(parts, place):
    layers = len(parts)
    height, half = parts[0].shape
    spec = pl.BlockSpec(memory_space=pltpu.VMEM)
    return pl.pallas_call(
        stack_kernel,
        out_shape=jax.ShapeDtypeStruct((layers * height, half), jnp.bfloat16),
        in_specs=[pl.BlockSpec(memory_space=pltpu.SMEM)] + [spec] * layers,
        out_specs=spec,
        scratch_shapes=[
            pltpu.VMEM((layers, height, half), jnp.float32),
            pltpu.VMEM((layers * height, half), jnp.float32),
        ],
        compiler_params=pltpu.CompilerParams(vmem_limit_bytes=16 * MIB),
        name="stack_part",
    )(place, *parts)


def partner(value, axis, size, bits):
    return lax.ppermute(value, axis, [(i, i ^ bits) for i in range(size)])


def pair_sum(values):
    while len(values) > 1:
        values = [values[i] + values[i + 1] for i in range(0, len(values), 2)]
    return values[0]


def group_sum(value, axis, size, stride, count):
    return pair_sum(
        [value] + [partner(value, axis, size, k * stride) for k in range(1, count)]
    )


def fresh_by_permutes(hidden, medusa_w, blocks, blk, mp):
    rows, model = hidden.shape
    units = medusa_w.shape[2]
    half = units // 2
    layers = blocks // 4
    height = rows // layers
    layer = blk // 4
    place = layer.reshape(1)
    parts = draft_part(hidden, medusa_w, blk)
    got = [partner(parts[k], "blk", blocks, k) for k in range(1, 4)]
    parts = fold_part(parts[0], got, place, layers)
    inner = parts[0]
    for k in range(1, layers):
        inner = inner + partner(parts[k], "blk", blocks, 4 * k).astype(jnp.float32)
    base = lax.dynamic_slice(
        hidden, (layer * height, mp * units + (blk & 1) * half), (height, half)
    )
    own = (base.astype(jnp.float32) + jax.nn.silu(inner)).astype(jnp.bfloat16)
    chunks = [own] + [partner(own, "blk", blocks, 4 * k) for k in range(1, layers)]
    quad = stack_part(chunks, place)
    pieces = [quad] + [partner(quad, "blk", blocks, k) for k in range(1, 4)]
    pieces = pieces + [partner(piece, "mp", 2, 1) for piece in pieces]
    places = []
    for side in (mp, 1 - mp):
        for k in range(4):
            which = (blk & 3) ^ k
            places += [which >> 1, side * 2 + (which & 1)]
    return pieces, jnp.stack(places)


def fresh_by_collectives(hidden, medusa_w, blocks, blk, mp):
    drafts, depth, units = medusa_w.shape
    rows = hidden.shape[0]
    own = drafts * rows // blocks
    hidden_cols = lax.dynamic_slice_in_dim(hidden, blk * depth, depth, 1)
    partial = jnp.einsum("rd,mdu->mru", hidden_cols, medusa_w, preferred_element_type=jnp.float32)
    partial = partial.reshape(blocks, own, units).astype(jnp.bfloat16)
    inner = lax.psum_scatter(partial, "blk", scatter_dimension=0).astype(jnp.float32)
    base = lax.dynamic_slice(hidden, ((blk * own) % rows, mp * units), (own, units))
    fresh = (base.astype(jnp.float32) + jax.nn.silu(inner)).astype(jnp.bfloat16)
    fresh = lax.all_gather(fresh, "blk", axis=0, tiled=True)
    return [lax.all_gather(fresh, "mp", axis=1, tiled=True)], jnp.zeros((2,), jnp.int32)


def ancestry(parents):
    count = parents.shape[1]
    column = jnp.arange(count, dtype=jnp.int32)
    linked = (parents[:, :, None] == column[None, None, :]) & (column[None, :, None] > 0)
    reach = jnp.eye(count, dtype=jnp.bfloat16)[None] + linked.astype(jnp.bfloat16)
    for sweep in range(count.bit_length()):
        met = jnp.einsum("gij,gjk->gik", reach, reach, preferred_element_type=jnp.float32)
        reach = jnp.minimum(met, 1.0).astype(jnp.bfloat16)
    return reach.astype(jnp.float32)


def per_device(
    hidden,
    medusa_w,
    embedding,
    cand_ids,
    tree_q,
    tree_key_value,
    prompt_key_value,
    block_group,
    block_len,
    block_empty,
    parents,
    out_weight,
    post_gain,
    resid,
):
    blocks, splits = lax.axis_size("blk"), lax.axis_size("mp")
    blk, mp = lax.axis_index("blk"), lax.axis_index("mp")
    drafts, depth, units = medusa_w.shape
    rows, model = hidden.shape
    lines = drafts * rows

    if splits == 2 and blocks % 4 == 0 and units % 256 == 0 and drafts == 2:
        pieces, places = fresh_by_permutes(hidden, medusa_w, blocks, blk, mp)
    else:
        pieces, places = fresh_by_collectives(hidden, medusa_w, blocks, blk, mp)

    groups, tree_size, features = tree_q.shape
    width = features // blocks
    meta = jnp.concatenate([block_group, block_len, block_empty])
    sent = prompt_part(tree_q, prompt_key_value, meta, width, blocks)
    got = lax.all_to_all(sent, "blk", 0, 0, tiled=True)

    repeats = features // tree_key_value.shape[3]
    column = blk * width
    head = column // HEAD_SIZE
    kv_head = head // repeats
    queries = lax.dynamic_slice_in_dim(tree_q, head * HEAD_SIZE, HEAD_SIZE, 2)
    keys = lax.dynamic_slice_in_dim(tree_key_value[0], kv_head * HEAD_SIZE, HEAD_SIZE, 2)
    values = lax.dynamic_slice_in_dim(
        tree_key_value[1], kv_head * HEAD_SIZE + column % HEAD_SIZE, width, 2
    )
    tree_numer, tree_denom = tree_part(queries, keys, values, ancestry(parents))
    heads_out = merge_part(got, tree_numer, tree_denom)
    heads_out = lax.all_to_all(heads_out, "blk", 0, 0, tiled=True)
    tokens = heads_out.shape[1]
    heads_out = heads_out.transpose(1, 0, 2).reshape(tokens, features)
    attn = jnp.dot(heads_out, out_weight, preferred_element_type=jnp.float32)
    attn = group_sum(attn, "mp", splits, 1, splits)
    normed = attn * lax.rsqrt(jnp.mean(attn * attn, -1, keepdims=True) + 1e-06) * post_gain
    layer_out = (normed + resid.astype(jnp.float32)).astype(jnp.bfloat16)

    vocab = embedding.shape[0]
    picks = cand_ids.shape[2]
    ids = cand_ids.reshape(lines, picks) - (blk * splits + mp) * vocab
    ids = jnp.pad(ids, ((0, 0), (0, LANES - picks)), constant_values=-1)
    score = score_part(pieces, places, embedding, ids, picks)
    score = group_sum(score, "mp", splits, 1, splits)
    score = group_sum(score, "blk", blocks, 1, 4)
    score = group_sum(score, "blk", blocks, 4, blocks // 4)
    draft_logprob = score[:picks] - jnp.log(score[picks : picks + 1])
    draft_logprob = draft_logprob.T.reshape(drafts, rows, picks)
    return (draft_logprob, layer_out)


def solution(mesh):
    placed = (
        P(),
        P(None, "blk", "mp"),
        P(("blk", "mp"), None),
        P(),
        P(None, None, "mp"),
        P(None, None, None, "mp"),
        P(None, "blk", None, "mp"),
        P("blk"),
        P("blk"),
        P("blk"),
        P(),
        P("mp", None),
        P(),
        P("blk", None),
    )
    return jax.shard_map(
        per_device, mesh=mesh, in_specs=placed, out_specs=(P(), P("blk", None)), check_vma=False
    )
```

```python
import functools

import jax
import jax.numpy as jnp
from jax import lax
from jax.experimental import pallas as pl
from jax.experimental.pallas import tpu as pltpu
from jax.sharding import PartitionSpec as P

HEAD_SIZE = 256
LANES = 128
MIB = 1 << 20

EXTRA = 16
HIGH, LOW, GROUP = 0, 4, 8


def soft_weights(scores):
    return jnp.exp(50.0 * jnp.tanh(scores * (HEAD_SIZE**-0.5 / 50.0)))


def dot_t(left, right):
    return lax.dot_general(left, right, (((1,), (1,)), ((), ())), preferred_element_type=jnp.float32)


def prompt_kernel(tree_size, repeats, width, meta, q_ref, k_ref, v_ref, out_ref):
    group, used, empty = meta[0], meta[1], meta[2]
    limit = jnp.where(empty == 0, used, 0)
    queries = jnp.concatenate(
        [q_ref[0, :, r * HEAD_SIZE : (r + 1) * HEAD_SIZE] for r in range(repeats)], axis=0
    )
    rows = tree_size * repeats
    slots = k_ref.shape[2]
    scores = dot_t(queries, k_ref[0, 0])
    slot = lax.broadcasted_iota(jnp.int32, (rows, slots), 1)
    weights = jnp.where(slot < limit, soft_weights(scores), 0.0)
    denom = jnp.sum(weights, axis=1, keepdims=True)
    numer = jnp.dot(weights.astype(jnp.bfloat16), v_ref[0, 0], preferred_element_type=jnp.float32)
    per_head = HEAD_SIZE // width
    row_id = lax.broadcasted_iota(jnp.int32, (tree_size, width), 0)
    lane_id = lax.broadcasted_iota(jnp.int32, (tree_size, width), 1)
    extra_id = lax.broadcasted_iota(jnp.int32, (EXTRA, width), 0)
    for r in range(repeats):
        mine = jnp.broadcast_to(denom[r * tree_size : (r + 1) * tree_size], (tree_size, width))
        extra = jnp.where(extra_id == GROUP, group.astype(jnp.float32), 0.0)
        for c in range(-(-tree_size // width)):
            line = jnp.sum(
                jnp.where(row_id == lane_id + c * width, mine, 0.0), axis=0, keepdims=True
            )
            high = line.astype(jnp.bfloat16).astype(jnp.float32)
            extra = jnp.where(extra_id == HIGH + c, high, extra)
            extra = jnp.where(extra_id == LOW + c, line - high, extra)
        for part in range(per_head):
            out_ref[r * per_head + part, :tree_size, :] = numer[
                r * tree_size : (r + 1) * tree_size, part * width : (part + 1) * width
            ].astype(jnp.bfloat16)
            out_ref[r * per_head + part, tree_size:, :] = extra.astype(jnp.bfloat16)


def prompt_part(tree_q, prompt_key_value, meta, width, blocks):
    groups, tree_size, features = tree_q.shape
    slots, key_features = prompt_key_value.shape[2:]
    kv_heads = key_features // HEAD_SIZE
    repeats = features // key_features
    per_step = repeats * HEAD_SIZE // width
    return pl.pallas_call(
        functools.partial(prompt_kernel, tree_size, repeats, width),
        out_shape=jax.ShapeDtypeStruct((blocks, tree_size + EXTRA, width), jnp.bfloat16),
        grid_spec=pltpu.PrefetchScalarGridSpec(
            num_scalar_prefetch=1,
            grid=(kv_heads,),
            in_specs=[
                pl.BlockSpec((1, tree_size, repeats * HEAD_SIZE), lambda h, meta: (meta[0], 0, h)),
                pl.BlockSpec((1, 1, slots, HEAD_SIZE), lambda h, meta: (0, 0, 0, h)),
                pl.BlockSpec((1, 1, slots, HEAD_SIZE), lambda h, meta: (1, 0, 0, h)),
            ],
            out_specs=pl.BlockSpec((per_step, tree_size + EXTRA, width), lambda h, meta: (h, 0, 0)),
        ),
        compiler_params=pltpu.CompilerParams(vmem_limit_bytes=24 * MIB),
        cost_estimate=pl.CostEstimate(
            flops=4 * tree_size * features * slots,
            bytes_accessed=4 * slots * key_features,
            transcendentals=2 * tree_size * slots * features // HEAD_SIZE,
        ),
        name="prompt_part",
    )(meta, tree_q, prompt_key_value, prompt_key_value)


def tree_kernel(meta, q_ref, k_ref, v_ref, reach_ref, numer_ref, denom_ref):
    width = numer_ref.shape[2]
    for g in range(q_ref.shape[0]):
        weights = soft_weights(dot_t(q_ref[g], k_ref[0, g])) * reach_ref[g]
        denom_ref[g] = jnp.broadcast_to(
            jnp.sum(weights, axis=1, keepdims=True), denom_ref.shape[1:]
        )
        numer = jnp.dot(
            weights.astype(jnp.bfloat16), v_ref[0, g], preferred_element_type=jnp.float32
        )
        mine = numer[:, :width]
        for j in range(1, HEAD_SIZE // width):
            mine = jnp.where(meta[2] == j, numer[:, j * width : (j + 1) * width], mine)
        numer_ref[g] = mine


def tree_part(tree_q, tree_key_value, reach, column, width):
    groups, tree_size, features = tree_q.shape
    repeats = features // tree_key_value.shape[3]
    head = column // HEAD_SIZE
    meta = jnp.stack([head, head // repeats, column % HEAD_SIZE // width])
    shape = (groups, tree_size, width)
    block = (1, groups, tree_size, HEAD_SIZE)
    return pl.pallas_call(
        tree_kernel,
        out_shape=[jax.ShapeDtypeStruct(shape, jnp.float32)] * 2,
        grid_spec=pltpu.PrefetchScalarGridSpec(
            num_scalar_prefetch=1,
            grid=(1,),
            in_specs=[
                pl.BlockSpec(block[1:], lambda i, meta: (0, 0, meta[0])),
                pl.BlockSpec(block, lambda i, meta: (0, 0, 0, meta[1])),
                pl.BlockSpec(block, lambda i, meta: (1, 0, 0, meta[1])),
                pl.BlockSpec(reach.shape, lambda i, meta: (0, 0, 0)),
            ],
            out_specs=[pl.BlockSpec(shape, lambda i, meta: (0, 0, 0))] * 2,
        ),
        compiler_params=pltpu.CompilerParams(vmem_limit_bytes=16 * MIB),
        name="tree_part",
    )(meta, tree_q, tree_key_value, tree_key_value, reach)


def merge_kernel(got_ref, numer_ref, denom_ref, out_ref, hold):
    blocks = got_ref.shape[0]
    groups, tree_size, width = numer_ref.shape
    row_id = lax.broadcasted_iota(jnp.int32, (tree_size, width), 0)
    lane_id = lax.broadcasted_iota(jnp.int32, (tree_size, width), 1)
    lines = -(-tree_size // width)

    @pl.loop(0, groups)
    def _(g):
        def add(b, carry):
            numer, extra = carry
            more = got_ref[b, tree_size:, :].astype(jnp.float32)
            same = more[GROUP : GROUP + 1, :] == g.astype(jnp.float32)
            numer = numer + jnp.where(same, got_ref[b, :tree_size, :].astype(jnp.float32), 0.0)
            extra = extra + jnp.where(same, more, 0.0)
            return numer, extra

        start = (numer_ref[g], jnp.zeros((EXTRA, width), jnp.float32))
        numer, extra = lax.fori_loop(0, blocks, add, start, unroll=True)
        denom = denom_ref[g]
        for c in range(lines):
            line = extra[HIGH + c : HIGH + c + 1, :] + extra[LOW + c : LOW + c + 1, :]
            spread = jnp.where(row_id == lane_id + c * width, line, 0.0)
            denom = denom + jnp.sum(spread, axis=1, keepdims=True)
        hold[pl.ds(pl.multiple_of(g * tree_size, 8), tree_size), :] = numer / denom

    count = out_ref.shape[1]
    for d in range(out_ref.shape[0]):
        out_ref[d] = hold[d * count : (d + 1) * count, :].astype(jnp.bfloat16)


def merge_part(got, numer, denom):
    blocks, _, width = got.shape
    groups, tree_size, _ = numer.shape
    tokens = groups * tree_size
    return pl.pallas_call(
        merge_kernel,
        out_shape=jax.ShapeDtypeStruct((blocks, tokens // blocks, width), jnp.bfloat16),
        scratch_shapes=[pltpu.VMEM((tokens, width), jnp.float32)],
        compiler_params=pltpu.CompilerParams(vmem_limit_bytes=24 * MIB),
        name="merge_part",
    )(got, numer, denom)


def score_kernel(picks, side, ids_ref, *refs):
    pieces, embed_ref, out_ref = refs[:-6], refs[-6], refs[-5]
    fresh, total, picked, before = refs[-4:]
    step = pl.program_id(0)
    tile = embed_ref.shape[0]
    span = before.shape[1]
    rows = fresh.shape[0]
    band = 32 if rows % 32 == 0 else rows

    @pl.when(step == 0)
    def _():
        before[...] = jnp.zeros_like(before)
        for n, piece in enumerate(pieces):
            if len(piece.shape) == 2:
                fresh[...] = piece[...]
                continue
            for q in range(4):
                height, wide = piece.shape[1:]
                row = q // 2 * height
                col = pl.multiple_of(((side[0] ^ n) * 2 + q % 2) * wide, LANES)
                fresh[row : row + height, pl.ds(col, wide)] = piece[q]

    def absorb(raw, start, keep=None):
        for r in range(0, rows, band):
            ids = ids_ref[r : r + band] - start
            lane = ids & (LANES - 1)
            chunk = ids >> 7
            sums, found = total[r : r + band], picked[r : r + band]
            for c in range(span // LANES):
                part = jnp.tanh(raw[r : r + band, c * LANES : (c + 1) * LANES] * (1.0 / 30.0))
                sums = sums + jnp.exp(30.0 * part)
                there = jnp.take_along_axis(part, lane, axis=1, mode="promise_in_bounds")
                found = found + jnp.where(chunk == c, there, 0.0)
            if keep is not None:
                sums, found = jnp.where(keep, sums, 0.0), jnp.where(keep, found, 0.0)
            total[r : r + band] = sums
            picked[r : r + band] = found

    base = step * tile
    raw = dot_t(fresh[...], embed_ref[:span])
    absorb(before[...], base - span, step > 0)
    for n in range(1, tile // span):
        more = dot_t(fresh[...], embed_ref[n * span : (n + 1) * span])
        absorb(raw, base + (n - 1) * span)
        raw = more
    before[...] = raw

    @pl.when(step == pl.num_programs(0) - 1)
    def _():
        absorb(before[...], base + tile - span)
        sums, found = total[...], picked[...]
        place = lax.broadcasted_iota(jnp.int32, sums.shape, 1)
        whole = jnp.sum(sums, axis=1, keepdims=True)
        both = jnp.where(place < picks, 30.0 * found, jnp.where(place == picks, whole, 0.0))
        out_ref[...] = both.T[: out_ref.shape[0]]


def score_part(side, pieces, embedding, ids, picks):
    rows = ids.shape[0]
    vocab, depth = embedding.shape
    tile = min(512, vocab)
    span = min(256, tile)
    lines = -(-(picks + 1) // 8) * 8
    return pl.pallas_call(
        functools.partial(score_kernel, picks),
        out_shape=jax.ShapeDtypeStruct((lines, rows), jnp.float32),
        grid_spec=pltpu.PrefetchScalarGridSpec(
            num_scalar_prefetch=1,
            grid=(vocab // tile,),
            in_specs=[pl.BlockSpec((rows, LANES), lambda i, side: (0, 0))]
            + [pl.BlockSpec(piece.shape, lambda i, side, n=piece.ndim: (0,) * n) for piece in pieces]
            + [pl.BlockSpec((tile, depth), lambda i, side: (i, 0))],
            out_specs=pl.BlockSpec((lines, rows), lambda i, side: (0, 0)),
            scratch_shapes=[pltpu.VMEM((rows, depth), jnp.bfloat16)]
            + [pltpu.VMEM((rows, LANES), jnp.float32)] * 2
            + [pltpu.VMEM((rows, span), jnp.float32)],
        ),
        compiler_params=pltpu.CompilerParams(vmem_limit_bytes=28 * MIB),
        cost_estimate=pl.CostEstimate(
            flops=2 * rows * depth * vocab,
            bytes_accessed=2 * vocab * depth,
            transcendentals=2 * rows * vocab,
        ),
        name="score_part",
    )(side, ids, *pieces, embedding)


def draft_kernel(meta, hidden_ref, weight_ref, out_ref, padded):
    depth = weight_ref.shape[1]
    window = padded.shape[0]

    @pl.when((pl.program_id(0) == 0) & (pl.program_id(1) == 0))
    def _():
        padded[...] = jnp.zeros_like(padded)

    padded[pl.ds(pl.multiple_of(meta[1], 16), depth), :] = weight_ref[0]
    columns = hidden_ref[:, pl.ds(pl.multiple_of(meta[0], LANES), window)]
    partial = jnp.dot(columns, padded[...], preferred_element_type=jnp.float32)
    out_ref[0] = partial.astype(jnp.bfloat16)


def draft_part(hidden, medusa_w, blk):
    rows, model = hidden.shape
    depth, units = medusa_w.shape[1:]
    half = units // 2
    window = -(-depth // LANES) * LANES + LANES
    start = blk * depth
    first = jnp.minimum(start // LANES * LANES, model - window)
    meta = jnp.stack([first, start - first])
    return pl.pallas_call(
        draft_kernel,
        out_shape=jax.ShapeDtypeStruct((4, rows, half), jnp.bfloat16),
        grid_spec=pltpu.PrefetchScalarGridSpec(
            num_scalar_prefetch=1,
            grid=(2, 2),
            in_specs=[
                pl.BlockSpec((rows, model), lambda m, c, meta: (0, 0)),
                pl.BlockSpec((1, depth, half), lambda m, c, meta: (m, 0, c)),
            ],
            out_specs=pl.BlockSpec((1, rows, half), lambda m, c, meta: (m * 2 + c, 0, 0)),
            scratch_shapes=[pltpu.VMEM((window, half), jnp.bfloat16)],
        ),
        compiler_params=pltpu.CompilerParams(vmem_limit_bytes=16 * MIB),
        name="draft_part",
    )(meta, hidden, medusa_w)


def in_vmem(kernel, name, out_shape, args, scratch=()):
    spec = pl.BlockSpec(memory_space=pltpu.VMEM)
    return pl.pallas_call(
        kernel,
        out_shape=out_shape,
        in_specs=[spec] * len(args),
        out_specs=spec,
        scratch_shapes=scratch,
        compiler_params=pltpu.CompilerParams(vmem_limit_bytes=16 * MIB),
        name=name,
    )(*args)


def fold_kernel(got_ref, out_ref, hold):
    hold[...] = sum(got_ref[k].astype(jnp.float32) for k in range(got_ref.shape[0]))
    height = out_ref.shape[1]
    for j in range(out_ref.shape[0]):
        out_ref[j] = hold[j * height : (j + 1) * height].astype(jnp.bfloat16)


def silu_kernel(got_ref, base_ref, out_ref):
    inner = sum(got_ref[k].astype(jnp.float32) for k in range(got_ref.shape[0]))
    fresh = base_ref[...].astype(jnp.float32) + inner / (1.0 + jnp.exp(-inner))
    for k in range(out_ref.shape[0]):
        out_ref[k] = fresh.astype(jnp.bfloat16)


def stack_kernel(got_ref, out_ref, hold):
    height = got_ref.shape[1]
    for j in range(got_ref.shape[0]):
        hold[j * height : (j + 1) * height, :] = got_ref[j].astype(jnp.float32)
    for k in range(out_ref.shape[0]):
        out_ref[k] = hold[...].astype(jnp.bfloat16)


PLANE = 4


def plane_groups(blocks):
    return [[base + k for k in range(PLANE)] for base in range(0, blocks, PLANE)]


def layer_groups(blocks):
    return [[base + k for k in range(0, blocks, PLANE)] for base in range(PLANE)]


def exchange(value, axis, groups=None):
    return lax.all_to_all(value, axis, 0, 0, axis_index_groups=groups, tiled=True)


def group_sum(value, axis, size, groups=None):
    if size == 2 and groups is None:
        return value + lax.ppermute(value, axis, [(0, 1), (1, 0)])
    return jnp.sum(exchange(jnp.broadcast_to(value[None], (size,) + value.shape), axis, groups), 0)


def fresh_by_stages(hidden, parts, units, blocks, blk, mp):
    rows = hidden.shape[0]
    half = units // 2
    layers = blocks // PLANE
    height = rows // layers
    planes, columns = plane_groups(blocks), layer_groups(blocks)
    quads = jax.ShapeDtypeStruct((PLANE, rows, half), jnp.bfloat16)
    chunks = jax.ShapeDtypeStruct((layers, height, half), jnp.bfloat16)
    hold = [pltpu.VMEM((rows, half), jnp.float32)]
    base = lax.dynamic_slice(
        hidden, (blk // PLANE * height, mp * units + (blk & 1) * half), (height, half)
    )
    got = exchange(parts, "blk", planes)
    got = exchange(in_vmem(fold_kernel, "fold_part", chunks, [got], hold), "blk", columns)
    got = exchange(in_vmem(silu_kernel, "silu_part", chunks, [got, base]), "blk", columns)
    got = exchange(in_vmem(stack_kernel, "stack_part", quads, [got], hold), "blk", planes)
    other = lax.ppermute(got, "mp", [(0, 1), (1, 0)])
    return [got, other]


def fresh_by_collectives(hidden, medusa_w, blocks, blk, mp):
    drafts, depth, units = medusa_w.shape
    rows = hidden.shape[0]
    own = drafts * rows // blocks
    hidden_cols = lax.dynamic_slice_in_dim(hidden, blk * depth, depth, 1)
    partial = jnp.einsum("rd,mdu->mru", hidden_cols, medusa_w, preferred_element_type=jnp.float32)
    partial = partial.reshape(blocks, own, units).astype(jnp.bfloat16)
    inner = lax.psum_scatter(partial, "blk", scatter_dimension=0).astype(jnp.float32)
    base = lax.dynamic_slice(hidden, ((blk * own) % rows, mp * units), (own, units))
    fresh = (base.astype(jnp.float32) + jax.nn.silu(inner)).astype(jnp.bfloat16)
    fresh = lax.all_gather(fresh, "blk", axis=0, tiled=True)
    return [lax.all_gather(fresh, "mp", axis=1, tiled=True)]


def ancestry(parents):
    count = parents.shape[1]
    column = jnp.arange(count, dtype=jnp.int32)
    linked = (parents[:, :, None] == column[None, None, :]) & (column[None, :, None] > 0)
    reach = jnp.eye(count, dtype=jnp.bfloat16)[None] + linked.astype(jnp.bfloat16)
    for sweep in range(count.bit_length()):
        met = jnp.einsum("gij,gjk->gik", reach, reach, preferred_element_type=jnp.float32)
        reach = jnp.minimum(met, 1.0).astype(jnp.bfloat16)
    return reach.astype(jnp.float32)


def per_device(
    hidden,
    medusa_w,
    embedding,
    cand_ids,
    tree_q,
    tree_key_value,
    prompt_key_value,
    block_group,
    block_len,
    block_empty,
    parents,
    out_weight,
    post_gain,
    resid,
):
    blocks, splits = lax.axis_size("blk"), lax.axis_size("mp")
    blk, mp = lax.axis_index("blk"), lax.axis_index("mp")
    drafts, depth, units = medusa_w.shape
    rows, model = hidden.shape
    lines = drafts * rows

    groups, tree_size, features = tree_q.shape
    width = features // blocks
    meta = jnp.concatenate([block_group, block_len, block_empty])

    if splits == 2 and blocks % PLANE == 0 and units % 256 == 0 and drafts == 2:
        parts = draft_part(hidden, medusa_w, blk)
        parts, meta = lax.optimization_barrier((parts, meta))
        pieces = fresh_by_stages(hidden, parts, units, blocks, blk, mp)
    else:
        pieces = fresh_by_collectives(hidden, medusa_w, blocks, blk, mp)

    sent = prompt_part(tree_q, prompt_key_value, meta, width, blocks)
    got = exchange(sent, "blk")
    tree_numer, tree_denom = tree_part(
        tree_q, tree_key_value, ancestry(parents), blk * width, width
    )
    heads_out = exchange(merge_part(got, tree_numer, tree_denom), "blk")
    tokens = heads_out.shape[1]
    heads_out = heads_out.transpose(1, 0, 2).reshape(tokens, features)
    attn = jnp.dot(heads_out, out_weight, preferred_element_type=jnp.float32)
    attn, pieces = lax.optimization_barrier((attn, pieces))
    attn = group_sum(attn, "mp", splits)
    normed = attn * lax.rsqrt(jnp.mean(attn * attn, -1, keepdims=True) + 1e-06) * post_gain
    layer_out = (normed + resid.astype(jnp.float32)).astype(jnp.bfloat16)

    vocab = embedding.shape[0]
    picks = cand_ids.shape[2]
    ids = cand_ids.reshape(lines, picks) - (blk * splits + mp) * vocab
    ids = jnp.pad(ids, ((0, 0), (0, LANES - picks)), constant_values=-1)
    score = score_part(mp.reshape(1), pieces, embedding, ids, picks)
    score = group_sum(score, "mp", splits)
    score = group_sum(score, "blk", PLANE, plane_groups(blocks))
    score = group_sum(score, "blk", blocks // PLANE, layer_groups(blocks))
    draft_logprob = score[:picks] - jnp.log(score[picks : picks + 1])
    draft_logprob = draft_logprob.T.reshape(drafts, rows, picks)
    return (draft_logprob, layer_out)


def solution(mesh):
    placed = (
        P(),
        P(None, "blk", "mp"),
        P(("blk", "mp"), None),
        P(),
        P(None, None, "mp"),
        P(None, None, None, "mp"),
        P(None, "blk", None, "mp"),
        P("blk"),
        P("blk"),
        P("blk"),
        P(),
        P("mp", None),
        P(),
        P("blk", None),
    )
    return jax.shard_map(
        per_device, mesh=mesh, in_specs=placed, out_specs=(P(), P("blk", None)), check_vma=False
    )
```

```python
import functools

import jax
import jax.numpy as jnp
from jax import lax
from jax.experimental import pallas as pl
from jax.experimental.pallas import tpu as pltpu
from jax.sharding import PartitionSpec as P

HEAD_SIZE = 256
LANES = 128
MIB = 1 << 20

EXTRA = 16
HIGH, LOW, GROUP = 0, 4, 8


def soft_weights(scores):
    return jnp.exp(50.0 * jnp.tanh(scores * (HEAD_SIZE**-0.5 / 50.0)))


def dot_t(left, right):
    return lax.dot_general(left, right, (((1,), (1,)), ((), ())), preferred_element_type=jnp.float32)


def in_hbm():
    return pl.BlockSpec(memory_space=pltpu.HBM)


def pin(value):
    return pltpu.with_memory_space_constraint(value, pltpu.HBM)


def in_vmem():
    return pl.BlockSpec(memory_space=pltpu.VMEM)


def in_smem():
    return pl.BlockSpec(memory_space=pltpu.SMEM)


def limit(mib):
    return pltpu.CompilerParams(vmem_limit_bytes=mib * MIB)


def prompt_kernel(meta, q_hbm, kv_hbm, out_ref, queries, held, sems):
    group, used, empty = meta[0], meta[1], meta[2]
    last = jnp.where(empty == 0, used, 0)
    kv_heads, slots = held.shape[1:3]
    tree_size, features = queries.shape
    repeats = features // HEAD_SIZE // kv_heads
    width = out_ref.shape[2]
    rows = tree_size * repeats
    ask = pltpu.make_async_copy(q_hbm.at[group], queries, sems.at[2 * kv_heads])
    ask.start()
    copies = []
    for h in range(kv_heads):
        for s in range(2):
            columns = pl.ds(h * HEAD_SIZE, HEAD_SIZE)
            copies.append(
                pltpu.make_async_copy(
                    kv_hbm.at[s, 0, :, columns], held.at[s, h], sems.at[2 * h + s]
                )
            )
            copies[-1].start()
    ask.wait()
    per_head = HEAD_SIZE // width
    row_id = lax.broadcasted_iota(jnp.int32, (tree_size, width), 0)
    lane_id = lax.broadcasted_iota(jnp.int32, (tree_size, width), 1)
    extra_id = lax.broadcasted_iota(jnp.int32, (EXTRA, width), 0)
    slot = lax.broadcasted_iota(jnp.int32, (rows, slots), 1)
    for h in range(kv_heads):
        asked = jnp.concatenate(
            [
                queries[:, (h * repeats + r) * HEAD_SIZE : (h * repeats + r + 1) * HEAD_SIZE]
                for r in range(repeats)
            ],
            axis=0,
        )
        copies[2 * h].wait()
        scores = dot_t(asked, held[0, h])
        weights = jnp.where(slot < last, soft_weights(scores), 0.0)
        denom = jnp.sum(weights, axis=1, keepdims=True)
        copies[2 * h + 1].wait()
        numer = jnp.dot(
            weights.astype(jnp.bfloat16), held[1, h], preferred_element_type=jnp.float32
        )
        for r in range(repeats):
            mine = jnp.broadcast_to(denom[r * tree_size : (r + 1) * tree_size], (tree_size, width))
            extra = jnp.where(extra_id == GROUP, group.astype(jnp.float32), 0.0)
            for c in range(-(-tree_size // width)):
                line = jnp.sum(
                    jnp.where(row_id == lane_id + c * width, mine, 0.0), axis=0, keepdims=True
                )
                high = line.astype(jnp.bfloat16).astype(jnp.float32)
                extra = jnp.where(extra_id == HIGH + c, high, extra)
                extra = jnp.where(extra_id == LOW + c, line - high, extra)
            for part in range(per_head):
                d = (h * repeats + r) * per_head + part
                out_ref[d, :tree_size, :] = numer[
                    r * tree_size : (r + 1) * tree_size, part * width : (part + 1) * width
                ].astype(jnp.bfloat16)
                out_ref[d, tree_size:, :] = extra.astype(jnp.bfloat16)


def prompt_part(tree_q, prompt_key_value, meta, width, blocks):
    groups, tree_size, features = tree_q.shape
    slots, key_features = prompt_key_value.shape[2:]
    kv_heads = key_features // HEAD_SIZE
    return pl.pallas_call(
        prompt_kernel,
        out_shape=jax.ShapeDtypeStruct((blocks, tree_size + EXTRA, width), jnp.bfloat16),
        in_specs=[in_smem(), in_hbm(), in_hbm()],
        out_specs=in_vmem(),
        scratch_shapes=[
            pltpu.VMEM((tree_size, features), jnp.bfloat16),
            pltpu.VMEM((2, kv_heads, slots, HEAD_SIZE), jnp.bfloat16),
            pltpu.SemaphoreType.DMA((2 * kv_heads + 1,)),
        ],
        compiler_params=limit(24),
        cost_estimate=pl.CostEstimate(
            flops=4 * tree_size * features * slots,
            bytes_accessed=4 * slots * key_features,
            transcendentals=2 * tree_size * slots * features // HEAD_SIZE,
        ),
        name="prompt_part",
    )(meta, pin(tree_q), pin(prompt_key_value))


def tree_kernel(meta, q_hbm, kv_hbm, reach_ref, numer_ref, denom_ref, held, sems):
    width = numer_ref.shape[2]
    query_columns = pl.ds(pl.multiple_of(meta[0] * HEAD_SIZE, HEAD_SIZE), HEAD_SIZE)
    key_columns = pl.ds(pl.multiple_of(meta[1] * HEAD_SIZE, HEAD_SIZE), HEAD_SIZE)
    copies = [
        pltpu.make_async_copy(q_hbm.at[:, :, query_columns], held.at[0], sems.at[0]),
        pltpu.make_async_copy(kv_hbm.at[0, :, :, key_columns], held.at[1], sems.at[1]),
        pltpu.make_async_copy(kv_hbm.at[1, :, :, key_columns], held.at[2], sems.at[2]),
    ]
    for copy in copies:
        copy.start()
    for copy in copies:
        copy.wait()
    for g in range(held.shape[1]):
        weights = soft_weights(dot_t(held[0, g], held[1, g])) * reach_ref[g]
        denom_ref[g] = jnp.broadcast_to(
            jnp.sum(weights, axis=1, keepdims=True), denom_ref.shape[1:]
        )
        numer = jnp.dot(
            weights.astype(jnp.bfloat16), held[2, g], preferred_element_type=jnp.float32
        )
        mine = numer[:, :width]
        for j in range(1, HEAD_SIZE // width):
            mine = jnp.where(meta[2] == j, numer[:, j * width : (j + 1) * width], mine)
        numer_ref[g] = mine


def tree_part(tree_q, tree_key_value, reach, column, width):
    groups, tree_size, features = tree_q.shape
    repeats = features // tree_key_value.shape[3]
    head = column // HEAD_SIZE
    meta = jnp.stack([head, head // repeats, column % HEAD_SIZE // width])
    return pl.pallas_call(
        tree_kernel,
        out_shape=[jax.ShapeDtypeStruct((groups, tree_size, width), jnp.float32)] * 2,
        in_specs=[in_smem(), in_hbm(), in_hbm(), in_vmem()],
        out_specs=[in_vmem()] * 2,
        scratch_shapes=[
            pltpu.VMEM((3, groups, tree_size, HEAD_SIZE), jnp.bfloat16),
            pltpu.SemaphoreType.DMA((3,)),
        ],
        compiler_params=limit(16),
        name="tree_part",
    )(meta, pin(tree_q), pin(tree_key_value), reach)


def merge_kernel(got_ref, numer_ref, denom_ref, out_ref, hold):
    blocks = got_ref.shape[0]
    groups, tree_size, width = numer_ref.shape
    row_id = lax.broadcasted_iota(jnp.int32, (tree_size, width), 0)
    lane_id = lax.broadcasted_iota(jnp.int32, (tree_size, width), 1)
    lines = -(-tree_size // width)

    @pl.loop(0, groups)
    def _(g):
        def add(b, carry):
            numer, extra = carry
            more = got_ref[b, tree_size:, :].astype(jnp.float32)
            same = more[GROUP : GROUP + 1, :] == g.astype(jnp.float32)
            numer = numer + jnp.where(same, got_ref[b, :tree_size, :].astype(jnp.float32), 0.0)
            extra = extra + jnp.where(same, more, 0.0)
            return numer, extra

        start = (numer_ref[g], jnp.zeros((EXTRA, width), jnp.float32))
        numer, extra = lax.fori_loop(0, blocks, add, start, unroll=True)
        denom = denom_ref[g]
        for c in range(lines):
            line = extra[HIGH + c : HIGH + c + 1, :] + extra[LOW + c : LOW + c + 1, :]
            spread = jnp.where(row_id == lane_id + c * width, line, 0.0)
            denom = denom + jnp.sum(spread, axis=1, keepdims=True)
        hold[pl.ds(pl.multiple_of(g * tree_size, 8), tree_size), :] = numer / denom

    count = out_ref.shape[1]
    for d in range(out_ref.shape[0]):
        out_ref[d] = hold[d * count : (d + 1) * count, :].astype(jnp.bfloat16)


def merge_part(got, numer, denom):
    blocks, _, width = got.shape
    groups, tree_size, _ = numer.shape
    tokens = groups * tree_size
    return pl.pallas_call(
        merge_kernel,
        out_shape=jax.ShapeDtypeStruct((blocks, tokens // blocks, width), jnp.bfloat16),
        scratch_shapes=[pltpu.VMEM((tokens, width), jnp.float32)],
        compiler_params=limit(16),
        name="merge_part",
    )(got, numer, denom)


def project_kernel(heads_ref, weight_hbm, out_ref, ring, sems):
    slots, span = ring.shape[:2]
    steps = weight_hbm.shape[0] // span
    per_step = span // heads_ref.shape[2]

    def copy(i):
        return pltpu.make_async_copy(
            weight_hbm.at[i * span : (i + 1) * span], ring.at[i % slots], sems.at[i % slots]
        )

    for i in range(min(slots, steps)):
        copy(i).start()
    for i in range(steps):
        left = jnp.concatenate([heads_ref[i * per_step + j] for j in range(per_step)], axis=1)
        copy(i).wait()
        more = jnp.dot(left, ring[i % slots], preferred_element_type=jnp.float32)
        out_ref[...] = more if i == 0 else out_ref[...] + more
        if i + slots < steps:
            copy(i + slots).start()


def project_part(heads_out, out_weight):
    blocks, tokens, width = heads_out.shape
    features, model = out_weight.shape
    if width % LANES or features % HEAD_SIZE:
        flat = heads_out.transpose(1, 0, 2).reshape(tokens, features)
        return jnp.dot(flat, out_weight, preferred_element_type=jnp.float32)
    slots = 4
    return pl.pallas_call(
        project_kernel,
        out_shape=jax.ShapeDtypeStruct((tokens, model), jnp.float32),
        in_specs=[in_vmem(), in_hbm()],
        out_specs=in_vmem(),
        scratch_shapes=[
            pltpu.VMEM((slots, HEAD_SIZE, model), jnp.bfloat16),
            pltpu.SemaphoreType.DMA((slots,)),
        ],
        compiler_params=limit(20),
        cost_estimate=pl.CostEstimate(
            flops=2 * tokens * features * model,
            bytes_accessed=2 * features * model,
            transcendentals=0,
        ),
        name="project_part",
    )(heads_out, pin(out_weight))


def score_kernel(picks, places, ids_ref, *refs):
    pieces, (embed_hbm, out_ref) = refs[:-8], refs[-8:-6]
    fresh, total, picked, raw, ring, sems = refs[-6:]
    slots, span = ring.shape[:2]
    rows = fresh.shape[0]
    chunks = embed_hbm.shape[0] // span
    band = 32 if rows % 32 == 0 else rows

    def copy(c):
        start = pl.multiple_of(c * span, span)
        return pltpu.make_async_copy(
            embed_hbm.at[pl.ds(start, span)], ring.at[c % slots], sems.at[c % slots]
        )

    def product(c):
        copy(c).wait()
        return dot_t(fresh[...], ring[c % slots])

    def refill(c):
        @pl.when(c + slots < chunks)
        def _():
            copy(c + slots).start()

    def absorb(side, start, keep=None):
        for r in range(0, rows, band):
            ids = ids_ref[r : r + band] - start
            lane = ids & (LANES - 1)
            chunk = ids >> 7
            sums, found = total[r : r + band], picked[r : r + band]
            for c in range(span // LANES):
                part = raw[side, r : r + band, c * LANES : (c + 1) * LANES]
                part = jnp.tanh(part * (1.0 / 30.0))
                sums = sums + jnp.exp(30.0 * part)
                there = jnp.take_along_axis(part, lane, axis=1, mode="promise_in_bounds")
                found = found + jnp.where(chunk == c, there, 0.0)
            if keep is not None:
                sums, found = jnp.where(keep, sums, 0.0), jnp.where(keep, found, 0.0)
            total[r : r + band] = sums
            picked[r : r + band] = found

    for c in range(min(slots, chunks)):
        copy(c).start()
    raw[1] = jnp.zeros(raw.shape[1:], jnp.float32)
    total[...] = jnp.zeros_like(total)
    picked[...] = jnp.zeros_like(picked)
    for n, piece in enumerate(pieces):
        height, wide = piece.shape
        row = pl.multiple_of(places[2 * n] * height, 16)
        col = pl.multiple_of(places[2 * n + 1] * wide, LANES)
        fresh[pl.ds(row, height), pl.ds(col, wide)] = piece[...]

    @pl.loop(0, chunks // 2)
    def _(pair):
        first = 2 * pair
        more = product(first)
        absorb(1, (first - 1) * span, pair > 0)
        raw[0] = more
        refill(first)
        more = product(first + 1)
        absorb(0, first * span)
        raw[1] = more
        refill(first + 1)

    absorb(1, (chunks - 1) * span)
    place = lax.broadcasted_iota(jnp.int32, total.shape, 1)
    whole = jnp.sum(total[...], axis=1, keepdims=True)
    both = jnp.where(place < picks, 30.0 * picked[...], jnp.where(place == picks, whole, 0.0))
    out_ref[...] = both.T[: out_ref.shape[0]]


def score_part(places, pieces, embedding, ids, picks):
    rows = ids.shape[0]
    vocab, depth = embedding.shape
    span, slots = HEAD_SIZE, 4
    lines = -(-(picks + 1) // 8) * 8
    return pl.pallas_call(
        functools.partial(score_kernel, picks),
        out_shape=jax.ShapeDtypeStruct((lines, rows), jnp.float32),
        in_specs=[in_smem()] + [in_vmem()] * (1 + len(pieces)) + [in_hbm()],
        out_specs=in_vmem(),
        scratch_shapes=[
            pltpu.VMEM((rows, depth), jnp.bfloat16),
            pltpu.VMEM((rows, LANES), jnp.float32),
            pltpu.VMEM((rows, LANES), jnp.float32),
            pltpu.VMEM((2, rows, span), jnp.float32),
            pltpu.VMEM((slots, span, depth), jnp.bfloat16),
            pltpu.SemaphoreType.DMA((slots,)),
        ],
        compiler_params=limit(24),
        cost_estimate=pl.CostEstimate(
            flops=2 * rows * depth * vocab,
            bytes_accessed=2 * vocab * depth,
            transcendentals=2 * rows * vocab,
        ),
        name="score_part",
    )(places, ids, *pieces, pin(embedding))


def draft_kernel(meta, hidden_hbm, weight_hbm, *refs):
    outs, columns, padded, sems = refs[:4], *refs[4:]
    depth = weight_hbm.shape[1]
    half = padded.shape[2]
    window = padded.shape[1]
    first = pl.multiple_of(meta[0], LANES)
    ask = pltpu.make_async_copy(hidden_hbm.at[:, pl.ds(first, window)], columns, sems.at[4])
    ask.start()
    padded[...] = jnp.zeros_like(padded)
    copies = []
    for k in (1, 2, 3, 0):
        quad = meta[2 + k]
        col = pl.multiple_of((quad & 1) * half, LANES)
        copies.append(
            pltpu.make_async_copy(
                weight_hbm.at[quad >> 1, :, pl.ds(col, half)],
                padded.at[k, pl.ds(pl.multiple_of(meta[1], 16), depth)],
                sems.at[k],
            )
        )
        copies[-1].start()
    ask.wait()
    for n, k in enumerate((1, 2, 3, 0)):
        copies[n].wait()
        partial = jnp.dot(columns[...], padded[k], preferred_element_type=jnp.float32)
        outs[k][...] = partial.astype(outs[k].dtype)


def draft_part(hidden, medusa_w, blk):
    rows, model = hidden.shape
    depth, units = medusa_w.shape[1:]
    half = units // 2
    window = -(-depth // LANES) * LANES + LANES
    start = blk * depth
    first = jnp.minimum(start // LANES * LANES, model - window)
    meta = jnp.stack([first, start - first] + [(blk & 3) ^ k for k in range(4)])
    return pl.pallas_call(
        draft_kernel,
        out_shape=[
            jax.ShapeDtypeStruct((rows, half), jnp.bfloat16 if k else jnp.float32)
            for k in range(4)
        ],
        in_specs=[in_smem(), in_hbm(), in_hbm()],
        out_specs=[in_vmem()] * 4,
        scratch_shapes=[
            pltpu.VMEM((rows, window), jnp.bfloat16),
            pltpu.VMEM((4, window, half), jnp.bfloat16),
            pltpu.SemaphoreType.DMA((5,)),
        ],
        compiler_params=limit(16),
        name="draft_part",
    )(meta, pin(hidden), pin(medusa_w))


def fold_kernel(place, own_ref, *refs):
    got, outs, hold = refs[:3], refs[3:-1], refs[-1]
    total = own_ref[...]
    for one in got:
        total = total + one[...].astype(jnp.float32)
    height = hold.shape[1]
    for j in range(len(outs)):
        hold[j] = total[j * height : (j + 1) * height]
    for k, out in enumerate(outs):
        out[...] = hold[place[0] ^ k].astype(out.dtype)


def fold_part(own, got, place, layers):
    rows, half = own.shape
    height = rows // layers
    return pl.pallas_call(
        fold_kernel,
        out_shape=[
            jax.ShapeDtypeStruct((height, half), jnp.bfloat16 if k else jnp.float32)
            for k in range(layers)
        ],
        in_specs=[in_smem()] + [in_vmem()] * 4,
        out_specs=[in_vmem()] * layers,
        scratch_shapes=[pltpu.VMEM((layers, height, half), jnp.float32)],
        compiler_params=limit(16),
        name="fold_part",
    )(place, own, *got)


def stack_kernel(place, *refs):
    parts, out_ref, hold, flat = refs[:-3], refs[-3], refs[-2], refs[-1]
    height = hold.shape[1]
    for k, part in enumerate(parts):
        hold[place[0] ^ k] = part[...].astype(jnp.float32)
    for j in range(len(parts)):
        flat[j * height : (j + 1) * height, :] = hold[j]
    out_ref[...] = flat[...].astype(jnp.bfloat16)


def stack_part(parts, place):
    layers = len(parts)
    height, half = parts[0].shape
    return pl.pallas_call(
        stack_kernel,
        out_shape=jax.ShapeDtypeStruct((layers * height, half), jnp.bfloat16),
        in_specs=[in_smem()] + [in_vmem()] * layers,
        out_specs=in_vmem(),
        scratch_shapes=[
            pltpu.VMEM((layers, height, half), jnp.float32),
            pltpu.VMEM((layers * height, half), jnp.float32),
        ],
        compiler_params=limit(16),
        name="stack_part",
    )(place, *parts)


def partner(value, axis, size, bits):
    return lax.ppermute(value, axis, [(i, i ^ bits) for i in range(size)])


def total_sum(value, sizes):
    for axis, size in sizes:
        step = 1
        while step < size:
            value = value + partner(value, axis, size, step)
            step *= 2
    return value


def both_by_stages(hidden, parts, units, blocks, blk, mp, prompt, merge):
    rows, model = hidden.shape
    half = units // 2
    layers = blocks // 4
    height = rows // layers
    layer = blk // 4
    place = layer.reshape(1)
    got = [partner(parts[k], "blk", blocks, k) for k in range(1, 4)]
    got, sent = lax.optimization_barrier((got, prompt()))
    parts = fold_part(parts[0], got, place, layers)
    more = [partner(parts[k], "blk", blocks, 4 * k) for k in range(1, layers)]
    more, partials = lax.optimization_barrier((more, spread(sent)))
    inner = parts[0] + sum(one.astype(jnp.float32) for one in more)
    base = lax.dynamic_slice(
        hidden, (layer * height, mp * units + (blk & 1) * half), (height, half)
    )
    own = (base.astype(jnp.float32) + jax.nn.silu(inner)).astype(jnp.bfloat16)
    chunks = [own] + [partner(own, "blk", blocks, 4 * k) for k in range(1, layers)]
    chunks, heads_out = lax.optimization_barrier((chunks, merge(partials)))
    quad = stack_part(chunks, place)
    pieces = [quad] + [partner(quad, "blk", blocks, k) for k in range(1, 4)]
    pieces = pieces + [partner(piece, "mp", 2, 1) for piece in pieces]
    places = []
    for side in (mp, 1 - mp):
        for k in range(4):
            which = (blk & 3) ^ k
            places += [which >> 1, side * 2 + (which & 1)]
    return pieces, jnp.stack(places), heads_out


def spread(value):
    return lax.all_to_all(value, "blk", 0, 0, tiled=True)


def fresh_by_collectives(hidden, medusa_w, blocks, blk, mp):
    drafts, depth, units = medusa_w.shape
    rows = hidden.shape[0]
    own = drafts * rows // blocks
    hidden_cols = lax.dynamic_slice_in_dim(hidden, blk * depth, depth, 1)
    partial = jnp.einsum("rd,mdu->mru", hidden_cols, medusa_w, preferred_element_type=jnp.float32)
    partial = partial.reshape(blocks, own, units).astype(jnp.bfloat16)
    inner = lax.psum_scatter(partial, "blk", scatter_dimension=0).astype(jnp.float32)
    base = lax.dynamic_slice(hidden, ((blk * own) % rows, mp * units), (own, units))
    fresh = (base.astype(jnp.float32) + jax.nn.silu(inner)).astype(jnp.bfloat16)
    fresh = lax.all_gather(fresh, "blk", axis=0, tiled=True)
    return [lax.all_gather(fresh, "mp", axis=1, tiled=True)]


def ancestry(parents):
    count = parents.shape[1]
    column = jnp.arange(count, dtype=jnp.int32)
    linked = (parents[:, :, None] == column[None, None, :]) & (column[None, :, None] > 0)
    reach = jnp.eye(count, dtype=jnp.bfloat16)[None] + linked.astype(jnp.bfloat16)
    for sweep in range(count.bit_length()):
        met = jnp.einsum("gij,gjk->gik", reach, reach, preferred_element_type=jnp.float32)
        reach = jnp.minimum(met, 1.0).astype(jnp.bfloat16)
    return reach.astype(jnp.float32)


def per_device(
    hidden,
    medusa_w,
    embedding,
    cand_ids,
    tree_q,
    tree_key_value,
    prompt_key_value,
    block_group,
    block_len,
    block_empty,
    parents,
    out_weight,
    post_gain,
    resid,
):
    blocks, splits = lax.axis_size("blk"), lax.axis_size("mp")
    blk, mp = lax.axis_index("blk"), lax.axis_index("mp")
    drafts, depth, units = medusa_w.shape
    rows, model = hidden.shape
    lines = drafts * rows

    groups, tree_size, features = tree_q.shape
    width = features // blocks
    meta = jnp.concatenate([block_group, block_len, block_empty])

    def prompt():
        return prompt_part(tree_q, prompt_key_value, meta, width, blocks)

    def merge(partials):
        reach = ancestry(parents)
        numer, denom = tree_part(tree_q, tree_key_value, reach, blk * width, width)
        return merge_part(partials, numer, denom)

    if splits == 2 and blocks % 4 == 0 and units % 256 == 0 and drafts == 2:
        parts = draft_part(hidden, medusa_w, blk)
        parts, meta = lax.optimization_barrier((parts, meta))
        pieces, places, heads_out = both_by_stages(
            hidden, parts, units, blocks, blk, mp, prompt, merge
        )
    else:
        pieces = fresh_by_collectives(hidden, medusa_w, blocks, blk, mp)
        places = jnp.zeros((2,), jnp.int32)
        heads_out = merge(spread(prompt()))
    heads_out = spread(heads_out)
    attn = project_part(heads_out, out_weight)
    attn, pieces = lax.optimization_barrier((attn, pieces))
    attn = total_sum(attn, [("mp", splits)])
    normed = attn * lax.rsqrt(jnp.mean(attn * attn, -1, keepdims=True) + 1e-06) * post_gain
    layer_out = (normed + resid.astype(jnp.float32)).astype(jnp.bfloat16)

    vocab = embedding.shape[0]
    picks = cand_ids.shape[2]
    ids = cand_ids.reshape(lines, picks) - (blk * splits + mp) * vocab
    ids = jnp.pad(ids, ((0, 0), (0, LANES - picks)), constant_values=-1)
    score = score_part(places, pieces, embedding, ids, picks)
    score = total_sum(score, [("mp", splits), ("blk", blocks)])
    draft_logprob = score[:picks] - jnp.log(score[picks : picks + 1])
    draft_logprob = draft_logprob.T.reshape(drafts, rows, picks)
    return (draft_logprob, layer_out)


def solution(mesh):
    placed = (
        P(),
        P(None, "blk", "mp"),
        P(("blk", "mp"), None),
        P(),
        P(None, None, "mp"),
        P(None, None, None, "mp"),
        P(None, "blk", None, "mp"),
        P("blk"),
        P("blk"),
        P("blk"),
        P(),
        P("mp", None),
        P(),
        P("blk", None),
    )
    return jax.shard_map(
        per_device, mesh=mesh, in_specs=placed, out_specs=(P(), P("blk", None)), check_vma=False
    )
```

```python
import functools

import jax
import jax.numpy as jnp
from jax import lax
from jax.experimental import pallas as pl
from jax.experimental.pallas import tpu as pltpu
from jax.sharding import PartitionSpec as P

HEAD_SIZE = 256
LANES = 128
MIB = 1 << 20

EXTRA = 16
HIGH, LOW, GROUP = 0, 4, 8


def soft_weights(scores):
    return jnp.exp(50.0 * jnp.tanh(scores * (HEAD_SIZE**-0.5 / 50.0)))


def dot_t(left, right):
    return lax.dot_general(left, right, (((1,), (1,)), ((), ())), preferred_element_type=jnp.float32)


def in_hbm():
    return pl.BlockSpec(memory_space=pltpu.HBM)


def pin(value):
    return pltpu.with_memory_space_constraint(value, pltpu.HBM)


def in_vmem():
    return pl.BlockSpec(memory_space=pltpu.VMEM)


def in_smem():
    return pl.BlockSpec(memory_space=pltpu.SMEM)


def limit(mib):
    return pltpu.CompilerParams(vmem_limit_bytes=mib * MIB)


def prompt_kernel(meta, q_hbm, kv_hbm, out_ref, queries, held, sems):
    group, used, empty = meta[0], meta[1], meta[2]
    last = jnp.where(empty == 0, used, 0)
    kv_heads, slots = held.shape[1:3]
    tree_size, features = queries.shape
    repeats = features // HEAD_SIZE // kv_heads
    width = out_ref.shape[2]
    rows = tree_size * repeats
    ask = pltpu.make_async_copy(q_hbm.at[group], queries, sems.at[2 * kv_heads])
    ask.start()
    copies = [
        pltpu.make_async_copy(
            kv_hbm.at[s, 0, :, pl.ds(h * HEAD_SIZE, HEAD_SIZE)], held.at[s, h], sems.at[2 * h + s]
        )
        for h in range(kv_heads)
        for s in range(2)
    ]
    ahead = 4
    for copy in copies[:ahead]:
        copy.start()
    ask.wait()
    per_head = HEAD_SIZE // width
    row_id = lax.broadcasted_iota(jnp.int32, (tree_size, width), 0)
    lane_id = lax.broadcasted_iota(jnp.int32, (tree_size, width), 1)
    extra_id = lax.broadcasted_iota(jnp.int32, (EXTRA, width), 0)
    slot = lax.broadcasted_iota(jnp.int32, (rows, slots), 1)
    for h in range(kv_heads):
        asked = jnp.concatenate(
            [
                queries[:, (h * repeats + r) * HEAD_SIZE : (h * repeats + r + 1) * HEAD_SIZE]
                for r in range(repeats)
            ],
            axis=0,
        )
        copies[2 * h].wait()
        if 2 * h + ahead < len(copies):
            copies[2 * h + ahead].start()
        scores = dot_t(asked, held[0, h])
        weights = jnp.where(slot < last, soft_weights(scores), 0.0)
        denom = jnp.sum(weights, axis=1, keepdims=True)
        copies[2 * h + 1].wait()
        if 2 * h + 1 + ahead < len(copies):
            copies[2 * h + 1 + ahead].start()
        numer = jnp.dot(
            weights.astype(jnp.bfloat16), held[1, h], preferred_element_type=jnp.float32
        )
        for r in range(repeats):
            mine = jnp.broadcast_to(denom[r * tree_size : (r + 1) * tree_size], (tree_size, width))
            extra = jnp.where(extra_id == GROUP, group.astype(jnp.float32), 0.0)
            for c in range(-(-tree_size // width)):
                line = jnp.sum(
                    jnp.where(row_id == lane_id + c * width, mine, 0.0), axis=0, keepdims=True
                )
                high = line.astype(jnp.bfloat16).astype(jnp.float32)
                extra = jnp.where(extra_id == HIGH + c, high, extra)
                extra = jnp.where(extra_id == LOW + c, line - high, extra)
            for part in range(per_head):
                d = (h * repeats + r) * per_head + part
                out_ref[d, :tree_size, :] = numer[
                    r * tree_size : (r + 1) * tree_size, part * width : (part + 1) * width
                ].astype(jnp.bfloat16)
                out_ref[d, tree_size:, :] = extra.astype(jnp.bfloat16)


def prompt_part(tree_q, prompt_key_value, meta, width, blocks):
    groups, tree_size, features = tree_q.shape
    slots, key_features = prompt_key_value.shape[2:]
    kv_heads = key_features // HEAD_SIZE
    return pl.pallas_call(
        prompt_kernel,
        out_shape=jax.ShapeDtypeStruct((blocks, tree_size + EXTRA, width), jnp.bfloat16),
        in_specs=[in_smem(), in_hbm(), in_hbm()],
        out_specs=in_vmem(),
        scratch_shapes=[
            pltpu.VMEM((tree_size, features), jnp.bfloat16),
            pltpu.VMEM((2, kv_heads, slots, HEAD_SIZE), jnp.bfloat16),
            pltpu.SemaphoreType.DMA((2 * kv_heads + 1,)),
        ],
        compiler_params=limit(24),
        cost_estimate=pl.CostEstimate(
            flops=4 * tree_size * features * slots,
            bytes_accessed=4 * slots * key_features,
            transcendentals=2 * tree_size * slots * features // HEAD_SIZE,
        ),
        name="prompt_part",
    )(meta, pin(tree_q), pin(prompt_key_value))


def tree_kernel(meta, q_hbm, kv_hbm, reach_ref, numer_ref, denom_ref, held, sems):
    width = numer_ref.shape[2]
    query_columns = pl.ds(pl.multiple_of(meta[0] * HEAD_SIZE, HEAD_SIZE), HEAD_SIZE)
    key_columns = pl.ds(pl.multiple_of(meta[1] * HEAD_SIZE, HEAD_SIZE), HEAD_SIZE)
    copies = [
        pltpu.make_async_copy(q_hbm.at[:, :, query_columns], held.at[0], sems.at[0]),
        pltpu.make_async_copy(kv_hbm.at[0, :, :, key_columns], held.at[1], sems.at[1]),
        pltpu.make_async_copy(kv_hbm.at[1, :, :, key_columns], held.at[2], sems.at[2]),
    ]
    for copy in copies:
        copy.start()
    for copy in copies:
        copy.wait()
    for g in range(held.shape[1]):
        weights = soft_weights(dot_t(held[0, g], held[1, g])) * reach_ref[g]
        denom_ref[g] = jnp.broadcast_to(
            jnp.sum(weights, axis=1, keepdims=True), denom_ref.shape[1:]
        )
        numer = jnp.dot(
            weights.astype(jnp.bfloat16), held[2, g], preferred_element_type=jnp.float32
        )
        mine = numer[:, :width]
        for j in range(1, HEAD_SIZE // width):
            mine = jnp.where(meta[2] == j, numer[:, j * width : (j + 1) * width], mine)
        numer_ref[g] = mine


def tree_part(tree_q, tree_key_value, reach, column, width):
    groups, tree_size, features = tree_q.shape
    repeats = features // tree_key_value.shape[3]
    head = column // HEAD_SIZE
    meta = jnp.stack([head, head // repeats, column % HEAD_SIZE // width])
    return pl.pallas_call(
        tree_kernel,
        out_shape=[jax.ShapeDtypeStruct((groups, tree_size, width), jnp.float32)] * 2,
        in_specs=[in_smem(), in_hbm(), in_hbm(), in_vmem()],
        out_specs=[in_vmem()] * 2,
        scratch_shapes=[
            pltpu.VMEM((3, groups, tree_size, HEAD_SIZE), jnp.bfloat16),
            pltpu.SemaphoreType.DMA((3,)),
        ],
        compiler_params=limit(16),
        name="tree_part",
    )(meta, pin(tree_q), pin(tree_key_value), reach)


def merge_kernel(got_ref, numer_ref, denom_ref, out_ref, hold):
    blocks = got_ref.shape[0]
    groups, tree_size, width = numer_ref.shape
    row_id = lax.broadcasted_iota(jnp.int32, (tree_size, width), 0)
    lane_id = lax.broadcasted_iota(jnp.int32, (tree_size, width), 1)
    lines = -(-tree_size // width)

    @pl.loop(0, groups)
    def _(g):
        def add(b, carry):
            numer, extra = carry
            more = got_ref[b, tree_size:, :].astype(jnp.float32)
            same = more[GROUP : GROUP + 1, :] == g.astype(jnp.float32)
            numer = numer + jnp.where(same, got_ref[b, :tree_size, :].astype(jnp.float32), 0.0)
            extra = extra + jnp.where(same, more, 0.0)
            return numer, extra

        start = (numer_ref[g], jnp.zeros((EXTRA, width), jnp.float32))
        numer, extra = lax.fori_loop(0, blocks, add, start, unroll=True)
        denom = denom_ref[g]
        for c in range(lines):
            line = extra[HIGH + c : HIGH + c + 1, :] + extra[LOW + c : LOW + c + 1, :]
            spread = jnp.where(row_id == lane_id + c * width, line, 0.0)
            denom = denom + jnp.sum(spread, axis=1, keepdims=True)
        hold[pl.ds(pl.multiple_of(g * tree_size, 8), tree_size), :] = numer / denom

    count = out_ref.shape[1]
    for d in range(out_ref.shape[0]):
        out_ref[d] = hold[d * count : (d + 1) * count, :].astype(jnp.bfloat16)


def merge_part(got, numer, denom):
    blocks, _, width = got.shape
    groups, tree_size, _ = numer.shape
    tokens = groups * tree_size
    return pl.pallas_call(
        merge_kernel,
        out_shape=jax.ShapeDtypeStruct((blocks, tokens // blocks, width), jnp.bfloat16),
        scratch_shapes=[pltpu.VMEM((tokens, width), jnp.float32)],
        compiler_params=limit(16),
        name="merge_part",
    )(got, numer, denom)


def project_kernel(heads_ref, weight_hbm, out_ref, ring, sems):
    slots, span = ring.shape[:2]
    steps = weight_hbm.shape[0] // span
    per_step = span // heads_ref.shape[2]

    def copy(i):
        return pltpu.make_async_copy(
            weight_hbm.at[i * span : (i + 1) * span], ring.at[i % slots], sems.at[i % slots]
        )

    for i in range(min(slots, steps)):
        copy(i).start()
    for i in range(steps):
        left = jnp.concatenate([heads_ref[i * per_step + j] for j in range(per_step)], axis=1)
        copy(i).wait()
        more = jnp.dot(left, ring[i % slots], preferred_element_type=jnp.float32)
        out_ref[...] = more if i == 0 else out_ref[...] + more
        if i + slots < steps:
            copy(i + slots).start()


def project_part(heads_out, out_weight):
    blocks, tokens, width = heads_out.shape
    features, model = out_weight.shape
    if width % LANES or features % HEAD_SIZE:
        flat = heads_out.transpose(1, 0, 2).reshape(tokens, features)
        return jnp.dot(flat, out_weight, preferred_element_type=jnp.float32)
    slots = 4
    return pl.pallas_call(
        project_kernel,
        out_shape=jax.ShapeDtypeStruct((tokens, model), jnp.float32),
        in_specs=[in_vmem(), in_hbm()],
        out_specs=in_vmem(),
        scratch_shapes=[
            pltpu.VMEM((slots, HEAD_SIZE, model), jnp.bfloat16),
            pltpu.SemaphoreType.DMA((slots,)),
        ],
        compiler_params=limit(20),
        cost_estimate=pl.CostEstimate(
            flops=2 * tokens * features * model,
            bytes_accessed=2 * features * model,
            transcendentals=0,
        ),
        name="project_part",
    )(heads_out, pin(out_weight))


def score_kernel(picks, streams, places, ids_ref, *refs):
    pieces, embeds, out_ref = refs[: -5 - 2 * streams], refs[-5 - 2 * streams : -5], refs[-5]
    fresh, total, picked, before = refs[-4:]
    step = pl.program_id(0)
    span = embeds[0].shape[0]
    rows = fresh.shape[0]
    band = 32 if rows % 32 == 0 else rows

    @pl.when(step == 0)
    def _():
        before[...] = jnp.zeros_like(before)
        for n, piece in enumerate(pieces):
            height, wide = piece.shape
            row = pl.multiple_of(places[2 * n] * height, 16)
            col = pl.multiple_of(places[2 * n + 1] * wide, LANES)
            fresh[pl.ds(row, height), pl.ds(col, wide)] = piece[...]

    def product(n):
        half = fresh.shape[1] // 2
        low, high = embeds[2 * n], embeds[2 * n + 1]
        return dot_t(fresh[:, :half], low[...]) + dot_t(fresh[:, half:], high[...])

    def absorb(raw, start, keep=None):
        for r in range(0, rows, band):
            ids = ids_ref[r : r + band] - start
            lane = ids & (LANES - 1)
            chunk = ids >> 7
            sums, found = total[r : r + band], picked[r : r + band]
            for c in range(span // LANES):
                part = jnp.tanh(raw[r : r + band, c * LANES : (c + 1) * LANES] * (1.0 / 30.0))
                sums = sums + jnp.exp(30.0 * part)
                there = jnp.take_along_axis(part, lane, axis=1, mode="promise_in_bounds")
                found = found + jnp.where(chunk == c, there, 0.0)
            if keep is not None:
                sums, found = jnp.where(keep, sums, 0.0), jnp.where(keep, found, 0.0)
            total[r : r + band] = sums
            picked[r : r + band] = found

    base = step * streams * span
    raw = product(0)
    absorb(before[...], base - span, step > 0)
    for n in range(1, streams):
        more = product(n)
        absorb(raw, base + (n - 1) * span)
        raw = more
    before[...] = raw

    @pl.when(step == pl.num_programs(0) - 1)
    def _():
        absorb(before[...], base + (streams - 1) * span)
        sums, found = total[...], picked[...]
        place = lax.broadcasted_iota(jnp.int32, sums.shape, 1)
        whole = jnp.sum(sums, axis=1, keepdims=True)
        both = jnp.where(place < picks, 30.0 * found, jnp.where(place == picks, whole, 0.0))
        out_ref[...] = both.T[: out_ref.shape[0]]


def score_part(places, pieces, embedding, ids, picks):
    rows = ids.shape[0]
    vocab, depth = embedding.shape
    span, streams = HEAD_SIZE, 2
    lines = -(-(picks + 1) // 8) * 8
    fixed = lambda i, places: (0, 0)
    return pl.pallas_call(
        functools.partial(score_kernel, picks, streams),
        out_shape=jax.ShapeDtypeStruct((lines, rows), jnp.float32),
        grid_spec=pltpu.PrefetchScalarGridSpec(
            num_scalar_prefetch=1,
            grid=(vocab // (span * streams),),
            in_specs=[pl.BlockSpec((rows, LANES), fixed)]
            + [pl.BlockSpec(piece.shape, fixed) for piece in pieces]
            + [
                pl.BlockSpec(
                    (span, depth // 2), lambda i, places, n=n, k=k: (i * streams + n, k)
                )
                for n in range(streams)
                for k in range(2)
            ],
            out_specs=pl.BlockSpec((lines, rows), fixed),
            scratch_shapes=[pltpu.VMEM((rows, depth), jnp.bfloat16)]
            + [pltpu.VMEM((rows, LANES), jnp.float32)] * 2
            + [pltpu.VMEM((rows, span), jnp.float32)],
        ),
        compiler_params=limit(32),
        cost_estimate=pl.CostEstimate(
            flops=2 * rows * depth * vocab,
            bytes_accessed=2 * vocab * depth,
            transcendentals=2 * rows * vocab,
        ),
        name="score_part",
    )(places, ids, *pieces, *[pin(embedding)] * (2 * streams))


def draft_kernel(meta, hidden_hbm, weight_hbm, *refs):
    outs, columns, padded, sems = refs[:4], *refs[4:]
    depth = weight_hbm.shape[1]
    half = padded.shape[2]
    window = padded.shape[1]
    first = pl.multiple_of(meta[0], LANES)
    ask = pltpu.make_async_copy(hidden_hbm.at[:, pl.ds(first, window)], columns, sems.at[4])
    ask.start()
    padded[...] = jnp.zeros_like(padded)
    copies = []
    for k in (1, 2, 3, 0):
        quad = meta[2 + k]
        col = pl.multiple_of((quad & 1) * half, LANES)
        copies.append(
            pltpu.make_async_copy(
                weight_hbm.at[quad >> 1, :, pl.ds(col, half)],
                padded.at[k, pl.ds(pl.multiple_of(meta[1], 16), depth)],
                sems.at[k],
            )
        )
        copies[-1].start()
    ask.wait()
    for n, k in enumerate((1, 2, 3, 0)):
        copies[n].wait()
        partial = jnp.dot(columns[...], padded[k], preferred_element_type=jnp.float32)
        outs[k][...] = partial.astype(outs[k].dtype)


def draft_part(hidden, medusa_w, blk):
    rows, model = hidden.shape
    depth, units = medusa_w.shape[1:]
    half = units // 2
    window = -(-depth // LANES) * LANES + LANES
    start = blk * depth
    first = jnp.minimum(start // LANES * LANES, model - window)
    meta = jnp.stack([first, start - first] + [(blk & 3) ^ k for k in range(4)])
    return pl.pallas_call(
        draft_kernel,
        out_shape=[
            jax.ShapeDtypeStruct((rows, half), jnp.bfloat16 if k else jnp.float32)
            for k in range(4)
        ],
        in_specs=[in_smem(), in_hbm(), in_hbm()],
        out_specs=[in_vmem()] * 4,
        scratch_shapes=[
            pltpu.VMEM((rows, window), jnp.bfloat16),
            pltpu.VMEM((4, window, half), jnp.bfloat16),
            pltpu.SemaphoreType.DMA((5,)),
        ],
        compiler_params=limit(16),
        name="draft_part",
    )(meta, pin(hidden), pin(medusa_w))


def fold_kernel(place, own_ref, *refs):
    got, outs, hold = refs[:3], refs[3:-1], refs[-1]
    total = own_ref[...]
    for one in got:
        total = total + one[...].astype(jnp.float32)
    height = hold.shape[1]
    for j in range(len(outs)):
        hold[j] = total[j * height : (j + 1) * height]
    for k, out in enumerate(outs):
        out[...] = hold[place[0] ^ k].astype(out.dtype)


def fold_part(own, got, place, layers):
    rows, half = own.shape
    height = rows // layers
    return pl.pallas_call(
        fold_kernel,
        out_shape=[
            jax.ShapeDtypeStruct((height, half), jnp.bfloat16 if k else jnp.float32)
            for k in range(layers)
        ],
        in_specs=[in_smem()] + [in_vmem()] * 4,
        out_specs=[in_vmem()] * layers,
        scratch_shapes=[pltpu.VMEM((layers, height, half), jnp.float32)],
        compiler_params=limit(16),
        name="fold_part",
    )(place, own, *got)


def stack_kernel(place, *refs):
    parts, out_ref, hold, flat = refs[:-3], refs[-3], refs[-2], refs[-1]
    height = hold.shape[1]
    for k, part in enumerate(parts):
        hold[place[0] ^ k] = part[...].astype(jnp.float32)
    for j in range(len(parts)):
        flat[j * height : (j + 1) * height, :] = hold[j]
    out_ref[...] = flat[...].astype(jnp.bfloat16)


def stack_part(parts, place):
    layers = len(parts)
    height, half = parts[0].shape
    return pl.pallas_call(
        stack_kernel,
        out_shape=jax.ShapeDtypeStruct((layers * height, half), jnp.bfloat16),
        in_specs=[in_smem()] + [in_vmem()] * layers,
        out_specs=in_vmem(),
        scratch_shapes=[
            pltpu.VMEM((layers, height, half), jnp.float32),
            pltpu.VMEM((layers * height, half), jnp.float32),
        ],
        compiler_params=limit(16),
        name="stack_part",
    )(place, *parts)


def partner(value, axis, size, bits):
    return lax.ppermute(value, axis, [(i, i ^ bits) for i in range(size)])


def group_sum(value, axis, size, stride, count):
    values = [value] + [partner(value, axis, size, k * stride) for k in range(1, count)]
    while len(values) > 1:
        values = [values[i] + values[i + 1] for i in range(0, len(values), 2)]
    return values[0]


def both_by_stages(hidden, parts, parents, units, blocks, blk, mp, prompt, merge):
    rows, model = hidden.shape
    half = units // 2
    layers = blocks // 4
    height = rows // layers
    layer = blk // 4
    place = layer.reshape(1)
    got = [partner(parts[k], "blk", blocks, k) for k in range(1, 4)]
    sent = prompt()
    partials = spread(sent)
    got, sent = lax.optimization_barrier((got, sent))
    parts = fold_part(parts[0], got, place, layers)
    parts, parents = lax.optimization_barrier((parts, parents))
    more = [partner(parts[k], "blk", blocks, 4 * k) for k in range(1, layers)]
    more, heads_out = lax.optimization_barrier((more, merge(partials, parents)))
    inner = parts[0] + sum(one.astype(jnp.float32) for one in more)
    base = lax.dynamic_slice(
        hidden, (layer * height, mp * units + (blk & 1) * half), (height, half)
    )
    own = (base.astype(jnp.float32) + jax.nn.silu(inner)).astype(jnp.bfloat16)
    own, heads_out = lax.optimization_barrier((own, heads_out))
    chunks = [own] + [partner(own, "blk", blocks, 4 * k) for k in range(1, layers)]
    quad = stack_part(chunks, place)
    pieces = [quad] + [partner(quad, "blk", blocks, k) for k in range(1, 4)]
    pieces = pieces + [partner(piece, "mp", 2, 1) for piece in pieces]
    places = []
    for side in (mp, 1 - mp):
        for k in range(4):
            which = (blk & 3) ^ k
            places += [which >> 1, side * 2 + (which & 1)]
    return pieces, jnp.stack(places), heads_out


def spread(value):
    return lax.all_to_all(value, "blk", 0, 0, tiled=True)


def fresh_by_collectives(hidden, medusa_w, blocks, blk, mp):
    drafts, depth, units = medusa_w.shape
    rows = hidden.shape[0]
    own = drafts * rows // blocks
    hidden_cols = lax.dynamic_slice_in_dim(hidden, blk * depth, depth, 1)
    partial = jnp.einsum("rd,mdu->mru", hidden_cols, medusa_w, preferred_element_type=jnp.float32)
    partial = partial.reshape(blocks, own, units).astype(jnp.bfloat16)
    inner = lax.psum_scatter(partial, "blk", scatter_dimension=0).astype(jnp.float32)
    base = lax.dynamic_slice(hidden, ((blk * own) % rows, mp * units), (own, units))
    fresh = (base.astype(jnp.float32) + jax.nn.silu(inner)).astype(jnp.bfloat16)
    fresh = lax.all_gather(fresh, "blk", axis=0, tiled=True)
    return [lax.all_gather(fresh, "mp", axis=1, tiled=True)]


def ancestry(parents):
    count = parents.shape[1]
    column = jnp.arange(count, dtype=jnp.int32)
    linked = (parents[:, :, None] == column[None, None, :]) & (column[None, :, None] > 0)
    reach = jnp.eye(count, dtype=jnp.bfloat16)[None] + linked.astype(jnp.bfloat16)
    for sweep in range(count.bit_length()):
        met = jnp.einsum("gij,gjk->gik", reach, reach, preferred_element_type=jnp.float32)
        reach = jnp.minimum(met, 1.0).astype(jnp.bfloat16)
    return reach.astype(jnp.float32)


def per_device(
    hidden,
    medusa_w,
    embedding,
    cand_ids,
    tree_q,
    tree_key_value,
    prompt_key_value,
    block_group,
    block_len,
    block_empty,
    parents,
    out_weight,
    post_gain,
    resid,
):
    blocks, splits = lax.axis_size("blk"), lax.axis_size("mp")
    blk, mp = lax.axis_index("blk"), lax.axis_index("mp")
    drafts, depth, units = medusa_w.shape
    rows, model = hidden.shape
    lines = drafts * rows

    groups, tree_size, features = tree_q.shape
    width = features // blocks
    meta = jnp.concatenate([block_group, block_len, block_empty])

    def prompt():
        return prompt_part(tree_q, prompt_key_value, meta, width, blocks)

    def merge(partials, parents):
        reach = ancestry(parents)
        numer, denom = tree_part(tree_q, tree_key_value, reach, blk * width, width)
        return merge_part(partials, numer, denom)

    if splits == 2 and blocks % 4 == 0 and units % 256 == 0 and drafts == 2:
        parts = draft_part(hidden, medusa_w, blk)
        parts, meta = lax.optimization_barrier((parts, meta))
        pieces, places, heads_out = both_by_stages(
            hidden, parts, parents, units, blocks, blk, mp, prompt, merge
        )
    else:
        pieces = fresh_by_collectives(hidden, medusa_w, blocks, blk, mp)
        places = jnp.zeros((2,), jnp.int32)
        heads_out = merge(spread(prompt()), parents)
    heads_out = spread(heads_out)
    attn = project_part(heads_out, out_weight)
    attn, pieces = lax.optimization_barrier((attn, pieces))
    attn = group_sum(attn, "mp", splits, 1, splits)
    normed = attn * lax.rsqrt(jnp.mean(attn * attn, -1, keepdims=True) + 1e-06) * post_gain
    layer_out = (normed + resid.astype(jnp.float32)).astype(jnp.bfloat16)

    vocab = embedding.shape[0]
    picks = cand_ids.shape[2]
    ids = cand_ids.reshape(lines, picks) - (blk * splits + mp) * vocab
    ids = jnp.pad(ids, ((0, 0), (0, LANES - picks)), constant_values=-1)
    score = score_part(places, pieces, embedding, ids, picks)
    score = group_sum(score, "mp", splits, 1, splits)
    score = group_sum(score, "blk", blocks, 1, 4)
    score = group_sum(score, "blk", blocks, 4, blocks // 4)
    draft_logprob = score[:picks] - jnp.log(score[picks : picks + 1])
    draft_logprob = draft_logprob.T.reshape(drafts, rows, picks)
    return (draft_logprob, layer_out)


def solution(mesh):
    placed = (
        P(),
        P(None, "blk", "mp"),
        P(("blk", "mp"), None),
        P(),
        P(None, None, "mp"),
        P(None, None, None, "mp"),
        P(None, "blk", None, "mp"),
        P("blk"),
        P("blk"),
        P("blk"),
        P(),
        P("mp", None),
        P(),
        P("blk", None),
    )
    return jax.shard_map(
        per_device, mesh=mesh, in_specs=placed, out_specs=(P(), P("blk", None)), check_vma=False
    )
```

```python
import functools

import jax
import jax.numpy as jnp
from jax import lax
from jax.experimental import pallas as pl
from jax.experimental.pallas import tpu as pltpu
from jax.sharding import PartitionSpec as P

HEAD_SIZE = 256
LANES = 128
MIB = 1 << 20

EXTRA = 16
HIGH, LOW, GROUP = 0, 4, 8


def soft_weights(scores):
    return jnp.exp(50.0 * jnp.tanh(scores * (HEAD_SIZE**-0.5 / 50.0)))


def dot_t(left, right):
    return lax.dot_general(left, right, (((1,), (1,)), ((), ())), preferred_element_type=jnp.float32)


def in_hbm():
    return pl.BlockSpec(memory_space=pltpu.HBM)


def pin(value):
    return pltpu.with_memory_space_constraint(value, pltpu.HBM)


def in_vmem():
    return pl.BlockSpec(memory_space=pltpu.VMEM)


def in_smem():
    return pl.BlockSpec(memory_space=pltpu.SMEM)


def limit(mib):
    return pltpu.CompilerParams(vmem_limit_bytes=mib * MIB)


def prompt_kernel(meta, q_hbm, kv_hbm, out_ref, queries, held, sems):
    group, used, empty = meta[0], meta[1], meta[2]
    last = jnp.where(empty == 0, used, 0)
    kv_heads, slots = held.shape[1:3]
    tree_size, features = queries.shape
    repeats = features // HEAD_SIZE // kv_heads
    width = out_ref.shape[2]
    rows = tree_size * repeats
    ask = pltpu.make_async_copy(q_hbm.at[group], queries, sems.at[2 * kv_heads])
    ask.start()
    copies = [
        pltpu.make_async_copy(
            kv_hbm.at[s, 0, :, pl.ds(h * HEAD_SIZE, HEAD_SIZE)], held.at[s, h], sems.at[2 * h + s]
        )
        for h in range(kv_heads)
        for s in range(2)
    ]
    ahead = 4
    for copy in copies[:ahead]:
        copy.start()
    ask.wait()
    per_head = HEAD_SIZE // width
    row_id = lax.broadcasted_iota(jnp.int32, (tree_size, width), 0)
    lane_id = lax.broadcasted_iota(jnp.int32, (tree_size, width), 1)
    extra_id = lax.broadcasted_iota(jnp.int32, (EXTRA, width), 0)
    span = min(512, slots)
    slot = lax.broadcasted_iota(jnp.int32, (rows, span), 1)
    for h in range(kv_heads):
        asked = jnp.concatenate(
            [
                queries[:, (h * repeats + r) * HEAD_SIZE : (h * repeats + r + 1) * HEAD_SIZE]
                for r in range(repeats)
            ],
            axis=0,
        )
        copies[2 * h].wait()
        if 2 * h + ahead < len(copies):
            copies[2 * h + ahead].start()
        numer = jnp.zeros((rows, HEAD_SIZE), jnp.float32)
        sums = jnp.zeros((rows, LANES), jnp.float32)
        for start in range(0, slots, span):
            scores = dot_t(asked, held[0, h, start : start + span])
            weights = jnp.where(slot < last - start, soft_weights(scores), 0.0)
            for c in range(0, span, LANES):
                sums = sums + weights[:, c : c + LANES]
            if start == 0:
                copies[2 * h + 1].wait()
                if 2 * h + 1 + ahead < len(copies):
                    copies[2 * h + 1 + ahead].start()
            numer = numer + jnp.dot(
                weights.astype(jnp.bfloat16),
                held[1, h, start : start + span],
                preferred_element_type=jnp.float32,
            )
        denom = jnp.sum(sums, axis=1, keepdims=True)
        for r in range(repeats):
            mine = jnp.broadcast_to(denom[r * tree_size : (r + 1) * tree_size], (tree_size, width))
            extra = jnp.where(extra_id == GROUP, group.astype(jnp.float32), 0.0)
            for c in range(-(-tree_size // width)):
                line = jnp.sum(
                    jnp.where(row_id == lane_id + c * width, mine, 0.0), axis=0, keepdims=True
                )
                high = line.astype(jnp.bfloat16).astype(jnp.float32)
                extra = jnp.where(extra_id == HIGH + c, high, extra)
                extra = jnp.where(extra_id == LOW + c, line - high, extra)
            for part in range(per_head):
                d = (h * repeats + r) * per_head + part
                out_ref[d, :tree_size, :] = numer[
                    r * tree_size : (r + 1) * tree_size, part * width : (part + 1) * width
                ].astype(jnp.bfloat16)
                out_ref[d, tree_size:, :] = extra.astype(jnp.bfloat16)


def prompt_part(tree_q, prompt_key_value, meta, width, blocks):
    groups, tree_size, features = tree_q.shape
    slots, key_features = prompt_key_value.shape[2:]
    kv_heads = key_features // HEAD_SIZE
    return pl.pallas_call(
        prompt_kernel,
        out_shape=jax.ShapeDtypeStruct((blocks, tree_size + EXTRA, width), jnp.bfloat16),
        in_specs=[in_smem(), in_hbm(), in_hbm()],
        out_specs=in_vmem(),
        scratch_shapes=[
            pltpu.VMEM((tree_size, features), jnp.bfloat16),
            pltpu.VMEM((2, kv_heads, slots, HEAD_SIZE), jnp.bfloat16),
            pltpu.SemaphoreType.DMA((2 * kv_heads + 1,)),
        ],
        compiler_params=limit(24),
        cost_estimate=pl.CostEstimate(
            flops=4 * tree_size * features * slots,
            bytes_accessed=4 * slots * key_features,
            transcendentals=2 * tree_size * slots * features // HEAD_SIZE,
        ),
        name="prompt_part",
    )(meta, pin(tree_q), pin(prompt_key_value))


def tree_kernel(meta, q_hbm, kv_hbm, parents_ref, numer_ref, denom_ref, held, sems):
    width = numer_ref.shape[2]
    query_columns = pl.ds(pl.multiple_of(meta[0] * HEAD_SIZE, HEAD_SIZE), HEAD_SIZE)
    key_columns = pl.ds(pl.multiple_of(meta[1] * HEAD_SIZE, HEAD_SIZE), HEAD_SIZE)
    copies = [
        pltpu.make_async_copy(q_hbm.at[:, :, query_columns], held.at[0], sems.at[0]),
        pltpu.make_async_copy(kv_hbm.at[0, :, :, key_columns], held.at[1], sems.at[1]),
        pltpu.make_async_copy(kv_hbm.at[1, :, :, key_columns], held.at[2], sems.at[2]),
    ]
    for copy in copies:
        copy.start()
    groups, count = parents_ref.shape
    above = lax.broadcasted_iota(jnp.int32, (count, count), 0)
    token = lax.broadcasted_iota(jnp.int32, (count, count), 1)
    met = [
        jnp.where(
            (above == token) | ((parents_ref[g : g + 1, :] == above) & (token > 0)), 1.0, 0.0
        )
        for g in range(groups)
    ]
    for sweep in range(count.bit_length()):
        small = [one.astype(jnp.bfloat16) for one in met]
        met = [
            jnp.minimum(jnp.dot(one, one, preferred_element_type=jnp.float32), 1.0)
            for one in small
        ]
    for copy in copies:
        copy.wait()
    for g in range(groups):
        weights = soft_weights(dot_t(held[0, g], held[1, g])) * met[g].T
        denom_ref[g] = jnp.broadcast_to(
            jnp.sum(weights, axis=1, keepdims=True), denom_ref.shape[1:]
        )
        numer = jnp.dot(
            weights.astype(jnp.bfloat16), held[2, g], preferred_element_type=jnp.float32
        )
        mine = numer[:, :width]
        for j in range(1, HEAD_SIZE // width):
            mine = jnp.where(meta[2] == j, numer[:, j * width : (j + 1) * width], mine)
        numer_ref[g] = mine


def tree_part(tree_q, tree_key_value, parents, column, width):
    groups, tree_size, features = tree_q.shape
    repeats = features // tree_key_value.shape[3]
    head = column // HEAD_SIZE
    meta = jnp.stack([head, head // repeats, column % HEAD_SIZE // width])
    return pl.pallas_call(
        tree_kernel,
        out_shape=[jax.ShapeDtypeStruct((groups, tree_size, width), jnp.float32)] * 2,
        in_specs=[in_smem(), in_hbm(), in_hbm(), in_vmem()],
        out_specs=[in_vmem()] * 2,
        scratch_shapes=[
            pltpu.VMEM((3, groups, tree_size, HEAD_SIZE), jnp.bfloat16),
            pltpu.SemaphoreType.DMA((3,)),
        ],
        compiler_params=limit(16),
        name="tree_part",
    )(meta, pin(tree_q), pin(tree_key_value), parents)


def merge_kernel(got_ref, numer_ref, denom_ref, out_ref, hold, sums, lines):
    blocks = got_ref.shape[0]
    groups, tree_size, width = numer_ref.shape
    row_id = lax.broadcasted_iota(jnp.int32, (tree_size, width), 0)
    lane_id = lax.broadcasted_iota(jnp.int32, (tree_size, width), 1)
    sums[...] = numer_ref[...]
    lines[...] = jnp.zeros_like(lines)
    owners = []
    for b in range(blocks):
        extra = got_ref[b, tree_size:, :].astype(jnp.float32)
        owners.append(jnp.max(extra[GROUP : GROUP + 1, :]).astype(jnp.int32))
    for b in range(blocks):
        sums[owners[b]] += got_ref[b, :tree_size, :].astype(jnp.float32)
        lines[owners[b]] += got_ref[b, tree_size:, :].astype(jnp.float32)
    for g in range(groups):
        denom = denom_ref[g]
        for c in range(-(-tree_size // width)):
            line = lines[g, HIGH + c : HIGH + c + 1, :] + lines[g, LOW + c : LOW + c + 1, :]
            spread = jnp.where(row_id == lane_id + c * width, line, 0.0)
            denom = denom + jnp.sum(spread, axis=1, keepdims=True)
        hold[g * tree_size : (g + 1) * tree_size, :] = sums[g] / denom

    count = out_ref.shape[1]
    for d in range(out_ref.shape[0]):
        out_ref[d] = hold[d * count : (d + 1) * count, :].astype(jnp.bfloat16)


def merge_part(got, numer, denom):
    blocks, _, width = got.shape
    groups, tree_size, _ = numer.shape
    tokens = groups * tree_size
    return pl.pallas_call(
        merge_kernel,
        out_shape=jax.ShapeDtypeStruct((blocks, tokens // blocks, width), jnp.bfloat16),
        scratch_shapes=[
            pltpu.VMEM((tokens, width), jnp.float32),
            pltpu.VMEM((groups, tree_size, width), jnp.float32),
            pltpu.VMEM((groups, EXTRA, width), jnp.float32),
        ],
        compiler_params=limit(16),
        name="merge_part",
    )(got, numer, denom)


def project_kernel(heads_ref, weight_hbm, out_ref, ring, sems):
    slots, span = ring.shape[:2]
    steps = weight_hbm.shape[0] // span
    per_step = span // heads_ref.shape[2]

    def copy(i):
        return pltpu.make_async_copy(
            weight_hbm.at[i * span : (i + 1) * span], ring.at[i % slots], sems.at[i % slots]
        )

    for i in range(min(slots, steps)):
        copy(i).start()
    for i in range(steps):
        left = jnp.concatenate([heads_ref[i * per_step + j] for j in range(per_step)], axis=1)
        copy(i).wait()
        more = jnp.dot(left, ring[i % slots], preferred_element_type=jnp.float32)
        out_ref[...] = more if i == 0 else out_ref[...] + more
        if i + slots < steps:
            copy(i + slots).start()


def project_part(heads_out, out_weight):
    blocks, tokens, width = heads_out.shape
    features, model = out_weight.shape
    if width % LANES or features % HEAD_SIZE:
        flat = heads_out.transpose(1, 0, 2).reshape(tokens, features)
        return jnp.dot(flat, out_weight, preferred_element_type=jnp.float32)
    slots = 4
    return pl.pallas_call(
        project_kernel,
        out_shape=jax.ShapeDtypeStruct((tokens, model), jnp.float32),
        in_specs=[in_vmem(), in_hbm()],
        out_specs=in_vmem(),
        scratch_shapes=[
            pltpu.VMEM((slots, HEAD_SIZE, model), jnp.bfloat16),
            pltpu.SemaphoreType.DMA((slots,)),
        ],
        compiler_params=limit(20),
        cost_estimate=pl.CostEstimate(
            flops=2 * tokens * features * model,
            bytes_accessed=2 * features * model,
            transcendentals=0,
        ),
        name="project_part",
    )(heads_out, pin(out_weight))


def score_kernel(picks, streams, places, ids_ref, *refs):
    pieces, embeds, out_ref = refs[: -5 - 2 * streams], refs[-5 - 2 * streams : -5], refs[-5]
    fresh, total, picked, before = refs[-4:]
    step = pl.program_id(0)
    span = embeds[0].shape[0]
    rows = fresh.shape[0]
    band = 32 if rows % 32 == 0 else rows

    @pl.when(step == 0)
    def _():
        before[...] = jnp.zeros_like(before)
        for n, piece in enumerate(pieces):
            height, wide = piece.shape
            row = pl.multiple_of(places[2 * n] * height, 16)
            col = pl.multiple_of(places[2 * n + 1] * wide, LANES)
            fresh[pl.ds(row, height), pl.ds(col, wide)] = piece[...]

    def product(n):
        half = fresh.shape[1] // 2
        low, high = embeds[2 * n], embeds[2 * n + 1]
        return dot_t(fresh[:, :half], low[...]) + dot_t(fresh[:, half:], high[...])

    def absorb(raw, start, keep=None):
        for r in range(0, rows, band):
            ids = ids_ref[r : r + band] - start
            lane = ids & (LANES - 1)
            chunk = ids >> 7
            sums, found = total[r : r + band], picked[r : r + band]
            for c in range(span // LANES):
                part = jnp.tanh(raw[r : r + band, c * LANES : (c + 1) * LANES] * (1.0 / 30.0))
                sums = sums + jnp.exp(30.0 * part)
                there = jnp.take_along_axis(part, lane, axis=1, mode="promise_in_bounds")
                found = found + jnp.where(chunk == c, there, 0.0)
            if keep is not None:
                sums, found = jnp.where(keep, sums, 0.0), jnp.where(keep, found, 0.0)
            total[r : r + band] = sums
            picked[r : r + band] = found

    base = step * streams * span
    raw = product(0)
    absorb(before[...], base - span, step > 0)
    for n in range(1, streams):
        more = product(n)
        absorb(raw, base + (n - 1) * span)
        raw = more
    before[...] = raw

    @pl.when(step == pl.num_programs(0) - 1)
    def _():
        absorb(before[...], base + (streams - 1) * span)
        sums, found = total[...], picked[...]
        place = lax.broadcasted_iota(jnp.int32, sums.shape, 1)
        whole = jnp.sum(sums, axis=1, keepdims=True)
        both = jnp.where(place < picks, 30.0 * found, jnp.where(place == picks, whole, 0.0))
        out_ref[...] = both.T[: out_ref.shape[0]]


def score_part(places, pieces, embedding, ids, picks):
    rows = ids.shape[0]
    vocab, depth = embedding.shape
    span, streams = min(512, vocab), 1
    lines = -(-(picks + 1) // 8) * 8
    fixed = lambda i, places: (0, 0)
    return pl.pallas_call(
        functools.partial(score_kernel, picks, streams),
        out_shape=jax.ShapeDtypeStruct((lines, rows), jnp.float32),
        grid_spec=pltpu.PrefetchScalarGridSpec(
            num_scalar_prefetch=1,
            grid=(vocab // (span * streams),),
            in_specs=[pl.BlockSpec((rows, LANES), fixed)]
            + [pl.BlockSpec(piece.shape, fixed) for piece in pieces]
            + [
                pl.BlockSpec(
                    (span, depth // 2), lambda i, places, n=n, k=k: (i * streams + n, k)
                )
                for n in range(streams)
                for k in range(2)
            ],
            out_specs=pl.BlockSpec((lines, rows), fixed),
            scratch_shapes=[pltpu.VMEM((rows, depth), jnp.bfloat16)]
            + [pltpu.VMEM((rows, LANES), jnp.float32)] * 2
            + [pltpu.VMEM((rows, span), jnp.float32)],
        ),
        compiler_params=limit(32),
        cost_estimate=pl.CostEstimate(
            flops=2 * rows * depth * vocab,
            bytes_accessed=2 * vocab * depth,
            transcendentals=2 * rows * vocab,
        ),
        name="score_part",
    )(places, ids, *pieces, *[pin(embedding)] * (2 * streams))


def draft_kernel(meta, hidden_hbm, weight_hbm, *refs):
    outs, columns, padded, sems = refs[:4], *refs[4:]
    depth = weight_hbm.shape[1]
    half = padded.shape[2]
    window = padded.shape[1]
    first = pl.multiple_of(meta[0], LANES)
    ask = pltpu.make_async_copy(hidden_hbm.at[:, pl.ds(first, window)], columns, sems.at[4])
    ask.start()
    padded[...] = jnp.zeros_like(padded)
    copies = []
    for k in (1, 2, 3, 0):
        quad = meta[2 + k]
        col = pl.multiple_of((quad & 1) * half, LANES)
        copies.append(
            pltpu.make_async_copy(
                weight_hbm.at[quad >> 1, :, pl.ds(col, half)],
                padded.at[k, pl.ds(pl.multiple_of(meta[1], 16), depth)],
                sems.at[k],
            )
        )
        copies[-1].start()
    ask.wait()
    for n, k in enumerate((1, 2, 3, 0)):
        copies[n].wait()
        partial = jnp.dot(columns[...], padded[k], preferred_element_type=jnp.float32)
        outs[k][...] = partial.astype(outs[k].dtype)


def draft_part(hidden, medusa_w, blk):
    rows, model = hidden.shape
    depth, units = medusa_w.shape[1:]
    half = units // 2
    window = -(-depth // LANES) * LANES + LANES
    start = blk * depth
    first = jnp.minimum(start // LANES * LANES, model - window)
    meta = jnp.stack([first, start - first] + [(blk & 3) ^ k for k in range(4)])
    return pl.pallas_call(
        draft_kernel,
        out_shape=[
            jax.ShapeDtypeStruct((rows, half), jnp.bfloat16 if k else jnp.float32)
            for k in range(4)
        ],
        in_specs=[in_smem(), in_hbm(), in_hbm()],
        out_specs=[in_vmem()] * 4,
        scratch_shapes=[
            pltpu.VMEM((rows, window), jnp.bfloat16),
            pltpu.VMEM((4, window, half), jnp.bfloat16),
            pltpu.SemaphoreType.DMA((5,)),
        ],
        compiler_params=limit(16),
        name="draft_part",
    )(meta, pin(hidden), pin(medusa_w))


def fold_kernel(place, own_ref, *refs):
    got, outs, hold = refs[:3], refs[3:-1], refs[-1]
    total = own_ref[...]
    for one in got:
        total = total + one[...].astype(jnp.float32)
    height = hold.shape[1]
    for j in range(len(outs)):
        hold[j] = total[j * height : (j + 1) * height]
    for k, out in enumerate(outs):
        out[...] = hold[place[0] ^ k].astype(out.dtype)


def fold_part(own, got, place, layers):
    rows, half = own.shape
    height = rows // layers
    return pl.pallas_call(
        fold_kernel,
        out_shape=[
            jax.ShapeDtypeStruct((height, half), jnp.bfloat16 if k else jnp.float32)
            for k in range(layers)
        ],
        in_specs=[in_smem()] + [in_vmem()] * 4,
        out_specs=[in_vmem()] * layers,
        scratch_shapes=[pltpu.VMEM((layers, height, half), jnp.float32)],
        compiler_params=limit(16),
        name="fold_part",
    )(place, own, *got)


def stack_kernel(place, *refs):
    parts, out_ref, hold, flat = refs[:-3], refs[-3], refs[-2], refs[-1]
    height = hold.shape[1]
    for k, part in enumerate(parts):
        hold[place[0] ^ k] = part[...].astype(jnp.float32)
    for j in range(len(parts)):
        flat[j * height : (j + 1) * height, :] = hold[j]
    out_ref[...] = flat[...].astype(jnp.bfloat16)


def stack_part(parts, place):
    layers = len(parts)
    height, half = parts[0].shape
    return pl.pallas_call(
        stack_kernel,
        out_shape=jax.ShapeDtypeStruct((layers * height, half), jnp.bfloat16),
        in_specs=[in_smem()] + [in_vmem()] * layers,
        out_specs=in_vmem(),
        scratch_shapes=[
            pltpu.VMEM((layers, height, half), jnp.float32),
            pltpu.VMEM((layers * height, half), jnp.float32),
        ],
        compiler_params=limit(16),
        name="stack_part",
    )(place, *parts)


def partner(value, axis, size, bits):
    return lax.ppermute(value, axis, [(i, i ^ bits) for i in range(size)])


def group_sum(value, axis, size, stride, count, beside=None):
    values = [value] + [partner(value, axis, size, k * stride) for k in range(1, count)]
    if beside is not None:
        values, _ = lax.optimization_barrier((values, beside))
    while len(values) > 1:
        values = [values[i] + values[i + 1] for i in range(0, len(values), 2)]
    return values[0]


def both_by_stages(hidden, parts, parents, units, blocks, blk, mp, prompt, merge):
    rows, model = hidden.shape
    half = units // 2
    layers = blocks // 4
    height = rows // layers
    layer = blk // 4
    place = layer.reshape(1)
    got = [partner(parts[k], "blk", blocks, k) for k in range(1, 4)]
    sent = prompt()
    partials = spread(sent)
    base = lax.dynamic_slice(
        hidden, (layer * height, mp * units + (blk & 1) * half), (height, half)
    )
    got, sent, base = lax.optimization_barrier((got, sent, base))
    parts = fold_part(parts[0], got, place, layers)
    parts, parents = lax.optimization_barrier((parts, parents))
    more = [partner(parts[k], "blk", blocks, 4 * k) for k in range(1, layers)]
    more, heads_out = lax.optimization_barrier((more, merge(partials, parents)))
    inner = parts[0] + sum(one.astype(jnp.float32) for one in more)
    own = (base.astype(jnp.float32) + jax.nn.silu(inner)).astype(jnp.bfloat16)
    own, heads_out = lax.optimization_barrier((own, heads_out))
    chunks = [own] + [partner(own, "blk", blocks, 4 * k) for k in range(1, layers)]
    chunks, heads_out = lax.optimization_barrier((chunks, spread(heads_out)))
    quad = stack_part(chunks, place)
    pieces = [quad] + [partner(quad, "blk", blocks, k) for k in range(1, 4)]
    pieces = pieces + [partner(piece, "mp", 2, 1) for piece in pieces]
    places = []
    for side in (mp, 1 - mp):
        for k in range(4):
            which = (blk & 3) ^ k
            places += [which >> 1, side * 2 + (which & 1)]
    return pieces, jnp.stack(places), heads_out


def spread(value):
    return lax.all_to_all(value, "blk", 0, 0, tiled=True)


def fresh_by_collectives(hidden, medusa_w, blocks, blk, mp):
    drafts, depth, units = medusa_w.shape
    rows = hidden.shape[0]
    own = drafts * rows // blocks
    hidden_cols = lax.dynamic_slice_in_dim(hidden, blk * depth, depth, 1)
    partial = jnp.einsum("rd,mdu->mru", hidden_cols, medusa_w, preferred_element_type=jnp.float32)
    partial = partial.reshape(blocks, own, units).astype(jnp.bfloat16)
    inner = lax.psum_scatter(partial, "blk", scatter_dimension=0).astype(jnp.float32)
    base = lax.dynamic_slice(hidden, ((blk * own) % rows, mp * units), (own, units))
    fresh = (base.astype(jnp.float32) + jax.nn.silu(inner)).astype(jnp.bfloat16)
    fresh = lax.all_gather(fresh, "blk", axis=0, tiled=True)
    return [lax.all_gather(fresh, "mp", axis=1, tiled=True)]


def per_device(
    hidden,
    medusa_w,
    embedding,
    cand_ids,
    tree_q,
    tree_key_value,
    prompt_key_value,
    block_group,
    block_len,
    block_empty,
    parents,
    out_weight,
    post_gain,
    resid,
):
    blocks, splits = lax.axis_size("blk"), lax.axis_size("mp")
    blk, mp = lax.axis_index("blk"), lax.axis_index("mp")
    drafts, depth, units = medusa_w.shape
    rows, model = hidden.shape
    lines = drafts * rows

    groups, tree_size, features = tree_q.shape
    width = features // blocks
    meta = jnp.concatenate([block_group, block_len, block_empty])

    def prompt():
        return prompt_part(tree_q, prompt_key_value, meta, width, blocks)

    def merge(partials, parents):
        numer, denom = tree_part(tree_q, tree_key_value, parents, blk * width, width)
        return merge_part(partials, numer, denom)

    if splits == 2 and blocks % 4 == 0 and units % 256 == 0 and drafts == 2:
        parts = draft_part(hidden, medusa_w, blk)
        parts, meta = lax.optimization_barrier((parts, meta))
        pieces, places, heads_out = both_by_stages(
            hidden, parts, parents, units, blocks, blk, mp, prompt, merge
        )
    else:
        pieces = fresh_by_collectives(hidden, medusa_w, blocks, blk, mp)
        places = jnp.zeros((2,), jnp.int32)
        heads_out = spread(merge(spread(prompt()), parents))
    attn = project_part(heads_out, out_weight)
    attn, pieces = lax.optimization_barrier((attn, pieces))
    attn = group_sum(attn, "mp", splits, 1, splits)
    normed = attn * lax.rsqrt(jnp.mean(attn * attn, -1, keepdims=True) + 1e-06) * post_gain
    layer_out = (normed + resid.astype(jnp.float32)).astype(jnp.bfloat16)

    vocab = embedding.shape[0]
    picks = cand_ids.shape[2]
    ids = cand_ids.reshape(lines, picks) - (blk * splits + mp) * vocab
    ids = jnp.pad(ids, ((0, 0), (0, LANES - picks)), constant_values=-1)
    score = score_part(places, pieces, embedding, ids, picks)
    score = group_sum(score, "mp", splits, 1, splits)
    score = group_sum(score, "blk", blocks, 1, 4, layer_out)
    score = group_sum(score, "blk", blocks, 4, blocks // 4)
    draft_logprob = score[:picks] - jnp.log(score[picks : picks + 1])
    draft_logprob = draft_logprob.T.reshape(drafts, rows, picks)
    return (draft_logprob, layer_out)


def solution(mesh):
    placed = (
        P(),
        P(None, "blk", "mp"),
        P(("blk", "mp"), None),
        P(),
        P(None, None, "mp"),
        P(None, None, None, "mp"),
        P(None, "blk", None, "mp"),
        P("blk"),
        P("blk"),
        P("blk"),
        P(),
        P("mp", None),
        P(),
        P("blk", None),
    )
    return jax.shard_map(
        per_device, mesh=mesh, in_specs=placed, out_specs=(P(), P("blk", None)), check_vma=False
    )
```

```python
import functools

import jax
import jax.numpy as jnp
from jax import lax
from jax.experimental import pallas as pl
from jax.experimental.pallas import tpu as pltpu
from jax.sharding import PartitionSpec as P

HEAD_SIZE = 256
LANES = 128
MIB = 1 << 20

EXTRA = 16
HIGH, LOW, GROUP = 0, 4, 8


def soft_weights(scores):
    return jnp.exp(50.0 * jnp.tanh(scores * (HEAD_SIZE**-0.5 / 50.0)))


def dot_t(left, right):
    return lax.dot_general(left, right, (((1,), (1,)), ((), ())), preferred_element_type=jnp.float32)


def in_hbm():
    return pl.BlockSpec(memory_space=pltpu.HBM)


def pin(value):
    return pltpu.with_memory_space_constraint(value, pltpu.HBM)


def in_vmem():
    return pl.BlockSpec(memory_space=pltpu.VMEM)


def in_smem():
    return pl.BlockSpec(memory_space=pltpu.SMEM)


def limit(mib):
    return pltpu.CompilerParams(vmem_limit_bytes=mib * MIB)


def prompt_kernel(meta, q_hbm, kv_hbm, out_ref, queries, held, sems):
    group, used, empty = meta[0], meta[1], meta[2]
    last = jnp.where(empty == 0, used, 0)
    kv_heads, slots = held.shape[1:3]
    tree_size, features = queries.shape
    repeats = features // HEAD_SIZE // kv_heads
    width = out_ref.shape[2]
    rows = tree_size * repeats
    ask = pltpu.make_async_copy(q_hbm.at[group], queries, sems.at[2 * kv_heads])
    ask.start()
    copies = [
        pltpu.make_async_copy(
            kv_hbm.at[s, 0, :, pl.ds(h * HEAD_SIZE, HEAD_SIZE)], held.at[s, h], sems.at[2 * h + s]
        )
        for h in range(kv_heads)
        for s in range(2)
    ]
    ahead = 4
    for copy in copies[:ahead]:
        copy.start()
    ask.wait()
    per_head = HEAD_SIZE // width
    row_id = lax.broadcasted_iota(jnp.int32, (tree_size, width), 0)
    lane_id = lax.broadcasted_iota(jnp.int32, (tree_size, width), 1)
    extra_id = lax.broadcasted_iota(jnp.int32, (EXTRA, width), 0)
    span = min(512, slots)
    slot = lax.broadcasted_iota(jnp.int32, (rows, span), 1)
    for h in range(kv_heads):
        asked = jnp.concatenate(
            [
                queries[:, (h * repeats + r) * HEAD_SIZE : (h * repeats + r + 1) * HEAD_SIZE]
                for r in range(repeats)
            ],
            axis=0,
        )
        copies[2 * h].wait()
        if 2 * h + ahead < len(copies):
            copies[2 * h + ahead].start()
        numer = jnp.zeros((rows, HEAD_SIZE), jnp.float32)
        sums = jnp.zeros((rows, LANES), jnp.float32)
        for start in range(0, slots, span):
            scores = dot_t(asked, held[0, h, start : start + span])
            weights = jnp.where(slot < last - start, soft_weights(scores), 0.0)
            for c in range(0, span, LANES):
                sums = sums + weights[:, c : c + LANES]
            if start == 0:
                copies[2 * h + 1].wait()
                if 2 * h + 1 + ahead < len(copies):
                    copies[2 * h + 1 + ahead].start()
            numer = numer + jnp.dot(
                weights.astype(jnp.bfloat16),
                held[1, h, start : start + span],
                preferred_element_type=jnp.float32,
            )
        denom = jnp.sum(sums, axis=1, keepdims=True)
        for r in range(repeats):
            mine = jnp.broadcast_to(denom[r * tree_size : (r + 1) * tree_size], (tree_size, width))
            extra = jnp.where(extra_id == GROUP, group.astype(jnp.float32), 0.0)
            for c in range(-(-tree_size // width)):
                line = jnp.sum(
                    jnp.where(row_id == lane_id + c * width, mine, 0.0), axis=0, keepdims=True
                )
                high = line.astype(jnp.bfloat16).astype(jnp.float32)
                extra = jnp.where(extra_id == HIGH + c, high, extra)
                extra = jnp.where(extra_id == LOW + c, line - high, extra)
            for part in range(per_head):
                d = (h * repeats + r) * per_head + part
                out_ref[d, :tree_size, :] = numer[
                    r * tree_size : (r + 1) * tree_size, part * width : (part + 1) * width
                ].astype(jnp.bfloat16)
                out_ref[d, tree_size:, :] = extra.astype(jnp.bfloat16)


def prompt_part(tree_q, prompt_key_value, meta, width, blocks):
    groups, tree_size, features = tree_q.shape
    slots, key_features = prompt_key_value.shape[2:]
    kv_heads = key_features // HEAD_SIZE
    return pl.pallas_call(
        prompt_kernel,
        out_shape=jax.ShapeDtypeStruct((blocks, tree_size + EXTRA, width), jnp.bfloat16),
        in_specs=[in_smem(), in_hbm(), in_hbm()],
        out_specs=in_vmem(),
        scratch_shapes=[
            pltpu.VMEM((tree_size, features), jnp.bfloat16),
            pltpu.VMEM((2, kv_heads, slots, HEAD_SIZE), jnp.bfloat16),
            pltpu.SemaphoreType.DMA((2 * kv_heads + 1,)),
        ],
        compiler_params=limit(24),
        cost_estimate=pl.CostEstimate(
            flops=4 * tree_size * features * slots,
            bytes_accessed=4 * slots * key_features,
            transcendentals=2 * tree_size * slots * features // HEAD_SIZE,
        ),
        name="prompt_part",
    )(meta, pin(tree_q), pin(prompt_key_value))


def tree_kernel(meta, q_hbm, kv_hbm, parents_ref, numer_ref, denom_ref, held, sems):
    width = numer_ref.shape[2]
    query_columns = pl.ds(pl.multiple_of(meta[0] * HEAD_SIZE, HEAD_SIZE), HEAD_SIZE)
    key_columns = pl.ds(pl.multiple_of(meta[1] * HEAD_SIZE, HEAD_SIZE), HEAD_SIZE)
    copies = [
        pltpu.make_async_copy(q_hbm.at[:, :, query_columns], held.at[0], sems.at[0]),
        pltpu.make_async_copy(kv_hbm.at[0, :, :, key_columns], held.at[1], sems.at[1]),
        pltpu.make_async_copy(kv_hbm.at[1, :, :, key_columns], held.at[2], sems.at[2]),
    ]
    for copy in copies:
        copy.start()
    groups, count = parents_ref.shape
    above = lax.broadcasted_iota(jnp.int32, (count, count), 0)
    token = lax.broadcasted_iota(jnp.int32, (count, count), 1)
    met = [
        jnp.where(
            (above == token) | ((parents_ref[g : g + 1, :] == above) & (token > 0)), 1.0, 0.0
        )
        for g in range(groups)
    ]
    for sweep in range(count.bit_length()):
        small = [one.astype(jnp.bfloat16) for one in met]
        met = [
            jnp.minimum(jnp.dot(one, one, preferred_element_type=jnp.float32), 1.0)
            for one in small
        ]
    for copy in copies:
        copy.wait()
    for g in range(groups):
        weights = soft_weights(dot_t(held[0, g], held[1, g])) * met[g].T
        denom_ref[g] = jnp.broadcast_to(
            jnp.sum(weights, axis=1, keepdims=True), denom_ref.shape[1:]
        )
        numer = jnp.dot(
            weights.astype(jnp.bfloat16), held[2, g], preferred_element_type=jnp.float32
        )
        mine = numer[:, :width]
        for j in range(1, HEAD_SIZE // width):
            mine = jnp.where(meta[2] == j, numer[:, j * width : (j + 1) * width], mine)
        numer_ref[g] = mine


def tree_part(tree_q, tree_key_value, parents, column, width):
    groups, tree_size, features = tree_q.shape
    repeats = features // tree_key_value.shape[3]
    head = column // HEAD_SIZE
    meta = jnp.stack([head, head // repeats, column % HEAD_SIZE // width])
    return pl.pallas_call(
        tree_kernel,
        out_shape=[jax.ShapeDtypeStruct((groups, tree_size, width), jnp.float32)] * 2,
        in_specs=[in_smem(), in_hbm(), in_hbm(), in_vmem()],
        out_specs=[in_vmem()] * 2,
        scratch_shapes=[
            pltpu.VMEM((3, groups, tree_size, HEAD_SIZE), jnp.bfloat16),
            pltpu.SemaphoreType.DMA((3,)),
        ],
        compiler_params=limit(16),
        name="tree_part",
    )(meta, pin(tree_q), pin(tree_key_value), parents)


def merge_kernel(got_ref, numer_ref, denom_ref, out_ref, hold, sums, lines):
    blocks = got_ref.shape[0]
    groups, tree_size, width = numer_ref.shape
    row_id = lax.broadcasted_iota(jnp.int32, (tree_size, width), 0)
    lane_id = lax.broadcasted_iota(jnp.int32, (tree_size, width), 1)
    sums[...] = numer_ref[...]
    lines[...] = jnp.zeros_like(lines)
    owners = []
    for b in range(blocks):
        extra = got_ref[b, tree_size:, :].astype(jnp.float32)
        owners.append(jnp.max(extra[GROUP : GROUP + 1, :]).astype(jnp.int32))
    for b in range(blocks):
        sums[owners[b]] += got_ref[b, :tree_size, :].astype(jnp.float32)
        lines[owners[b]] += got_ref[b, tree_size:, :].astype(jnp.float32)
    for g in range(groups):
        denom = denom_ref[g]
        for c in range(-(-tree_size // width)):
            line = lines[g, HIGH + c : HIGH + c + 1, :] + lines[g, LOW + c : LOW + c + 1, :]
            spread = jnp.where(row_id == lane_id + c * width, line, 0.0)
            denom = denom + jnp.sum(spread, axis=1, keepdims=True)
        hold[g * tree_size : (g + 1) * tree_size, :] = sums[g] / denom

    count = out_ref.shape[1]
    for d in range(out_ref.shape[0]):
        out_ref[d] = hold[d * count : (d + 1) * count, :].astype(jnp.bfloat16)


def merge_part(got, numer, denom):
    blocks, _, width = got.shape
    groups, tree_size, _ = numer.shape
    tokens = groups * tree_size
    return pl.pallas_call(
        merge_kernel,
        out_shape=jax.ShapeDtypeStruct((blocks, tokens // blocks, width), jnp.bfloat16),
        scratch_shapes=[
            pltpu.VMEM((tokens, width), jnp.float32),
            pltpu.VMEM((groups, tree_size, width), jnp.float32),
            pltpu.VMEM((groups, EXTRA, width), jnp.float32),
        ],
        compiler_params=limit(16),
        name="merge_part",
    )(got, numer, denom)


def project_kernel(heads_ref, weight_hbm, out_ref, ring, sems):
    slots, span = ring.shape[:2]
    steps = weight_hbm.shape[0] // span
    per_step = span // heads_ref.shape[2]

    def copy(i):
        return pltpu.make_async_copy(
            weight_hbm.at[i * span : (i + 1) * span], ring.at[i % slots], sems.at[i % slots]
        )

    for i in range(min(slots, steps)):
        copy(i).start()
    for i in range(steps):
        left = jnp.concatenate([heads_ref[i * per_step + j] for j in range(per_step)], axis=1)
        copy(i).wait()
        more = jnp.dot(left, ring[i % slots], preferred_element_type=jnp.float32)
        out_ref[...] = more if i == 0 else out_ref[...] + more
        if i + slots < steps:
            copy(i + slots).start()


def project_part(heads_out, out_weight):
    blocks, tokens, width = heads_out.shape
    features, model = out_weight.shape
    if width % LANES or features % HEAD_SIZE:
        flat = heads_out.transpose(1, 0, 2).reshape(tokens, features)
        return jnp.dot(flat, out_weight, preferred_element_type=jnp.float32)
    slots = 4
    return pl.pallas_call(
        project_kernel,
        out_shape=jax.ShapeDtypeStruct((tokens, model), jnp.float32),
        in_specs=[in_vmem(), in_hbm()],
        out_specs=in_vmem(),
        scratch_shapes=[
            pltpu.VMEM((slots, HEAD_SIZE, model), jnp.bfloat16),
            pltpu.SemaphoreType.DMA((slots,)),
        ],
        compiler_params=limit(20),
        cost_estimate=pl.CostEstimate(
            flops=2 * tokens * features * model,
            bytes_accessed=2 * features * model,
            transcendentals=0,
        ),
        name="project_part",
    )(heads_out, pin(out_weight))


def score_kernel(picks, streams, places, ids_ref, *refs):
    pieces, embeds, out_ref = refs[: -5 - 2 * streams], refs[-5 - 2 * streams : -5], refs[-5]
    fresh, total, picked, before = refs[-4:]
    step = pl.program_id(0)
    span = embeds[0].shape[0]
    rows = fresh.shape[0]
    band = 32 if rows % 32 == 0 else rows

    @pl.when(step == 0)
    def _():
        before[...] = jnp.zeros_like(before)
        for n, piece in enumerate(pieces):
            height, wide = piece.shape
            row = pl.multiple_of(places[2 * n] * height, 16)
            col = pl.multiple_of(places[2 * n + 1] * wide, LANES)
            fresh[pl.ds(row, height), pl.ds(col, wide)] = piece[...]

    def product(n):
        half = fresh.shape[1] // 2
        low, high = embeds[2 * n], embeds[2 * n + 1]
        return dot_t(fresh[:, :half], low[...]) + dot_t(fresh[:, half:], high[...])

    def absorb(raw, start, keep=None):
        for r in range(0, rows, band):
            ids = ids_ref[r : r + band] - start
            lane = ids & (LANES - 1)
            chunk = ids >> 7
            sums, found = total[r : r + band], picked[r : r + band]
            for c in range(span // LANES):
                part = jnp.tanh(raw[r : r + band, c * LANES : (c + 1) * LANES] * (1.0 / 30.0))
                sums = sums + jnp.exp(30.0 * part)
                there = jnp.take_along_axis(part, lane, axis=1, mode="promise_in_bounds")
                found = found + jnp.where(chunk == c, there, 0.0)
            if keep is not None:
                sums, found = jnp.where(keep, sums, 0.0), jnp.where(keep, found, 0.0)
            total[r : r + band] = sums
            picked[r : r + band] = found

    base = step * streams * span
    raw = product(0)
    absorb(before[...], base - span, step > 0)
    for n in range(1, streams):
        more = product(n)
        absorb(raw, base + (n - 1) * span)
        raw = more
    before[...] = raw

    @pl.when(step == pl.num_programs(0) - 1)
    def _():
        absorb(before[...], base + (streams - 1) * span)
        sums, found = total[...], picked[...]
        place = lax.broadcasted_iota(jnp.int32, sums.shape, 1)
        whole = jnp.sum(sums, axis=1, keepdims=True)
        both = jnp.where(place < picks, 30.0 * found, jnp.where(place == picks, whole, 0.0))
        out_ref[...] = both.T[: out_ref.shape[0]]


def score_part(places, pieces, embedding, ids, picks):
    rows = ids.shape[0]
    vocab, depth = embedding.shape
    span, streams = min(512, vocab), 1
    lines = -(-(picks + 1) // 8) * 8
    fixed = lambda i, places: (0, 0)
    return pl.pallas_call(
        functools.partial(score_kernel, picks, streams),
        out_shape=jax.ShapeDtypeStruct((lines, rows), jnp.float32),
        grid_spec=pltpu.PrefetchScalarGridSpec(
            num_scalar_prefetch=1,
            grid=(vocab // (span * streams),),
            in_specs=[pl.BlockSpec((rows, LANES), fixed)]
            + [pl.BlockSpec(piece.shape, fixed) for piece in pieces]
            + [
                pl.BlockSpec(
                    (span, depth // 2), lambda i, places, n=n, k=k: (i * streams + n, k)
                )
                for n in range(streams)
                for k in range(2)
            ],
            out_specs=pl.BlockSpec((lines, rows), fixed),
            scratch_shapes=[pltpu.VMEM((rows, depth), jnp.bfloat16)]
            + [pltpu.VMEM((rows, LANES), jnp.float32)] * 2
            + [pltpu.VMEM((rows, span), jnp.float32)],
        ),
        compiler_params=limit(32),
        cost_estimate=pl.CostEstimate(
            flops=2 * rows * depth * vocab,
            bytes_accessed=2 * vocab * depth,
            transcendentals=2 * rows * vocab,
        ),
        name="score_part",
    )(places, ids, *pieces, *[pin(embedding)] * (2 * streams))


def draft_kernel(meta, hidden_hbm, weight_hbm, *refs):
    outs, base_ref, columns, padded, sems = refs[:4], *refs[4:]
    depth = weight_hbm.shape[1]
    half = padded.shape[2]
    window = padded.shape[1]
    first = pl.multiple_of(meta[0], LANES)
    ask = pltpu.make_async_copy(hidden_hbm.at[:, pl.ds(first, window)], columns, sems.at[4])
    ask.start()
    padded[...] = jnp.zeros_like(padded)
    copies = []
    for k in (1, 2, 3, 0):
        quad = meta[2 + k]
        col = pl.multiple_of((quad & 1) * half, LANES)
        copies.append(
            pltpu.make_async_copy(
                weight_hbm.at[quad >> 1, :, pl.ds(col, half)],
                padded.at[k, pl.ds(pl.multiple_of(meta[1], 16), depth)],
                sems.at[k],
            )
        )
        copies[-1].start()
    base_columns = pl.ds(pl.multiple_of(meta[6], LANES), half)
    base = pltpu.make_async_copy(hidden_hbm.at[:, base_columns], base_ref, sems.at[5])
    base.start()
    ask.wait()
    for n, k in enumerate((1, 2, 3, 0)):
        copies[n].wait()
        partial = jnp.dot(columns[...], padded[k], preferred_element_type=jnp.float32)
        outs[k][...] = partial.astype(outs[k].dtype)
    base.wait()


def draft_part(hidden, medusa_w, blk, mp):
    rows, model = hidden.shape
    depth, units = medusa_w.shape[1:]
    half = units // 2
    window = -(-depth // LANES) * LANES + LANES
    start = blk * depth
    first = jnp.minimum(start // LANES * LANES, model - window)
    meta = [first, start - first] + [(blk & 3) ^ k for k in range(4)]
    meta = jnp.stack(meta + [mp * units + (blk & 1) * half])
    return pl.pallas_call(
        draft_kernel,
        out_shape=[
            jax.ShapeDtypeStruct((rows, half), jnp.bfloat16 if k else jnp.float32)
            for k in range(5)
        ],
        in_specs=[in_smem(), in_hbm(), in_hbm()],
        out_specs=[in_vmem()] * 5,
        scratch_shapes=[
            pltpu.VMEM((rows, window), jnp.bfloat16),
            pltpu.VMEM((4, window, half), jnp.bfloat16),
            pltpu.SemaphoreType.DMA((6,)),
        ],
        compiler_params=limit(16),
        name="draft_part",
    )(meta, pin(hidden), pin(medusa_w))


def fold_kernel(place, base_ref, own_ref, *refs):
    got, chunk_ref, outs, hold = refs[:3], refs[3], refs[4:-1], refs[-1]
    height = hold.shape[1]

    def cut(whole):
        for j in range(len(outs)):
            hold[j] = whole[j * height : (j + 1) * height]

    cut(base_ref[...].astype(jnp.float32))
    chunk_ref[...] = hold[place[0]]
    total = own_ref[...]
    for one in got:
        total = total + one[...].astype(jnp.float32)
    cut(total)
    for k, out in enumerate(outs):
        out[...] = hold[place[0] ^ k].astype(out.dtype)


def fold_part(base, own, got, place, layers):
    rows, half = own.shape
    height = rows // layers
    kinds = [jnp.float32, jnp.float32] + [jnp.bfloat16] * (layers - 1)
    return pl.pallas_call(
        fold_kernel,
        out_shape=[jax.ShapeDtypeStruct((height, half), kind) for kind in kinds],
        in_specs=[in_smem()] + [in_vmem()] * 5,
        out_specs=[in_vmem()] * (1 + layers),
        scratch_shapes=[pltpu.VMEM((layers, height, half), jnp.float32)],
        compiler_params=limit(16),
        name="fold_part",
    )(place, base, own, *got)


def stack_kernel(place, *refs):
    parts, out_ref, hold, flat = refs[:-3], refs[-3], refs[-2], refs[-1]
    height = hold.shape[1]
    for k, part in enumerate(parts):
        hold[place[0] ^ k] = part[...].astype(jnp.float32)
    for j in range(len(parts)):
        flat[j * height : (j + 1) * height, :] = hold[j]
    out_ref[...] = flat[...].astype(jnp.bfloat16)


def stack_part(parts, place):
    layers = len(parts)
    height, half = parts[0].shape
    return pl.pallas_call(
        stack_kernel,
        out_shape=jax.ShapeDtypeStruct((layers * height, half), jnp.bfloat16),
        in_specs=[in_smem()] + [in_vmem()] * layers,
        out_specs=in_vmem(),
        scratch_shapes=[
            pltpu.VMEM((layers, height, half), jnp.float32),
            pltpu.VMEM((layers * height, half), jnp.float32),
        ],
        compiler_params=limit(16),
        name="stack_part",
    )(place, *parts)


def partner(value, axis, size, bits):
    return lax.ppermute(value, axis, [(i, i ^ bits) for i in range(size)])


def group_sum(value, axis, size, stride, count):
    values = [value] + [partner(value, axis, size, k * stride) for k in range(1, count)]
    while len(values) > 1:
        values = [values[i] + values[i + 1] for i in range(0, len(values), 2)]
    return values[0]


def both_by_stages(parts, parents, blocks, blk, mp, prompt, merge):
    layers = blocks // 4
    place = (blk // 4).reshape(1)
    got = [partner(parts[k], "blk", blocks, k) for k in range(1, 4)]
    sent = prompt()
    partials = spread(sent)
    got, sent = lax.optimization_barrier((got, sent))
    parts = fold_part(parts[4], parts[0], got, place, layers)
    parts, parents = lax.optimization_barrier((parts, parents))
    more = [partner(parts[1 + k], "blk", blocks, 4 * k) for k in range(1, layers)]
    more, heads_out = lax.optimization_barrier((more, merge(partials, parents)))
    inner = parts[1] + sum(one.astype(jnp.float32) for one in more)
    own = (parts[0] + jax.nn.silu(inner)).astype(jnp.bfloat16)
    own, heads_out = lax.optimization_barrier((own, heads_out))
    chunks = [own] + [partner(own, "blk", blocks, 4 * k) for k in range(1, layers)]
    quad = stack_part(chunks, place)
    pieces = [quad] + [partner(quad, "blk", blocks, k) for k in range(1, 4)]
    pieces = pieces + [partner(piece, "mp", 2, 1) for piece in pieces]
    places = []
    for side in (mp, 1 - mp):
        for k in range(4):
            which = (blk & 3) ^ k
            places += [which >> 1, side * 2 + (which & 1)]
    return pieces, jnp.stack(places), spread(heads_out)


def spread(value):
    return lax.all_to_all(value, "blk", 0, 0, tiled=True)


def fresh_by_collectives(hidden, medusa_w, blocks, blk, mp):
    drafts, depth, units = medusa_w.shape
    rows = hidden.shape[0]
    own = drafts * rows // blocks
    hidden_cols = lax.dynamic_slice_in_dim(hidden, blk * depth, depth, 1)
    partial = jnp.einsum("rd,mdu->mru", hidden_cols, medusa_w, preferred_element_type=jnp.float32)
    partial = partial.reshape(blocks, own, units).astype(jnp.bfloat16)
    inner = lax.psum_scatter(partial, "blk", scatter_dimension=0).astype(jnp.float32)
    base = lax.dynamic_slice(hidden, ((blk * own) % rows, mp * units), (own, units))
    fresh = (base.astype(jnp.float32) + jax.nn.silu(inner)).astype(jnp.bfloat16)
    fresh = lax.all_gather(fresh, "blk", axis=0, tiled=True)
    return [lax.all_gather(fresh, "mp", axis=1, tiled=True)]


def per_device(
    hidden,
    medusa_w,
    embedding,
    cand_ids,
    tree_q,
    tree_key_value,
    prompt_key_value,
    block_group,
    block_len,
    block_empty,
    parents,
    out_weight,
    post_gain,
    resid,
):
    blocks, splits = lax.axis_size("blk"), lax.axis_size("mp")
    blk, mp = lax.axis_index("blk"), lax.axis_index("mp")
    drafts, depth, units = medusa_w.shape
    rows, model = hidden.shape
    lines = drafts * rows

    groups, tree_size, features = tree_q.shape
    width = features // blocks
    meta = jnp.concatenate([block_group, block_len, block_empty])

    def prompt():
        return prompt_part(tree_q, prompt_key_value, meta, width, blocks)

    def merge(partials, parents):
        numer, denom = tree_part(tree_q, tree_key_value, parents, blk * width, width)
        return merge_part(partials, numer, denom)

    if splits == 2 and blocks % 4 == 0 and units % 256 == 0 and drafts == 2:
        parts = draft_part(hidden, medusa_w, blk, mp)
        parts, meta = lax.optimization_barrier((parts, meta))
        pieces, places, heads_out = both_by_stages(
            parts, parents, blocks, blk, mp, prompt, merge
        )
    else:
        pieces = fresh_by_collectives(hidden, medusa_w, blocks, blk, mp)
        places = jnp.zeros((2,), jnp.int32)
        heads_out = spread(merge(spread(prompt()), parents))
    vocab = embedding.shape[0]
    picks = cand_ids.shape[2]
    ids = cand_ids.reshape(lines, picks) - (blk * splits + mp) * vocab
    ids = jnp.pad(ids, ((0, 0), (0, LANES - picks)), constant_values=-1)
    score = score_part(places, pieces, embedding, ids, picks)
    score = group_sum(score, "mp", splits, 1, splits)
    score, heads_out = lax.optimization_barrier((score, heads_out))
    score = group_sum(score, "blk", blocks, 1, 4)
    score = group_sum(score, "blk", blocks, 4, blocks // 4)
    draft_logprob = score[:picks] - jnp.log(score[picks : picks + 1])
    draft_logprob = draft_logprob.T.reshape(drafts, rows, picks)

    attn = project_part(heads_out, out_weight)
    attn = group_sum(attn, "mp", splits, 1, splits)
    normed = attn * lax.rsqrt(jnp.mean(attn * attn, -1, keepdims=True) + 1e-06) * post_gain
    layer_out = (normed + resid.astype(jnp.float32)).astype(jnp.bfloat16)
    return (draft_logprob, layer_out)


def solution(mesh):
    placed = (
        P(),
        P(None, "blk", "mp"),
        P(("blk", "mp"), None),
        P(),
        P(None, None, "mp"),
        P(None, None, None, "mp"),
        P(None, "blk", None, "mp"),
        P("blk"),
        P("blk"),
        P("blk"),
        P(),
        P("mp", None),
        P(),
        P("blk", None),
    )
    return jax.shard_map(
        per_device, mesh=mesh, in_specs=placed, out_specs=(P(), P("blk", None)), check_vma=False
    )
```

```python
import functools

import jax
import jax.numpy as jnp
from jax import lax
from jax.experimental import pallas as pl
from jax.experimental.pallas import tpu as pltpu
from jax.sharding import PartitionSpec as P

HEAD_SIZE = 256
LANES = 128
MIB = 1 << 20
LOG2_E = 1.4426950408889634

EXTRA = 16
HIGH, LOW, GROUP = 0, 4, 8


def soft_weights(scores):
    return jnp.exp(50.0 * jnp.tanh(scores * (HEAD_SIZE**-0.5 / 50.0)))


def dot_t(left, right):
    return lax.dot_general(left, right, (((1,), (1,)), ((), ())), preferred_element_type=jnp.float32)


def in_hbm():
    return pl.BlockSpec(memory_space=pltpu.HBM)


def pin(value):
    return pltpu.with_memory_space_constraint(value, pltpu.HBM)


def in_vmem():
    return pl.BlockSpec(memory_space=pltpu.VMEM)


def in_smem():
    return pl.BlockSpec(memory_space=pltpu.SMEM)


def limit(mib):
    return pltpu.CompilerParams(vmem_limit_bytes=mib * MIB)


def prompt_kernel(meta, q_hbm, kv_hbm, out_ref, queries, held, sems):
    group, used, empty = meta[0], meta[1], meta[2]
    last = jnp.where(empty == 0, used, 0)
    kv_heads, slots = held.shape[1:3]
    tree_size, features = queries.shape
    repeats = features // HEAD_SIZE // kv_heads
    width = out_ref.shape[2]
    rows = tree_size * repeats
    ask = pltpu.make_async_copy(q_hbm.at[group], queries, sems.at[2 * kv_heads])
    ask.start()
    copies = [
        pltpu.make_async_copy(
            kv_hbm.at[s, 0, :, pl.ds(h * HEAD_SIZE, HEAD_SIZE)], held.at[s, h], sems.at[2 * h + s]
        )
        for h in range(kv_heads)
        for s in range(2)
    ]
    ahead = 4
    for copy in copies[:ahead]:
        copy.start()
    ask.wait()
    per_head = HEAD_SIZE // width
    row_id = lax.broadcasted_iota(jnp.int32, (tree_size, width), 0)
    lane_id = lax.broadcasted_iota(jnp.int32, (tree_size, width), 1)
    extra_id = lax.broadcasted_iota(jnp.int32, (EXTRA, width), 0)
    span = min(512, slots)
    slot = lax.broadcasted_iota(jnp.int32, (rows, span), 1)
    for h in range(kv_heads):
        asked = jnp.concatenate(
            [
                queries[:, (h * repeats + r) * HEAD_SIZE : (h * repeats + r + 1) * HEAD_SIZE]
                for r in range(repeats)
            ],
            axis=0,
        )
        copies[2 * h].wait()
        if 2 * h + ahead < len(copies):
            copies[2 * h + ahead].start()
        numer = jnp.zeros((rows, HEAD_SIZE), jnp.float32)
        sums = jnp.zeros((rows, LANES), jnp.float32)
        for start in range(0, slots, span):
            scores = dot_t(asked, held[0, h, start : start + span])
            weights = jnp.where(slot < last - start, soft_weights(scores), 0.0)
            for c in range(0, span, LANES):
                sums = sums + weights[:, c : c + LANES]
            if start == 0:
                copies[2 * h + 1].wait()
                if 2 * h + 1 + ahead < len(copies):
                    copies[2 * h + 1 + ahead].start()
            numer = numer + jnp.dot(
                weights.astype(jnp.bfloat16),
                held[1, h, start : start + span],
                preferred_element_type=jnp.float32,
            )
        denom = jnp.sum(sums, axis=1, keepdims=True)
        for r in range(repeats):
            mine = jnp.broadcast_to(denom[r * tree_size : (r + 1) * tree_size], (tree_size, width))
            extra = jnp.where(extra_id == GROUP, group.astype(jnp.float32), 0.0)
            for c in range(-(-tree_size // width)):
                line = jnp.sum(
                    jnp.where(row_id == lane_id + c * width, mine, 0.0), axis=0, keepdims=True
                )
                high = line.astype(jnp.bfloat16).astype(jnp.float32)
                extra = jnp.where(extra_id == HIGH + c, high, extra)
                extra = jnp.where(extra_id == LOW + c, line - high, extra)
            for part in range(per_head):
                d = (h * repeats + r) * per_head + part
                out_ref[d, :tree_size, :] = numer[
                    r * tree_size : (r + 1) * tree_size, part * width : (part + 1) * width
                ].astype(jnp.bfloat16)
                out_ref[d, tree_size:, :] = extra.astype(jnp.bfloat16)


def prompt_part(tree_q, prompt_key_value, meta, width, blocks):
    groups, tree_size, features = tree_q.shape
    slots, key_features = prompt_key_value.shape[2:]
    kv_heads = key_features // HEAD_SIZE
    return pl.pallas_call(
        prompt_kernel,
        out_shape=jax.ShapeDtypeStruct((blocks, tree_size + EXTRA, width), jnp.bfloat16),
        in_specs=[in_smem(), in_hbm(), in_hbm()],
        out_specs=in_vmem(),
        scratch_shapes=[
            pltpu.VMEM((tree_size, features), jnp.bfloat16),
            pltpu.VMEM((2, kv_heads, slots, HEAD_SIZE), jnp.bfloat16),
            pltpu.SemaphoreType.DMA((2 * kv_heads + 1,)),
        ],
        compiler_params=limit(24),
        cost_estimate=pl.CostEstimate(
            flops=4 * tree_size * features * slots,
            bytes_accessed=4 * slots * key_features,
            transcendentals=2 * tree_size * slots * features // HEAD_SIZE,
        ),
        name="prompt_part",
    )(meta, pin(tree_q), pin(prompt_key_value))


def tree_kernel(meta, q_hbm, kv_hbm, parents_ref, numer_ref, denom_ref, held, sems):
    width = numer_ref.shape[2]
    query_columns = pl.ds(pl.multiple_of(meta[0] * HEAD_SIZE, HEAD_SIZE), HEAD_SIZE)
    key_columns = pl.ds(pl.multiple_of(meta[1] * HEAD_SIZE, HEAD_SIZE), HEAD_SIZE)
    copies = [
        pltpu.make_async_copy(q_hbm.at[:, :, query_columns], held.at[0], sems.at[0]),
        pltpu.make_async_copy(kv_hbm.at[0, :, :, key_columns], held.at[1], sems.at[1]),
        pltpu.make_async_copy(kv_hbm.at[1, :, :, key_columns], held.at[2], sems.at[2]),
    ]
    for copy in copies:
        copy.start()
    groups, count = parents_ref.shape
    above = lax.broadcasted_iota(jnp.int32, (count, count), 0)
    token = lax.broadcasted_iota(jnp.int32, (count, count), 1)
    met = [
        jnp.where(
            (above == token) | ((parents_ref[g : g + 1, :] == above) & (token > 0)), 1.0, 0.0
        )
        for g in range(groups)
    ]
    for sweep in range(count.bit_length()):
        small = [one.astype(jnp.bfloat16) for one in met]
        met = [
            jnp.minimum(jnp.dot(one, one, preferred_element_type=jnp.float32), 1.0)
            for one in small
        ]
    for copy in copies:
        copy.wait()
    for g in range(groups):
        weights = soft_weights(dot_t(held[0, g], held[1, g])) * met[g].T
        denom_ref[g] = jnp.broadcast_to(
            jnp.sum(weights, axis=1, keepdims=True), denom_ref.shape[1:]
        )
        numer = jnp.dot(
            weights.astype(jnp.bfloat16), held[2, g], preferred_element_type=jnp.float32
        )
        mine = numer[:, :width]
        for j in range(1, HEAD_SIZE // width):
            mine = jnp.where(meta[2] == j, numer[:, j * width : (j + 1) * width], mine)
        numer_ref[g] = mine


def tree_part(tree_q, tree_key_value, parents, column, width):
    groups, tree_size, features = tree_q.shape
    repeats = features // tree_key_value.shape[3]
    head = column // HEAD_SIZE
    meta = jnp.stack([head, head // repeats, column % HEAD_SIZE // width])
    return pl.pallas_call(
        tree_kernel,
        out_shape=[jax.ShapeDtypeStruct((groups, tree_size, width), jnp.float32)] * 2,
        in_specs=[in_smem(), in_hbm(), in_hbm(), in_vmem()],
        out_specs=[in_vmem()] * 2,
        scratch_shapes=[
            pltpu.VMEM((3, groups, tree_size, HEAD_SIZE), jnp.bfloat16),
            pltpu.SemaphoreType.DMA((3,)),
        ],
        compiler_params=limit(16),
        cost_estimate=pl.CostEstimate(flops=0, bytes_accessed=20 * MIB, transcendentals=0),
        name="tree_part",
    )(meta, pin(tree_q), pin(tree_key_value), parents)


def merge_kernel(got_ref, numer_ref, denom_ref, out_ref, hold, sums, lines):
    blocks = got_ref.shape[0]
    groups, tree_size, width = numer_ref.shape
    row_id = lax.broadcasted_iota(jnp.int32, (tree_size, width), 0)
    lane_id = lax.broadcasted_iota(jnp.int32, (tree_size, width), 1)
    sums[...] = numer_ref[...]
    lines[...] = jnp.zeros_like(lines)
    owners = []
    for b in range(blocks):
        extra = got_ref[b, tree_size:, :].astype(jnp.float32)
        owners.append(jnp.max(extra[GROUP : GROUP + 1, :]).astype(jnp.int32))
    for b in range(blocks):
        sums[owners[b]] += got_ref[b, :tree_size, :].astype(jnp.float32)
        lines[owners[b]] += got_ref[b, tree_size:, :].astype(jnp.float32)
    for g in range(groups):
        denom = denom_ref[g]
        for c in range(-(-tree_size // width)):
            line = lines[g, HIGH + c : HIGH + c + 1, :] + lines[g, LOW + c : LOW + c + 1, :]
            spread = jnp.where(row_id == lane_id + c * width, line, 0.0)
            denom = denom + jnp.sum(spread, axis=1, keepdims=True)
        hold[g * tree_size : (g + 1) * tree_size, :] = sums[g] / denom

    count = out_ref.shape[1]
    for d in range(out_ref.shape[0]):
        out_ref[d] = hold[d * count : (d + 1) * count, :].astype(jnp.bfloat16)


def merge_part(got, numer, denom):
    blocks, _, width = got.shape
    groups, tree_size, _ = numer.shape
    tokens = groups * tree_size
    return pl.pallas_call(
        merge_kernel,
        out_shape=jax.ShapeDtypeStruct((blocks, tokens // blocks, width), jnp.bfloat16),
        scratch_shapes=[
            pltpu.VMEM((tokens, width), jnp.float32),
            pltpu.VMEM((groups, tree_size, width), jnp.float32),
            pltpu.VMEM((groups, EXTRA, width), jnp.float32),
        ],
        compiler_params=limit(16),
        name="merge_part",
    )(got, numer, denom)


def project_kernel(heads_ref, weight_hbm, out_ref, ring, sems):
    slots, span = ring.shape[:2]
    steps = weight_hbm.shape[0] // span
    per_step = span // heads_ref.shape[2]

    def copy(i):
        return pltpu.make_async_copy(
            weight_hbm.at[i * span : (i + 1) * span], ring.at[i % slots], sems.at[i % slots]
        )

    for i in range(min(slots, steps)):
        copy(i).start()
    for i in range(steps):
        left = jnp.concatenate([heads_ref[i * per_step + j] for j in range(per_step)], axis=1)
        copy(i).wait()
        more = jnp.dot(left, ring[i % slots], preferred_element_type=jnp.float32)
        out_ref[...] = more if i == 0 else out_ref[...] + more
        if i + slots < steps:
            copy(i + slots).start()


def project_part(heads_out, out_weight):
    blocks, tokens, width = heads_out.shape
    features, model = out_weight.shape
    if width % LANES or features % HEAD_SIZE:
        flat = heads_out.transpose(1, 0, 2).reshape(tokens, features)
        return jnp.dot(flat, out_weight, preferred_element_type=jnp.float32)
    slots = 4
    return pl.pallas_call(
        project_kernel,
        out_shape=jax.ShapeDtypeStruct((tokens, model), jnp.float32),
        in_specs=[in_vmem(), in_hbm()],
        out_specs=in_vmem(),
        scratch_shapes=[
            pltpu.VMEM((slots, HEAD_SIZE, model), jnp.bfloat16),
            pltpu.SemaphoreType.DMA((slots,)),
        ],
        compiler_params=limit(20),
        cost_estimate=pl.CostEstimate(
            flops=2 * tokens * features * model,
            bytes_accessed=2 * features * model,
            transcendentals=0,
        ),
        name="project_part",
    )(heads_out, pin(out_weight))


def score_kernel(picks, streams, places, ids_ref, *refs):
    pieces, embeds, out_ref = refs[: -5 - 2 * streams], refs[-5 - 2 * streams : -5], refs[-5]
    fresh, total, picked, before = refs[-4:]
    step = pl.program_id(0)
    span = embeds[0].shape[0]
    rows = fresh.shape[0]
    band = 32 if rows % 32 == 0 else rows

    @pl.when(step == 0)
    def _():
        before[...] = jnp.zeros_like(before)
        for n, piece in enumerate(pieces):
            height, wide = piece.shape
            row = pl.multiple_of(places[2 * n] * height, 16)
            col = pl.multiple_of(places[2 * n + 1] * wide, LANES)
            fresh[pl.ds(row, height), pl.ds(col, wide)] = piece[...]

    def product(n):
        half = fresh.shape[1] // 2
        low, high = embeds[2 * n], embeds[2 * n + 1]
        return dot_t(fresh[:, :half], low[...]) + dot_t(fresh[:, half:], high[...])

    def absorb(raw, start, keep=None):
        for r in range(0, rows, band):
            ids = ids_ref[r : r + band] - start
            lane = ids & (LANES - 1)
            chunk = ids >> 7
            sums, found = total[r : r + band], picked[r : r + band]
            for c in range(span // LANES):
                part = jnp.tanh(raw[r : r + band, c * LANES : (c + 1) * LANES] * (1.0 / 30.0))
                sums = sums + jnp.exp2(part * (30.0 * LOG2_E))
                there = jnp.take_along_axis(part, lane, axis=1, mode="promise_in_bounds")
                found = found + jnp.where(chunk == c, there, 0.0)
            if keep is not None:
                sums, found = jnp.where(keep, sums, 0.0), jnp.where(keep, found, 0.0)
            total[r : r + band] = sums
            picked[r : r + band] = found

    base = step * streams * span
    raw = product(0)
    absorb(before[...], base - span, step > 0)
    for n in range(1, streams):
        more = product(n)
        absorb(raw, base + (n - 1) * span)
        raw = more
    before[...] = raw

    @pl.when(step == pl.num_programs(0) - 1)
    def _():
        absorb(before[...], base + (streams - 1) * span)
        sums, found = total[...], picked[...]
        place = lax.broadcasted_iota(jnp.int32, sums.shape, 1)
        whole = jnp.sum(sums, axis=1, keepdims=True)
        both = jnp.where(place < picks, 30.0 * found, jnp.where(place == picks, whole, 0.0))
        out_ref[...] = both.T[: out_ref.shape[0]]


def score_part(places, pieces, embedding, ids, picks):
    rows = ids.shape[0]
    vocab, depth = embedding.shape
    span, streams = min(512, vocab), 1
    lines = -(-(picks + 1) // 8) * 8
    fixed = lambda i, places: (0, 0)
    return pl.pallas_call(
        functools.partial(score_kernel, picks, streams),
        out_shape=jax.ShapeDtypeStruct((lines, rows), jnp.float32),
        grid_spec=pltpu.PrefetchScalarGridSpec(
            num_scalar_prefetch=1,
            grid=(vocab // (span * streams),),
            in_specs=[pl.BlockSpec((rows, LANES), fixed)]
            + [pl.BlockSpec(piece.shape, fixed) for piece in pieces]
            + [
                pl.BlockSpec(
                    (span, depth // 2), lambda i, places, n=n, k=k: (i * streams + n, k)
                )
                for n in range(streams)
                for k in range(2)
            ],
            out_specs=pl.BlockSpec((lines, rows), fixed),
            scratch_shapes=[pltpu.VMEM((rows, depth), jnp.bfloat16)]
            + [pltpu.VMEM((rows, LANES), jnp.float32)] * 2
            + [pltpu.VMEM((rows, span), jnp.float32)],
        ),
        compiler_params=limit(32),
        cost_estimate=pl.CostEstimate(
            flops=2 * rows * depth * vocab,
            bytes_accessed=2 * vocab * depth,
            transcendentals=2 * rows * vocab,
        ),
        name="score_part",
    )(places, ids, *pieces, *[pin(embedding)] * (2 * streams))


def draft_kernel(meta, hidden_hbm, weight_hbm, *refs):
    outs, base_ref, columns, padded, sems = refs[:4], *refs[4:]
    depth = weight_hbm.shape[1]
    half = padded.shape[2]
    window = padded.shape[1]
    first = pl.multiple_of(meta[0], LANES)
    ask = pltpu.make_async_copy(hidden_hbm.at[:, pl.ds(first, window)], columns, sems.at[4])
    ask.start()
    padded[...] = jnp.zeros_like(padded)
    copies = []
    for k in (1, 2, 3, 0):
        quad = meta[2 + k]
        col = pl.multiple_of((quad & 1) * half, LANES)
        copies.append(
            pltpu.make_async_copy(
                weight_hbm.at[quad >> 1, :, pl.ds(col, half)],
                padded.at[k, pl.ds(pl.multiple_of(meta[1], 16), depth)],
                sems.at[k],
            )
        )
        copies[-1].start()
    base_columns = pl.ds(pl.multiple_of(meta[6], LANES), half)
    base = pltpu.make_async_copy(hidden_hbm.at[:, base_columns], base_ref, sems.at[5])
    base.start()
    ask.wait()
    for n, k in enumerate((1, 2, 3, 0)):
        copies[n].wait()
        partial = jnp.dot(columns[...], padded[k], preferred_element_type=jnp.float32)
        outs[k][...] = partial.astype(outs[k].dtype)
    base.wait()


def draft_part(hidden, medusa_w, blk, mp):
    rows, model = hidden.shape
    depth, units = medusa_w.shape[1:]
    half = units // 2
    window = -(-depth // LANES) * LANES + LANES
    start = blk * depth
    first = jnp.minimum(start // LANES * LANES, model - window)
    meta = [first, start - first] + [(blk & 3) ^ k for k in range(4)]
    meta = jnp.stack(meta + [mp * units + (blk & 1) * half])
    return pl.pallas_call(
        draft_kernel,
        out_shape=[
            jax.ShapeDtypeStruct((rows, half), jnp.bfloat16 if k else jnp.float32)
            for k in range(5)
        ],
        in_specs=[in_smem(), in_hbm(), in_hbm()],
        out_specs=[in_vmem()] * 5,
        scratch_shapes=[
            pltpu.VMEM((rows, window), jnp.bfloat16),
            pltpu.VMEM((4, window, half), jnp.bfloat16),
            pltpu.SemaphoreType.DMA((6,)),
        ],
        compiler_params=limit(16),
        name="draft_part",
    )(meta, pin(hidden), pin(medusa_w))


def fold_kernel(place, base_ref, own_ref, *refs):
    got, chunk_ref, outs, hold = refs[:3], refs[3], refs[4:-1], refs[-1]
    height = hold.shape[1]

    def cut(whole):
        for j in range(len(outs)):
            hold[j] = whole[j * height : (j + 1) * height]

    cut(base_ref[...].astype(jnp.float32))
    chunk_ref[...] = hold[place[0]]
    total = own_ref[...]
    for one in got:
        total = total + one[...].astype(jnp.float32)
    cut(total)
    for k, out in enumerate(outs):
        out[...] = hold[place[0] ^ k].astype(out.dtype)


def fold_part(base, own, got, place, layers):
    rows, half = own.shape
    height = rows // layers
    kinds = [jnp.float32, jnp.float32] + [jnp.bfloat16] * (layers - 1)
    return pl.pallas_call(
        fold_kernel,
        out_shape=[jax.ShapeDtypeStruct((height, half), kind) for kind in kinds],
        in_specs=[in_smem()] + [in_vmem()] * 5,
        out_specs=[in_vmem()] * (1 + layers),
        scratch_shapes=[pltpu.VMEM((layers, height, half), jnp.float32)],
        compiler_params=limit(16),
        name="fold_part",
    )(place, base, own, *got)


def stack_kernel(place, *refs):
    parts, out_ref, hold, flat = refs[:-3], refs[-3], refs[-2], refs[-1]
    height = hold.shape[1]
    for k, part in enumerate(parts):
        hold[place[0] ^ k] = part[...].astype(jnp.float32)
    for j in range(len(parts)):
        flat[j * height : (j + 1) * height, :] = hold[j]
    out_ref[...] = flat[...].astype(jnp.bfloat16)


def stack_part(parts, place):
    layers = len(parts)
    height, half = parts[0].shape
    return pl.pallas_call(
        stack_kernel,
        out_shape=jax.ShapeDtypeStruct((layers * height, half), jnp.bfloat16),
        in_specs=[in_smem()] + [in_vmem()] * layers,
        out_specs=in_vmem(),
        scratch_shapes=[
            pltpu.VMEM((layers, height, half), jnp.float32),
            pltpu.VMEM((layers * height, half), jnp.float32),
        ],
        compiler_params=limit(16),
        name="stack_part",
    )(place, *parts)


def partner(value, axis, size, bits):
    return lax.ppermute(value, axis, [(i, i ^ bits) for i in range(size)])


def group_sum(value, axis, size, stride, count, beside=None):
    values = [value] + [partner(value, axis, size, k * stride) for k in range(1, count)]
    if beside is not None:
        values, _ = lax.optimization_barrier((values, beside))
    while len(values) > 1:
        values = [values[i] + values[i + 1] for i in range(0, len(values), 2)]
    return values[0]


def both_by_stages(parts, parents, blocks, blk, mp, prompt, merge):
    layers = blocks // 4
    place = (blk // 4).reshape(1)
    got = [partner(parts[k], "blk", blocks, k) for k in range(1, 4)]
    sent = prompt()
    partials = spread(sent)
    got, sent = lax.optimization_barrier((got, sent))
    parts = fold_part(parts[4], parts[0], got, place, layers)
    parts, parents = lax.optimization_barrier((parts, parents))
    more = [partner(parts[1 + k], "blk", blocks, 4 * k) for k in range(1, layers)]
    more, heads_out = lax.optimization_barrier((more, merge(partials, parents)))
    inner = parts[1] + sum(one.astype(jnp.float32) for one in more)
    own = (parts[0] + jax.nn.silu(inner)).astype(jnp.bfloat16)
    own, heads_out = lax.optimization_barrier((own, heads_out))
    chunks = [own] + [partner(own, "blk", blocks, 4 * k) for k in range(1, layers)]
    quad = stack_part(chunks, place)
    pieces = [quad] + [partner(quad, "blk", blocks, k) for k in range(1, 4)]
    pieces = pieces + [partner(piece, "mp", 2, 1) for piece in pieces]
    places = []
    for side in (mp, 1 - mp):
        for k in range(4):
            which = (blk & 3) ^ k
            places += [which >> 1, side * 2 + (which & 1)]
    return pieces, jnp.stack(places), spread(heads_out)


def spread(value):
    return lax.all_to_all(value, "blk", 0, 0, tiled=True)


def fresh_by_collectives(hidden, medusa_w, blocks, blk, mp):
    drafts, depth, units = medusa_w.shape
    rows = hidden.shape[0]
    own = drafts * rows // blocks
    hidden_cols = lax.dynamic_slice_in_dim(hidden, blk * depth, depth, 1)
    partial = jnp.einsum("rd,mdu->mru", hidden_cols, medusa_w, preferred_element_type=jnp.float32)
    partial = partial.reshape(blocks, own, units).astype(jnp.bfloat16)
    inner = lax.psum_scatter(partial, "blk", scatter_dimension=0).astype(jnp.float32)
    base = lax.dynamic_slice(hidden, ((blk * own) % rows, mp * units), (own, units))
    fresh = (base.astype(jnp.float32) + jax.nn.silu(inner)).astype(jnp.bfloat16)
    fresh = lax.all_gather(fresh, "blk", axis=0, tiled=True)
    return [lax.all_gather(fresh, "mp", axis=1, tiled=True)]


def per_device(
    hidden,
    medusa_w,
    embedding,
    cand_ids,
    tree_q,
    tree_key_value,
    prompt_key_value,
    block_group,
    block_len,
    block_empty,
    parents,
    out_weight,
    post_gain,
    resid,
):
    blocks, splits = lax.axis_size("blk"), lax.axis_size("mp")
    blk, mp = lax.axis_index("blk"), lax.axis_index("mp")
    drafts, depth, units = medusa_w.shape
    rows, model = hidden.shape
    lines = drafts * rows

    groups, tree_size, features = tree_q.shape
    width = features // blocks
    meta = jnp.concatenate([block_group, block_len, block_empty])

    def prompt():
        return prompt_part(tree_q, prompt_key_value, meta, width, blocks)

    def merge(partials, parents):
        numer, denom = tree_part(tree_q, tree_key_value, parents, blk * width, width)
        return merge_part(partials, numer, denom)

    if splits == 2 and blocks % 4 == 0 and units % 256 == 0 and drafts == 2:
        parts = draft_part(hidden, medusa_w, blk, mp)
        parts, meta = lax.optimization_barrier((parts, meta))
        pieces, places, heads_out = both_by_stages(
            parts, parents, blocks, blk, mp, prompt, merge
        )
    else:
        pieces = fresh_by_collectives(hidden, medusa_w, blocks, blk, mp)
        places = jnp.zeros((2,), jnp.int32)
        heads_out = spread(merge(spread(prompt()), parents))
    vocab = embedding.shape[0]
    picks = cand_ids.shape[2]
    ids = cand_ids.reshape(lines, picks) - (blk * splits + mp) * vocab
    ids = jnp.pad(ids, ((0, 0), (0, LANES - picks)), constant_values=-1)
    score = score_part(places, pieces, embedding, ids, picks)
    score = group_sum(score, "mp", splits, 1, splits)
    score, heads_out = lax.optimization_barrier((score, heads_out))
    attn = project_part(heads_out, out_weight)
    score = group_sum(score, "blk", blocks, 1, 4, attn)
    score = group_sum(score, "blk", blocks, 4, blocks // 4)
    draft_logprob = score[:picks] - jnp.log(score[picks : picks + 1])
    draft_logprob = draft_logprob.T.reshape(drafts, rows, picks)

    attn = group_sum(attn, "mp", splits, 1, splits)
    normed = attn * lax.rsqrt(jnp.mean(attn * attn, -1, keepdims=True) + 1e-06) * post_gain
    layer_out = (normed + resid.astype(jnp.float32)).astype(jnp.bfloat16)
    return (draft_logprob, layer_out)


def solution(mesh):
    placed = (
        P(),
        P(None, "blk", "mp"),
        P(("blk", "mp"), None),
        P(),
        P(None, None, "mp"),
        P(None, None, None, "mp"),
        P(None, "blk", None, "mp"),
        P("blk"),
        P("blk"),
        P("blk"),
        P(),
        P("mp", None),
        P(),
        P("blk", None),
    )
    return jax.shard_map(
        per_device, mesh=mesh, in_specs=placed, out_specs=(P(), P("blk", None)), check_vma=False
    )
```

```python
import functools

import jax
import jax.numpy as jnp
from jax import lax
from jax.experimental import pallas as pl
from jax.experimental.pallas import tpu as pltpu
from jax.sharding import PartitionSpec as P

HEAD_SIZE = 256
LANES = 128
MIB = 1 << 20
LOG2_E = 1.4426950408889634

EXTRA = 16
HIGH, LOW, GROUP = 0, 4, 8


def soft_weights(scores):
    return jnp.exp(50.0 * jnp.tanh(scores * (HEAD_SIZE**-0.5 / 50.0)))


def dot_t(left, right):
    return lax.dot_general(left, right, (((1,), (1,)), ((), ())), preferred_element_type=jnp.float32)


def in_hbm():
    return pl.BlockSpec(memory_space=pltpu.HBM)


def pin(value):
    return pltpu.with_memory_space_constraint(value, pltpu.HBM)


def in_vmem():
    return pl.BlockSpec(memory_space=pltpu.VMEM)


def in_smem():
    return pl.BlockSpec(memory_space=pltpu.SMEM)


def limit(mib):
    return pltpu.CompilerParams(vmem_limit_bytes=mib * MIB)


def prompt_kernel(meta, q_hbm, kv_hbm, out_ref, queries, held, sems):
    group, used, empty = meta[0], meta[1], meta[2]
    last = jnp.where(empty == 0, used, 0)
    kv_heads, slots = held.shape[1:3]
    tree_size, features = queries.shape
    repeats = features // HEAD_SIZE // kv_heads
    width = out_ref.shape[2]
    rows = tree_size * repeats
    ask = pltpu.make_async_copy(q_hbm.at[group], queries, sems.at[2 * kv_heads])
    ask.start()
    copies = [
        pltpu.make_async_copy(
            kv_hbm.at[s, 0, :, pl.ds(h * HEAD_SIZE, HEAD_SIZE)], held.at[s, h], sems.at[2 * h + s]
        )
        for h in range(kv_heads)
        for s in range(2)
    ]
    ahead = 4
    for copy in copies[:ahead]:
        copy.start()
    ask.wait()
    per_head = HEAD_SIZE // width
    row_id = lax.broadcasted_iota(jnp.int32, (tree_size, width), 0)
    lane_id = lax.broadcasted_iota(jnp.int32, (tree_size, width), 1)
    extra_id = lax.broadcasted_iota(jnp.int32, (EXTRA, width), 0)
    slot = lax.broadcasted_iota(jnp.int32, (rows, slots), 1)
    for h in range(kv_heads):
        asked = jnp.concatenate(
            [
                queries[:, (h * repeats + r) * HEAD_SIZE : (h * repeats + r + 1) * HEAD_SIZE]
                for r in range(repeats)
            ],
            axis=0,
        )
        copies[2 * h].wait()
        if 2 * h + ahead < len(copies):
            copies[2 * h + ahead].start()
        scores = dot_t(asked, held[0, h])
        weights = jnp.where(slot < last, soft_weights(scores), 0.0)
        denom = jnp.sum(weights, axis=1, keepdims=True)
        copies[2 * h + 1].wait()
        if 2 * h + 1 + ahead < len(copies):
            copies[2 * h + 1 + ahead].start()
        numer = jnp.dot(
            weights.astype(jnp.bfloat16), held[1, h], preferred_element_type=jnp.float32
        )
        for r in range(repeats):
            mine = jnp.broadcast_to(denom[r * tree_size : (r + 1) * tree_size], (tree_size, width))
            extra = jnp.where(extra_id == GROUP, group.astype(jnp.float32), 0.0)
            for c in range(-(-tree_size // width)):
                line = jnp.sum(
                    jnp.where(row_id == lane_id + c * width, mine, 0.0), axis=0, keepdims=True
                )
                high = line.astype(jnp.bfloat16).astype(jnp.float32)
                extra = jnp.where(extra_id == HIGH + c, high, extra)
                extra = jnp.where(extra_id == LOW + c, line - high, extra)
            for part in range(per_head):
                d = (h * repeats + r) * per_head + part
                out_ref[d, :tree_size, :] = numer[
                    r * tree_size : (r + 1) * tree_size, part * width : (part + 1) * width
                ].astype(jnp.bfloat16)
                out_ref[d, tree_size:, :] = extra.astype(jnp.bfloat16)


def prompt_part(tree_q, prompt_key_value, meta, width, blocks):
    groups, tree_size, features = tree_q.shape
    slots, key_features = prompt_key_value.shape[2:]
    kv_heads = key_features // HEAD_SIZE
    return pl.pallas_call(
        prompt_kernel,
        out_shape=jax.ShapeDtypeStruct((blocks, tree_size + EXTRA, width), jnp.bfloat16),
        in_specs=[in_smem(), in_hbm(), in_hbm()],
        out_specs=in_vmem(),
        scratch_shapes=[
            pltpu.VMEM((tree_size, features), jnp.bfloat16),
            pltpu.VMEM((2, kv_heads, slots, HEAD_SIZE), jnp.bfloat16),
            pltpu.SemaphoreType.DMA((2 * kv_heads + 1,)),
        ],
        compiler_params=limit(24),
        cost_estimate=pl.CostEstimate(
            flops=4 * tree_size * features * slots,
            bytes_accessed=4 * slots * key_features,
            transcendentals=2 * tree_size * slots * features // HEAD_SIZE,
        ),
        name="prompt_part",
    )(meta, pin(tree_q), pin(prompt_key_value))


def tree_kernel(meta, q_hbm, kv_hbm, reach_ref, numer_ref, denom_ref, held, sems):
    width = numer_ref.shape[2]
    query_columns = pl.ds(pl.multiple_of(meta[0] * HEAD_SIZE, HEAD_SIZE), HEAD_SIZE)
    key_columns = pl.ds(pl.multiple_of(meta[1] * HEAD_SIZE, HEAD_SIZE), HEAD_SIZE)
    copies = [
        pltpu.make_async_copy(q_hbm.at[:, :, query_columns], held.at[0], sems.at[0]),
        pltpu.make_async_copy(kv_hbm.at[0, :, :, key_columns], held.at[1], sems.at[1]),
        pltpu.make_async_copy(kv_hbm.at[1, :, :, key_columns], held.at[2], sems.at[2]),
    ]
    for copy in copies:
        copy.start()
    for copy in copies:
        copy.wait()
    for g in range(held.shape[1]):
        weights = soft_weights(dot_t(held[0, g], held[1, g])) * reach_ref[g]
        denom_ref[g] = jnp.broadcast_to(
            jnp.sum(weights, axis=1, keepdims=True), denom_ref.shape[1:]
        )
        numer = jnp.dot(
            weights.astype(jnp.bfloat16), held[2, g], preferred_element_type=jnp.float32
        )
        mine = numer[:, :width]
        for j in range(1, HEAD_SIZE // width):
            mine = jnp.where(meta[2] == j, numer[:, j * width : (j + 1) * width], mine)
        numer_ref[g] = mine


def tree_part(tree_q, tree_key_value, reach, column, width):
    groups, tree_size, features = tree_q.shape
    repeats = features // tree_key_value.shape[3]
    head = column // HEAD_SIZE
    meta = jnp.stack([head, head // repeats, column % HEAD_SIZE // width])
    return pl.pallas_call(
        tree_kernel,
        out_shape=[jax.ShapeDtypeStruct((groups, tree_size, width), jnp.float32)] * 2,
        in_specs=[in_smem(), in_hbm(), in_hbm(), in_vmem()],
        out_specs=[in_vmem()] * 2,
        scratch_shapes=[
            pltpu.VMEM((3, groups, tree_size, HEAD_SIZE), jnp.bfloat16),
            pltpu.SemaphoreType.DMA((3,)),
        ],
        compiler_params=limit(16),
        name="tree_part",
    )(meta, pin(tree_q), pin(tree_key_value), reach)


def merge_kernel(got_ref, numer_ref, denom_ref, out_ref, hold, sums, lines):
    blocks = got_ref.shape[0]
    groups, tree_size, width = numer_ref.shape
    row_id = lax.broadcasted_iota(jnp.int32, (tree_size, width), 0)
    lane_id = lax.broadcasted_iota(jnp.int32, (tree_size, width), 1)
    sums[...] = numer_ref[...]
    lines[...] = jnp.zeros_like(lines)
    owners = []
    for b in range(blocks):
        extra = got_ref[b, tree_size:, :].astype(jnp.float32)
        owners.append(jnp.max(extra[GROUP : GROUP + 1, :]).astype(jnp.int32))
    for b in range(blocks):
        sums[owners[b]] += got_ref[b, :tree_size, :].astype(jnp.float32)
        lines[owners[b]] += got_ref[b, tree_size:, :].astype(jnp.float32)
    for g in range(groups):
        denom = denom_ref[g]
        for c in range(-(-tree_size // width)):
            line = lines[g, HIGH + c : HIGH + c + 1, :] + lines[g, LOW + c : LOW + c + 1, :]
            spread = jnp.where(row_id == lane_id + c * width, line, 0.0)
            denom = denom + jnp.sum(spread, axis=1, keepdims=True)
        hold[g * tree_size : (g + 1) * tree_size, :] = sums[g] / denom

    count = out_ref.shape[1]
    for d in range(out_ref.shape[0]):
        out_ref[d] = hold[d * count : (d + 1) * count, :].astype(jnp.bfloat16)


def merge_part(got, numer, denom):
    blocks, _, width = got.shape
    groups, tree_size, _ = numer.shape
    tokens = groups * tree_size
    return pl.pallas_call(
        merge_kernel,
        out_shape=jax.ShapeDtypeStruct((blocks, tokens // blocks, width), jnp.bfloat16),
        scratch_shapes=[
            pltpu.VMEM((tokens, width), jnp.float32),
            pltpu.VMEM((groups, tree_size, width), jnp.float32),
            pltpu.VMEM((groups, EXTRA, width), jnp.float32),
        ],
        compiler_params=limit(16),
        name="merge_part",
    )(got, numer, denom)


def project_kernel(heads_ref, weight_hbm, out_ref, ring, sems):
    slots, span = ring.shape[:2]
    steps = weight_hbm.shape[0] // span
    per_step = span // heads_ref.shape[2]

    def copy(i):
        return pltpu.make_async_copy(
            weight_hbm.at[i * span : (i + 1) * span], ring.at[i % slots], sems.at[i % slots]
        )

    for i in range(min(slots, steps)):
        copy(i).start()
    for i in range(steps):
        left = jnp.concatenate([heads_ref[i * per_step + j] for j in range(per_step)], axis=1)
        copy(i).wait()
        more = jnp.dot(left, ring[i % slots], preferred_element_type=jnp.float32)
        out_ref[...] = more if i == 0 else out_ref[...] + more
        if i + slots < steps:
            copy(i + slots).start()


def project_part(heads_out, out_weight):
    blocks, tokens, width = heads_out.shape
    features, model = out_weight.shape
    if width % LANES or features % HEAD_SIZE:
        flat = heads_out.transpose(1, 0, 2).reshape(tokens, features)
        return jnp.dot(flat, out_weight, preferred_element_type=jnp.float32)
    slots = 4
    return pl.pallas_call(
        project_kernel,
        out_shape=jax.ShapeDtypeStruct((tokens, model), jnp.float32),
        in_specs=[in_vmem(), in_hbm()],
        out_specs=in_vmem(),
        scratch_shapes=[
            pltpu.VMEM((slots, HEAD_SIZE, model), jnp.bfloat16),
            pltpu.SemaphoreType.DMA((slots,)),
        ],
        compiler_params=limit(20),
        cost_estimate=pl.CostEstimate(
            flops=2 * tokens * features * model,
            bytes_accessed=2 * features * model,
            transcendentals=0,
        ),
        name="project_part",
    )(heads_out, pin(out_weight))


def score_kernel(picks, streams, places, ids_ref, *refs):
    pieces, embeds, out_ref = refs[: -5 - 2 * streams], refs[-5 - 2 * streams : -5], refs[-5]
    fresh, total, picked, before = refs[-4:]
    step = pl.program_id(0)
    span = embeds[0].shape[0]
    rows = fresh.shape[0]
    band = 32 if rows % 32 == 0 else rows

    @pl.when(step == 0)
    def _():
        before[...] = jnp.zeros_like(before)
        for n, piece in enumerate(pieces):
            height, wide = piece.shape
            row = pl.multiple_of(places[2 * n] * height, 16)
            col = pl.multiple_of(places[2 * n + 1] * wide, LANES)
            fresh[pl.ds(row, height), pl.ds(col, wide)] = piece[...]

    def product(n):
        half = fresh.shape[1] // 2
        low, high = embeds[2 * n], embeds[2 * n + 1]
        return dot_t(fresh[:, :half], low[...]) + dot_t(fresh[:, half:], high[...])

    def absorb(raw, start, keep=None):
        for r in range(0, rows, band):
            ids = ids_ref[r : r + band] - start
            lane = ids & (LANES - 1)
            chunk = ids >> 7
            sums, found = total[r : r + band], picked[r : r + band]
            for c in range(span // LANES):
                part = jnp.tanh(raw[r : r + band, c * LANES : (c + 1) * LANES] * (1.0 / 30.0))
                sums = sums + jnp.exp2(part * (30.0 * LOG2_E))
                there = jnp.take_along_axis(part, lane, axis=1, mode="promise_in_bounds")
                found = found + jnp.where(chunk == c, there, 0.0)
            if keep is not None:
                sums, found = jnp.where(keep, sums, 0.0), jnp.where(keep, found, 0.0)
            total[r : r + band] = sums
            picked[r : r + band] = found

    base = step * streams * span
    raw = product(0)
    absorb(before[...], base - span, step > 0)
    for n in range(1, streams):
        more = product(n)
        absorb(raw, base + (n - 1) * span)
        raw = more
    before[...] = raw

    @pl.when(step == pl.num_programs(0) - 1)
    def _():
        absorb(before[...], base + (streams - 1) * span)
        sums, found = total[...], picked[...]
        place = lax.broadcasted_iota(jnp.int32, sums.shape, 1)
        whole = jnp.sum(sums, axis=1, keepdims=True)
        both = jnp.where(place < picks, 30.0 * found, jnp.where(place == picks, whole, 0.0))
        out_ref[...] = both.T[: out_ref.shape[0]]


def score_part(places, pieces, embedding, ids, picks):
    rows = ids.shape[0]
    vocab, depth = embedding.shape
    span, streams = min(512, vocab), 1
    lines = -(-(picks + 1) // 8) * 8
    fixed = lambda i, places: (0, 0)
    return pl.pallas_call(
        functools.partial(score_kernel, picks, streams),
        out_shape=jax.ShapeDtypeStruct((lines, rows), jnp.float32),
        grid_spec=pltpu.PrefetchScalarGridSpec(
            num_scalar_prefetch=1,
            grid=(vocab // (span * streams),),
            in_specs=[pl.BlockSpec((rows, LANES), fixed)]
            + [pl.BlockSpec(piece.shape, fixed) for piece in pieces]
            + [
                pl.BlockSpec(
                    (span, depth // 2), lambda i, places, n=n, k=k: (i * streams + n, k)
                )
                for n in range(streams)
                for k in range(2)
            ],
            out_specs=pl.BlockSpec((lines, rows), fixed),
            scratch_shapes=[pltpu.VMEM((rows, depth), jnp.bfloat16)]
            + [pltpu.VMEM((rows, LANES), jnp.float32)] * 2
            + [pltpu.VMEM((rows, span), jnp.float32)],
        ),
        compiler_params=limit(32),
        cost_estimate=pl.CostEstimate(
            flops=2 * rows * depth * vocab,
            bytes_accessed=2 * vocab * depth,
            transcendentals=2 * rows * vocab,
        ),
        name="score_part",
    )(places, ids, *pieces, *[pin(embedding)] * (2 * streams))


def draft_kernel(meta, hidden_hbm, weight_hbm, *refs):
    outs, columns, padded, sems = refs[:4], *refs[4:]
    depth = weight_hbm.shape[1]
    half = padded.shape[2]
    window = padded.shape[1]
    first = pl.multiple_of(meta[0], LANES)
    ask = pltpu.make_async_copy(hidden_hbm.at[:, pl.ds(first, window)], columns, sems.at[4])
    ask.start()
    padded[...] = jnp.zeros_like(padded)
    copies = []
    for k in (1, 2, 3, 0):
        quad = meta[2 + k]
        col = pl.multiple_of((quad & 1) * half, LANES)
        copies.append(
            pltpu.make_async_copy(
                weight_hbm.at[quad >> 1, :, pl.ds(col, half)],
                padded.at[k, pl.ds(pl.multiple_of(meta[1], 16), depth)],
                sems.at[k],
            )
        )
        copies[-1].start()
    ask.wait()
    for n, k in enumerate((1, 2, 3, 0)):
        copies[n].wait()
        partial = jnp.dot(columns[...], padded[k], preferred_element_type=jnp.float32)
        outs[k][...] = partial.astype(outs[k].dtype)


def draft_part(hidden, medusa_w, blk):
    rows, model = hidden.shape
    depth, units = medusa_w.shape[1:]
    half = units // 2
    window = -(-depth // LANES) * LANES + LANES
    start = blk * depth
    first = jnp.minimum(start // LANES * LANES, model - window)
    meta = jnp.stack([first, start - first] + [(blk & 3) ^ k for k in range(4)])
    return pl.pallas_call(
        draft_kernel,
        out_shape=[
            jax.ShapeDtypeStruct((rows, half), jnp.bfloat16 if k else jnp.float32)
            for k in range(4)
        ],
        in_specs=[in_smem(), in_hbm(), in_hbm()],
        out_specs=[in_vmem()] * 4,
        scratch_shapes=[
            pltpu.VMEM((rows, window), jnp.bfloat16),
            pltpu.VMEM((4, window, half), jnp.bfloat16),
            pltpu.SemaphoreType.DMA((5,)),
        ],
        compiler_params=limit(16),
        name="draft_part",
    )(meta, pin(hidden), pin(medusa_w))


def fold_kernel(place, own_ref, *refs):
    got, outs, hold = refs[:3], refs[3:-1], refs[-1]
    total = own_ref[...]
    for one in got:
        total = total + one[...].astype(jnp.float32)
    height = hold.shape[1]
    for j in range(len(outs)):
        hold[j] = total[j * height : (j + 1) * height]
    for k, out in enumerate(outs):
        out[...] = hold[place[0] ^ k].astype(out.dtype)


def fold_part(own, got, place, layers):
    rows, half = own.shape
    height = rows // layers
    return pl.pallas_call(
        fold_kernel,
        out_shape=[
            jax.ShapeDtypeStruct((height, half), jnp.bfloat16 if k else jnp.float32)
            for k in range(layers)
        ],
        in_specs=[in_smem()] + [in_vmem()] * 4,
        out_specs=[in_vmem()] * layers,
        scratch_shapes=[pltpu.VMEM((layers, height, half), jnp.float32)],
        compiler_params=limit(16),
        name="fold_part",
    )(place, own, *got)


def stack_kernel(place, *refs):
    parts, out_ref, hold, flat = refs[:-3], refs[-3], refs[-2], refs[-1]
    height = hold.shape[1]
    for k, part in enumerate(parts):
        hold[place[0] ^ k] = part[...].astype(jnp.float32)
    for j in range(len(parts)):
        flat[j * height : (j + 1) * height, :] = hold[j]
    out_ref[...] = flat[...].astype(jnp.bfloat16)


def stack_part(parts, place):
    layers = len(parts)
    height, half = parts[0].shape
    return pl.pallas_call(
        stack_kernel,
        out_shape=jax.ShapeDtypeStruct((layers * height, half), jnp.bfloat16),
        in_specs=[in_smem()] + [in_vmem()] * layers,
        out_specs=in_vmem(),
        scratch_shapes=[
            pltpu.VMEM((layers, height, half), jnp.float32),
            pltpu.VMEM((layers * height, half), jnp.float32),
        ],
        compiler_params=limit(16),
        name="stack_part",
    )(place, *parts)


def partner(value, axis, size, bits):
    return lax.ppermute(value, axis, [(i, i ^ bits) for i in range(size)])


def group_sum(value, axis, size, stride, count, beside=None):
    values = [value] + [partner(value, axis, size, k * stride) for k in range(1, count)]
    if beside is not None:
        values, _ = lax.optimization_barrier((values, beside))
    while len(values) > 1:
        values = [values[i] + values[i + 1] for i in range(0, len(values), 2)]
    return values[0]


def both_by_stages(hidden, parts, parents, units, blocks, blk, mp, prompt, merge, project):
    rows, model = hidden.shape
    half = units // 2
    layers = blocks // 4
    height = rows // layers
    layer = blk // 4
    place = layer.reshape(1)
    got = [partner(parts[k], "blk", blocks, k) for k in range(1, 4)]
    sent = prompt()
    partials = spread(sent)
    got, sent = lax.optimization_barrier((got, sent))
    parts = fold_part(parts[0], got, place, layers)
    parts, parents = lax.optimization_barrier((parts, parents))
    more = [partner(parts[k], "blk", blocks, 4 * k) for k in range(1, layers)]
    more, heads_out = lax.optimization_barrier((more, merge(partials, parents)))
    inner = parts[0] + sum(one.astype(jnp.float32) for one in more)
    base = lax.dynamic_slice(
        hidden, (layer * height, mp * units + (blk & 1) * half), (height, half)
    )
    own = (base.astype(jnp.float32) + jax.nn.silu(inner)).astype(jnp.bfloat16)
    own, heads_out = lax.optimization_barrier((own, heads_out))
    chunks = [own] + [partner(own, "blk", blocks, 4 * k) for k in range(1, layers)]
    chunks, heads_out = lax.optimization_barrier((chunks, spread(heads_out)))
    quad = stack_part(chunks, place)
    pieces = [partner(quad, "blk", blocks, k) for k in range(1, 4)]
    pieces, attn = lax.optimization_barrier((pieces, project(heads_out)))
    pieces = [quad] + pieces
    pieces = pieces + [partner(piece, "mp", 2, 1) for piece in pieces]
    places = []
    for side in (mp, 1 - mp):
        for k in range(4):
            which = (blk & 3) ^ k
            places += [which >> 1, side * 2 + (which & 1)]
    return pieces, jnp.stack(places), attn


def spread(value):
    return lax.all_to_all(value, "blk", 0, 0, tiled=True)


def fresh_by_collectives(hidden, medusa_w, blocks, blk, mp):
    drafts, depth, units = medusa_w.shape
    rows = hidden.shape[0]
    own = drafts * rows // blocks
    hidden_cols = lax.dynamic_slice_in_dim(hidden, blk * depth, depth, 1)
    partial = jnp.einsum("rd,mdu->mru", hidden_cols, medusa_w, preferred_element_type=jnp.float32)
    partial = partial.reshape(blocks, own, units).astype(jnp.bfloat16)
    inner = lax.psum_scatter(partial, "blk", scatter_dimension=0).astype(jnp.float32)
    base = lax.dynamic_slice(hidden, ((blk * own) % rows, mp * units), (own, units))
    fresh = (base.astype(jnp.float32) + jax.nn.silu(inner)).astype(jnp.bfloat16)
    fresh = lax.all_gather(fresh, "blk", axis=0, tiled=True)
    return [lax.all_gather(fresh, "mp", axis=1, tiled=True)]


def ancestry(parents):
    count = parents.shape[1]
    column = jnp.arange(count, dtype=jnp.int32)
    linked = (parents[:, :, None] == column[None, None, :]) & (column[None, :, None] > 0)
    reach = jnp.eye(count, dtype=jnp.bfloat16)[None] + linked.astype(jnp.bfloat16)
    for sweep in range(count.bit_length()):
        met = jnp.einsum("gij,gjk->gik", reach, reach, preferred_element_type=jnp.float32)
        reach = jnp.minimum(met, 1.0).astype(jnp.bfloat16)
    return reach.astype(jnp.float32)


def per_device(
    hidden,
    medusa_w,
    embedding,
    cand_ids,
    tree_q,
    tree_key_value,
    prompt_key_value,
    block_group,
    block_len,
    block_empty,
    parents,
    out_weight,
    post_gain,
    resid,
):
    blocks, splits = lax.axis_size("blk"), lax.axis_size("mp")
    blk, mp = lax.axis_index("blk"), lax.axis_index("mp")
    drafts, depth, units = medusa_w.shape
    rows, model = hidden.shape
    lines = drafts * rows

    groups, tree_size, features = tree_q.shape
    width = features // blocks
    meta = jnp.concatenate([block_group, block_len, block_empty])

    def prompt():
        return prompt_part(tree_q, prompt_key_value, meta, width, blocks)

    def merge(partials, parents):
        reach = ancestry(parents)
        numer, denom = tree_part(tree_q, tree_key_value, reach, blk * width, width)
        return merge_part(partials, numer, denom)

    def project(heads_out):
        return project_part(heads_out, out_weight)

    if splits == 2 and blocks % 4 == 0 and units % 256 == 0 and drafts == 2:
        parts = draft_part(hidden, medusa_w, blk)
        parts, meta = lax.optimization_barrier((parts, meta))
        pieces, places, attn = both_by_stages(
            hidden, parts, parents, units, blocks, blk, mp, prompt, merge, project
        )
    else:
        pieces = fresh_by_collectives(hidden, medusa_w, blocks, blk, mp)
        places = jnp.zeros((2,), jnp.int32)
        attn = project(spread(merge(spread(prompt()), parents)))
    attn, pieces = lax.optimization_barrier((attn, pieces))
    attn = group_sum(attn, "mp", splits, 1, splits)
    normed = attn * lax.rsqrt(jnp.mean(attn * attn, -1, keepdims=True) + 1e-06) * post_gain
    layer_out = (normed + resid.astype(jnp.float32)).astype(jnp.bfloat16)

    vocab = embedding.shape[0]
    picks = cand_ids.shape[2]
    ids = cand_ids.reshape(lines, picks) - (blk * splits + mp) * vocab
    ids = jnp.pad(ids, ((0, 0), (0, LANES - picks)), constant_values=-1)
    score = score_part(places, pieces, embedding, ids, picks)
    score = group_sum(score, "mp", splits, 1, splits)
    score = group_sum(score, "blk", blocks, 1, 4, layer_out)
    score = group_sum(score, "blk", blocks, 4, blocks // 4)
    draft_logprob = score[:picks] - jnp.log(score[picks : picks + 1])
    draft_logprob = draft_logprob.T.reshape(drafts, rows, picks)
    return (draft_logprob, layer_out)


def solution(mesh):
    placed = (
        P(),
        P(None, "blk", "mp"),
        P(("blk", "mp"), None),
        P(),
        P(None, None, "mp"),
        P(None, None, None, "mp"),
        P(None, "blk", None, "mp"),
        P("blk"),
        P("blk"),
        P("blk"),
        P(),
        P("mp", None),
        P(),
        P("blk", None),
    )
    return jax.shard_map(
        per_device, mesh=mesh, in_specs=placed, out_specs=(P(), P("blk", None)), check_vma=False
    )
```

```python
import functools

import jax
import jax.numpy as jnp
from jax import lax
from jax.experimental import pallas as pl
from jax.experimental.pallas import tpu as pltpu
from jax.sharding import PartitionSpec as P

HEAD_SIZE = 256
LANES = 128
MIB = 1 << 20
LOG2_E = 1.4426950408889634

EXTRA = 16
HIGH, LOW, GROUP = 0, 4, 8


def soft_weights(scores):
    return jnp.exp(50.0 * jnp.tanh(scores * (HEAD_SIZE**-0.5 / 50.0)))


def dot_t(left, right):
    return lax.dot_general(left, right, (((1,), (1,)), ((), ())), preferred_element_type=jnp.float32)


def in_hbm():
    return pl.BlockSpec(memory_space=pltpu.HBM)


def pin(value):
    return pltpu.with_memory_space_constraint(value, pltpu.HBM)


def in_vmem():
    return pl.BlockSpec(memory_space=pltpu.VMEM)


def in_smem():
    return pl.BlockSpec(memory_space=pltpu.SMEM)


def limit(mib):
    return pltpu.CompilerParams(vmem_limit_bytes=mib * MIB)


def prompt_kernel(meta, q_hbm, kv_hbm, out_ref, queries, held, sems):
    group, used, empty = meta[0], meta[1], meta[2]
    last = jnp.where(empty == 0, used, 0)
    kv_heads, slots = held.shape[1:3]
    tree_size, features = queries.shape
    repeats = features // HEAD_SIZE // kv_heads
    width = out_ref.shape[2]
    rows = tree_size * repeats
    ask = pltpu.make_async_copy(q_hbm.at[group], queries, sems.at[2 * kv_heads])
    ask.start()
    copies = [
        pltpu.make_async_copy(
            kv_hbm.at[s, 0, :, pl.ds(h * HEAD_SIZE, HEAD_SIZE)], held.at[s, h], sems.at[2 * h + s]
        )
        for h in range(kv_heads)
        for s in range(2)
    ]
    ahead = 4
    for copy in copies[:ahead]:
        copy.start()
    ask.wait()
    per_head = HEAD_SIZE // width
    row_id = lax.broadcasted_iota(jnp.int32, (tree_size, width), 0)
    lane_id = lax.broadcasted_iota(jnp.int32, (tree_size, width), 1)
    extra_id = lax.broadcasted_iota(jnp.int32, (EXTRA, width), 0)
    span = min(512, slots)
    slot = lax.broadcasted_iota(jnp.int32, (rows, span), 1)
    for h in range(kv_heads):
        asked = jnp.concatenate(
            [
                queries[:, (h * repeats + r) * HEAD_SIZE : (h * repeats + r + 1) * HEAD_SIZE]
                for r in range(repeats)
            ],
            axis=0,
        )
        copies[2 * h].wait()
        if 2 * h + ahead < len(copies):
            copies[2 * h + ahead].start()
        numer = jnp.zeros((rows, HEAD_SIZE), jnp.float32)
        sums = jnp.zeros((rows, LANES), jnp.float32)
        for start in range(0, slots, span):
            scores = dot_t(asked, held[0, h, start : start + span])
            weights = jnp.where(slot < last - start, soft_weights(scores), 0.0)
            for c in range(0, span, LANES):
                sums = sums + weights[:, c : c + LANES]
            if start == 0:
                copies[2 * h + 1].wait()
                if 2 * h + 1 + ahead < len(copies):
                    copies[2 * h + 1 + ahead].start()
            numer = numer + jnp.dot(
                weights.astype(jnp.bfloat16),
                held[1, h, start : start + span],
                preferred_element_type=jnp.float32,
            )
        denom = jnp.sum(sums, axis=1, keepdims=True)
        for r in range(repeats):
            mine = jnp.broadcast_to(denom[r * tree_size : (r + 1) * tree_size], (tree_size, width))
            extra = jnp.where(extra_id == GROUP, group.astype(jnp.float32), 0.0)
            for c in range(-(-tree_size // width)):
                line = jnp.sum(
                    jnp.where(row_id == lane_id + c * width, mine, 0.0), axis=0, keepdims=True
                )
                high = line.astype(jnp.bfloat16).astype(jnp.float32)
                extra = jnp.where(extra_id == HIGH + c, high, extra)
                extra = jnp.where(extra_id == LOW + c, line - high, extra)
            for part in range(per_head):
                d = (h * repeats + r) * per_head + part
                out_ref[d, :tree_size, :] = numer[
                    r * tree_size : (r + 1) * tree_size, part * width : (part + 1) * width
                ].astype(jnp.bfloat16)
                out_ref[d, tree_size:, :] = extra.astype(jnp.bfloat16)


def prompt_part(tree_q, prompt_key_value, meta, width, blocks):
    groups, tree_size, features = tree_q.shape
    slots, key_features = prompt_key_value.shape[2:]
    kv_heads = key_features // HEAD_SIZE
    return pl.pallas_call(
        prompt_kernel,
        out_shape=jax.ShapeDtypeStruct((blocks, tree_size + EXTRA, width), jnp.bfloat16),
        in_specs=[in_smem(), in_hbm(), in_hbm()],
        out_specs=in_vmem(),
        scratch_shapes=[
            pltpu.VMEM((tree_size, features), jnp.bfloat16),
            pltpu.VMEM((2, kv_heads, slots, HEAD_SIZE), jnp.bfloat16),
            pltpu.SemaphoreType.DMA((2 * kv_heads + 1,)),
        ],
        compiler_params=limit(24),
        cost_estimate=pl.CostEstimate(
            flops=4 * tree_size * features * slots,
            bytes_accessed=4 * slots * key_features,
            transcendentals=2 * tree_size * slots * features // HEAD_SIZE,
        ),
        name="prompt_part",
    )(meta, pin(tree_q), pin(prompt_key_value))


def tree_kernel(meta, q_hbm, kv_hbm, parents_ref, numer_ref, denom_ref, held, sems):
    width = numer_ref.shape[2]
    query_columns = pl.ds(pl.multiple_of(meta[0] * HEAD_SIZE, HEAD_SIZE), HEAD_SIZE)
    key_columns = pl.ds(pl.multiple_of(meta[1] * HEAD_SIZE, HEAD_SIZE), HEAD_SIZE)
    copies = [
        pltpu.make_async_copy(q_hbm.at[:, :, query_columns], held.at[0], sems.at[0]),
        pltpu.make_async_copy(kv_hbm.at[0, :, :, key_columns], held.at[1], sems.at[1]),
        pltpu.make_async_copy(kv_hbm.at[1, :, :, key_columns], held.at[2], sems.at[2]),
    ]
    for copy in copies:
        copy.start()
    groups, count = parents_ref.shape
    above = lax.broadcasted_iota(jnp.int32, (count, count), 0)
    token = lax.broadcasted_iota(jnp.int32, (count, count), 1)
    met = [
        jnp.where(
            (above == token) | ((parents_ref[g : g + 1, :] == above) & (token > 0)), 1.0, 0.0
        )
        for g in range(groups)
    ]
    for sweep in range(count.bit_length()):
        small = [one.astype(jnp.bfloat16) for one in met]
        met = [
            jnp.minimum(jnp.dot(one, one, preferred_element_type=jnp.float32), 1.0)
            for one in small
        ]
    for copy in copies:
        copy.wait()
    for g in range(groups):
        weights = soft_weights(dot_t(held[0, g], held[1, g])) * met[g].T
        denom_ref[g] = jnp.broadcast_to(
            jnp.sum(weights, axis=1, keepdims=True), denom_ref.shape[1:]
        )
        numer = jnp.dot(
            weights.astype(jnp.bfloat16), held[2, g], preferred_element_type=jnp.float32
        )
        mine = numer[:, :width]
        for j in range(1, HEAD_SIZE // width):
            mine = jnp.where(meta[2] == j, numer[:, j * width : (j + 1) * width], mine)
        numer_ref[g] = mine


def tree_part(tree_q, tree_key_value, parents, column, width):
    groups, tree_size, features = tree_q.shape
    repeats = features // tree_key_value.shape[3]
    head = column // HEAD_SIZE
    meta = jnp.stack([head, head // repeats, column % HEAD_SIZE // width])
    return pl.pallas_call(
        tree_kernel,
        out_shape=[jax.ShapeDtypeStruct((groups, tree_size, width), jnp.float32)] * 2,
        in_specs=[in_smem(), in_hbm(), in_hbm(), in_vmem()],
        out_specs=[in_vmem()] * 2,
        scratch_shapes=[
            pltpu.VMEM((3, groups, tree_size, HEAD_SIZE), jnp.bfloat16),
            pltpu.SemaphoreType.DMA((3,)),
        ],
        compiler_params=limit(16),
        cost_estimate=pl.CostEstimate(flops=0, bytes_accessed=64 * MIB, transcendentals=0),
        name="tree_part",
    )(meta, pin(tree_q), pin(tree_key_value), parents)


def merge_kernel(got_ref, numer_ref, denom_ref, out_ref, hold, sums, lines):
    blocks = got_ref.shape[0]
    groups, tree_size, width = numer_ref.shape
    row_id = lax.broadcasted_iota(jnp.int32, (tree_size, width), 0)
    lane_id = lax.broadcasted_iota(jnp.int32, (tree_size, width), 1)
    sums[...] = numer_ref[...]
    lines[...] = jnp.zeros_like(lines)
    owners = []
    for b in range(blocks):
        extra = got_ref[b, tree_size:, :].astype(jnp.float32)
        owners.append(jnp.max(extra[GROUP : GROUP + 1, :]).astype(jnp.int32))
    for b in range(blocks):
        sums[owners[b]] += got_ref[b, :tree_size, :].astype(jnp.float32)
        lines[owners[b]] += got_ref[b, tree_size:, :].astype(jnp.float32)
    for g in range(groups):
        denom = denom_ref[g]
        for c in range(-(-tree_size // width)):
            line = lines[g, HIGH + c : HIGH + c + 1, :] + lines[g, LOW + c : LOW + c + 1, :]
            spread = jnp.where(row_id == lane_id + c * width, line, 0.0)
            denom = denom + jnp.sum(spread, axis=1, keepdims=True)
        hold[g * tree_size : (g + 1) * tree_size, :] = sums[g] / denom

    count = out_ref.shape[1]
    for d in range(out_ref.shape[0]):
        out_ref[d] = hold[d * count : (d + 1) * count, :].astype(jnp.bfloat16)


def merge_part(got, numer, denom):
    blocks, _, width = got.shape
    groups, tree_size, _ = numer.shape
    tokens = groups * tree_size
    return pl.pallas_call(
        merge_kernel,
        out_shape=jax.ShapeDtypeStruct((blocks, tokens // blocks, width), jnp.bfloat16),
        scratch_shapes=[
            pltpu.VMEM((tokens, width), jnp.float32),
            pltpu.VMEM((groups, tree_size, width), jnp.float32),
            pltpu.VMEM((groups, EXTRA, width), jnp.float32),
        ],
        compiler_params=limit(16),
        name="merge_part",
    )(got, numer, denom)


def project_kernel(heads_ref, weight_hbm, out_ref, ring, sems):
    slots, span = ring.shape[:2]
    steps = weight_hbm.shape[0] // span
    per_step = span // heads_ref.shape[2]

    def copy(i):
        return pltpu.make_async_copy(
            weight_hbm.at[i * span : (i + 1) * span], ring.at[i % slots], sems.at[i % slots]
        )

    for i in range(min(slots, steps)):
        copy(i).start()
    for i in range(steps):
        left = jnp.concatenate([heads_ref[i * per_step + j] for j in range(per_step)], axis=1)
        copy(i).wait()
        more = jnp.dot(left, ring[i % slots], preferred_element_type=jnp.float32)
        out_ref[...] = more if i == 0 else out_ref[...] + more
        if i + slots < steps:
            copy(i + slots).start()


def project_part(heads_out, out_weight):
    blocks, tokens, width = heads_out.shape
    features, model = out_weight.shape
    if width % LANES or features % HEAD_SIZE:
        flat = heads_out.transpose(1, 0, 2).reshape(tokens, features)
        return jnp.dot(flat, out_weight, preferred_element_type=jnp.float32)
    slots = 4
    return pl.pallas_call(
        project_kernel,
        out_shape=jax.ShapeDtypeStruct((tokens, model), jnp.float32),
        in_specs=[in_vmem(), in_hbm()],
        out_specs=in_vmem(),
        scratch_shapes=[
            pltpu.VMEM((slots, HEAD_SIZE, model), jnp.bfloat16),
            pltpu.SemaphoreType.DMA((slots,)),
        ],
        compiler_params=limit(20),
        cost_estimate=pl.CostEstimate(
            flops=2 * tokens * features * model,
            bytes_accessed=2 * features * model,
            transcendentals=0,
        ),
        name="project_part",
    )(heads_out, pin(out_weight))


def score_kernel(picks, streams, places, ids_ref, *refs):
    pieces, embeds, out_ref = refs[: -5 - 2 * streams], refs[-5 - 2 * streams : -5], refs[-5]
    fresh, total, picked, before = refs[-4:]
    step = pl.program_id(0)
    span = embeds[0].shape[0]
    rows = fresh.shape[0]
    band = 32 if rows % 32 == 0 else rows

    @pl.when(step == 0)
    def _():
        before[...] = jnp.zeros_like(before)
        for n, piece in enumerate(pieces):
            height, wide = piece.shape
            row = pl.multiple_of(places[2 * n] * height, 16)
            col = pl.multiple_of(places[2 * n + 1] * wide, LANES)
            fresh[pl.ds(row, height), pl.ds(col, wide)] = piece[...]

    def product(n):
        half = fresh.shape[1] // 2
        low, high = embeds[2 * n], embeds[2 * n + 1]
        return dot_t(fresh[:, :half], low[...]) + dot_t(fresh[:, half:], high[...])

    def absorb(raw, start, keep=None):
        for r in range(0, rows, band):
            ids = ids_ref[r : r + band] - start
            lane = ids & (LANES - 1)
            chunk = ids >> 7
            sums, found = total[r : r + band], picked[r : r + band]
            for c in range(span // LANES):
                part = jnp.tanh(raw[r : r + band, c * LANES : (c + 1) * LANES] * (1.0 / 30.0))
                sums = sums + jnp.exp2(part * (30.0 * LOG2_E))
                there = jnp.take_along_axis(part, lane, axis=1, mode="promise_in_bounds")
                found = found + jnp.where(chunk == c, there, 0.0)
            if keep is not None:
                sums, found = jnp.where(keep, sums, 0.0), jnp.where(keep, found, 0.0)
            total[r : r + band] = sums
            picked[r : r + band] = found

    base = step * streams * span
    raw = product(0)
    absorb(before[...], base - span, step > 0)
    for n in range(1, streams):
        more = product(n)
        absorb(raw, base + (n - 1) * span)
        raw = more
    before[...] = raw

    @pl.when(step == pl.num_programs(0) - 1)
    def _():
        absorb(before[...], base + (streams - 1) * span)
        sums, found = total[...], picked[...]
        place = lax.broadcasted_iota(jnp.int32, sums.shape, 1)
        whole = jnp.sum(sums, axis=1, keepdims=True)
        both = jnp.where(place < picks, 30.0 * found, jnp.where(place == picks, whole, 0.0))
        out_ref[...] = both.T[: out_ref.shape[0]]


def score_part(places, pieces, embedding, ids, picks):
    rows = ids.shape[0]
    vocab, depth = embedding.shape
    span, streams = min(512, vocab), 1
    lines = -(-(picks + 1) // 8) * 8
    fixed = lambda i, places: (0, 0)
    return pl.pallas_call(
        functools.partial(score_kernel, picks, streams),
        out_shape=jax.ShapeDtypeStruct((lines, rows), jnp.float32),
        grid_spec=pltpu.PrefetchScalarGridSpec(
            num_scalar_prefetch=1,
            grid=(vocab // (span * streams),),
            in_specs=[pl.BlockSpec((rows, LANES), fixed)]
            + [pl.BlockSpec(piece.shape, fixed) for piece in pieces]
            + [
                pl.BlockSpec(
                    (span, depth // 2), lambda i, places, n=n, k=k: (i * streams + n, k)
                )
                for n in range(streams)
                for k in range(2)
            ],
            out_specs=pl.BlockSpec((lines, rows), fixed),
            scratch_shapes=[pltpu.VMEM((rows, depth), jnp.bfloat16)]
            + [pltpu.VMEM((rows, LANES), jnp.float32)] * 2
            + [pltpu.VMEM((rows, span), jnp.float32)],
        ),
        compiler_params=limit(32),
        cost_estimate=pl.CostEstimate(
            flops=2 * rows * depth * vocab,
            bytes_accessed=2 * vocab * depth,
            transcendentals=2 * rows * vocab,
        ),
        name="score_part",
    )(places, ids, *pieces, *[pin(embedding)] * (2 * streams))


def draft_kernel(meta, hidden_hbm, weight_hbm, *refs):
    outs, base_ref, columns, padded, sems = refs[:4], *refs[4:]
    depth = weight_hbm.shape[1]
    half = padded.shape[2]
    window = padded.shape[1]
    first = pl.multiple_of(meta[0], LANES)
    ask = pltpu.make_async_copy(hidden_hbm.at[:, pl.ds(first, window)], columns, sems.at[4])
    ask.start()
    padded[...] = jnp.zeros_like(padded)
    copies = []
    for k in (1, 2, 3, 0):
        quad = meta[2 + k]
        col = pl.multiple_of((quad & 1) * half, LANES)
        copies.append(
            pltpu.make_async_copy(
                weight_hbm.at[quad >> 1, :, pl.ds(col, half)],
                padded.at[k, pl.ds(pl.multiple_of(meta[1], 16), depth)],
                sems.at[k],
            )
        )
        copies[-1].start()
    base_columns = pl.ds(pl.multiple_of(meta[6], LANES), half)
    base = pltpu.make_async_copy(hidden_hbm.at[:, base_columns], base_ref, sems.at[5])
    base.start()
    ask.wait()
    for n, k in enumerate((1, 2, 3, 0)):
        copies[n].wait()
        partial = jnp.dot(columns[...], padded[k], preferred_element_type=jnp.float32)
        outs[k][...] = partial.astype(outs[k].dtype)
    base.wait()


def draft_part(hidden, medusa_w, blk, mp):
    rows, model = hidden.shape
    depth, units = medusa_w.shape[1:]
    half = units // 2
    window = -(-depth // LANES) * LANES + LANES
    start = blk * depth
    first = jnp.minimum(start // LANES * LANES, model - window)
    meta = [first, start - first] + [(blk & 3) ^ k for k in range(4)]
    meta = jnp.stack(meta + [mp * units + (blk & 1) * half])
    return pl.pallas_call(
        draft_kernel,
        out_shape=[
            jax.ShapeDtypeStruct((rows, half), jnp.bfloat16 if k else jnp.float32)
            for k in range(5)
        ],
        in_specs=[in_smem(), in_hbm(), in_hbm()],
        out_specs=[in_vmem()] * 5,
        scratch_shapes=[
            pltpu.VMEM((rows, window), jnp.bfloat16),
            pltpu.VMEM((4, window, half), jnp.bfloat16),
            pltpu.SemaphoreType.DMA((6,)),
        ],
        compiler_params=limit(16),
        name="draft_part",
    )(meta, pin(hidden), pin(medusa_w))


def fold_kernel(place, base_ref, own_ref, *refs):
    got, chunk_ref, outs, hold = refs[:3], refs[3], refs[4:-1], refs[-1]
    height = hold.shape[1]

    def cut(whole):
        for j in range(len(outs)):
            hold[j] = whole[j * height : (j + 1) * height]

    cut(base_ref[...].astype(jnp.float32))
    chunk_ref[...] = hold[place[0]]
    total = own_ref[...]
    for one in got:
        total = total + one[...].astype(jnp.float32)
    cut(total)
    for k, out in enumerate(outs):
        out[...] = hold[place[0] ^ k].astype(out.dtype)


def fold_part(base, own, got, place, layers):
    rows, half = own.shape
    height = rows // layers
    kinds = [jnp.float32, jnp.float32] + [jnp.bfloat16] * (layers - 1)
    return pl.pallas_call(
        fold_kernel,
        out_shape=[jax.ShapeDtypeStruct((height, half), kind) for kind in kinds],
        in_specs=[in_smem()] + [in_vmem()] * 5,
        out_specs=[in_vmem()] * (1 + layers),
        scratch_shapes=[pltpu.VMEM((layers, height, half), jnp.float32)],
        compiler_params=limit(16),
        name="fold_part",
    )(place, base, own, *got)


def stack_kernel(place, *refs):
    parts, out_ref, hold, flat = refs[:-3], refs[-3], refs[-2], refs[-1]
    height = hold.shape[1]
    for k, part in enumerate(parts):
        hold[place[0] ^ k] = part[...].astype(jnp.float32)
    for j in range(len(parts)):
        flat[j * height : (j + 1) * height, :] = hold[j]
    out_ref[...] = flat[...].astype(jnp.bfloat16)


def stack_part(parts, place):
    layers = len(parts)
    height, half = parts[0].shape
    return pl.pallas_call(
        stack_kernel,
        out_shape=jax.ShapeDtypeStruct((layers * height, half), jnp.bfloat16),
        in_specs=[in_smem()] + [in_vmem()] * layers,
        out_specs=in_vmem(),
        scratch_shapes=[
            pltpu.VMEM((layers, height, half), jnp.float32),
            pltpu.VMEM((layers * height, half), jnp.float32),
        ],
        compiler_params=limit(16),
        name="stack_part",
    )(place, *parts)


def partner(value, axis, size, bits):
    return lax.ppermute(value, axis, [(i, i ^ bits) for i in range(size)])


def group_sum(value, axis, size, stride, count, beside=None):
    values = [value] + [partner(value, axis, size, k * stride) for k in range(1, count)]
    if beside is not None:
        values, _ = lax.optimization_barrier((values, beside))
    while len(values) > 1:
        values = [values[i] + values[i + 1] for i in range(0, len(values), 2)]
    return values[0]


def both_by_stages(parts, parents, blocks, blk, mp, prompt, merge):
    layers = blocks // 4
    place = (blk // 4).reshape(1)
    got = [partner(parts[k], "blk", blocks, k) for k in range(1, 4)]
    got, sent = lax.optimization_barrier((got, prompt()))
    parts = fold_part(parts[4], parts[0], got, place, layers)
    parts, parents, sent = lax.optimization_barrier((parts, parents, sent))
    partials = spread(sent)
    more = [partner(parts[1 + k], "blk", blocks, 4 * k) for k in range(1, layers)]
    more, heads_out = lax.optimization_barrier((more, merge(partials, parents)))
    inner = parts[1] + sum(one.astype(jnp.float32) for one in more)
    own = (parts[0] + jax.nn.silu(inner)).astype(jnp.bfloat16)
    own, heads_out = lax.optimization_barrier((own, heads_out))
    chunks = [own] + [partner(own, "blk", blocks, 4 * k) for k in range(1, layers)]
    quad = stack_part(chunks, place)
    pieces = [quad] + [partner(quad, "blk", blocks, k) for k in range(1, 4)]
    pieces = pieces + [partner(piece, "mp", 2, 1) for piece in pieces]
    places = []
    for side in (mp, 1 - mp):
        for k in range(4):
            which = (blk & 3) ^ k
            places += [which >> 1, side * 2 + (which & 1)]
    return pieces, jnp.stack(places), spread(heads_out)


def spread(value):
    return lax.all_to_all(value, "blk", 0, 0, tiled=True)


def fresh_by_collectives(hidden, medusa_w, blocks, blk, mp):
    drafts, depth, units = medusa_w.shape
    rows = hidden.shape[0]
    own = drafts * rows // blocks
    hidden_cols = lax.dynamic_slice_in_dim(hidden, blk * depth, depth, 1)
    partial = jnp.einsum("rd,mdu->mru", hidden_cols, medusa_w, preferred_element_type=jnp.float32)
    partial = partial.reshape(blocks, own, units).astype(jnp.bfloat16)
    inner = lax.psum_scatter(partial, "blk", scatter_dimension=0).astype(jnp.float32)
    base = lax.dynamic_slice(hidden, ((blk * own) % rows, mp * units), (own, units))
    fresh = (base.astype(jnp.float32) + jax.nn.silu(inner)).astype(jnp.bfloat16)
    fresh = lax.all_gather(fresh, "blk", axis=0, tiled=True)
    return [lax.all_gather(fresh, "mp", axis=1, tiled=True)]


def per_device(
    hidden,
    medusa_w,
    embedding,
    cand_ids,
    tree_q,
    tree_key_value,
    prompt_key_value,
    block_group,
    block_len,
    block_empty,
    parents,
    out_weight,
    post_gain,
    resid,
):
    blocks, splits = lax.axis_size("blk"), lax.axis_size("mp")
    blk, mp = lax.axis_index("blk"), lax.axis_index("mp")
    drafts, depth, units = medusa_w.shape
    rows, model = hidden.shape
    lines = drafts * rows

    groups, tree_size, features = tree_q.shape
    width = features // blocks
    meta = jnp.concatenate([block_group, block_len, block_empty])

    def prompt():
        return prompt_part(tree_q, prompt_key_value, meta, width, blocks)

    def merge(partials, parents):
        numer, denom = tree_part(tree_q, tree_key_value, parents, blk * width, width)
        return merge_part(partials, numer, denom)

    if splits == 2 and blocks % 4 == 0 and units % 256 == 0 and drafts == 2:
        parts = draft_part(hidden, medusa_w, blk, mp)
        parts, meta = lax.optimization_barrier((parts, meta))
        pieces, places, heads_out = both_by_stages(
            parts, parents, blocks, blk, mp, prompt, merge
        )
    else:
        pieces = fresh_by_collectives(hidden, medusa_w, blocks, blk, mp)
        places = jnp.zeros((2,), jnp.int32)
        heads_out = spread(merge(spread(prompt()), parents))
    vocab = embedding.shape[0]
    picks = cand_ids.shape[2]
    ids = cand_ids.reshape(lines, picks) - (blk * splits + mp) * vocab
    ids = jnp.pad(ids, ((0, 0), (0, LANES - picks)), constant_values=-1)
    score = score_part(places, pieces, embedding, ids, picks)
    score = group_sum(score, "mp", splits, 1, splits)
    score, heads_out = lax.optimization_barrier((score, heads_out))
    attn = project_part(heads_out, out_weight)
    score = group_sum(score, "blk", blocks, 1, 4, attn)
    score = group_sum(score, "blk", blocks, 4, blocks // 4)
    draft_logprob = score[:picks] - jnp.log(score[picks : picks + 1])
    draft_logprob = draft_logprob.T.reshape(drafts, rows, picks)

    attn = group_sum(attn, "mp", splits, 1, splits)
    normed = attn * lax.rsqrt(jnp.mean(attn * attn, -1, keepdims=True) + 1e-06) * post_gain
    layer_out = (normed + resid.astype(jnp.float32)).astype(jnp.bfloat16)
    return (draft_logprob, layer_out)


def solution(mesh):
    placed = (
        P(),
        P(None, "blk", "mp"),
        P(("blk", "mp"), None),
        P(),
        P(None, None, "mp"),
        P(None, None, None, "mp"),
        P(None, "blk", None, "mp"),
        P("blk"),
        P("blk"),
        P("blk"),
        P(),
        P("mp", None),
        P(),
        P("blk", None),
    )
    return jax.shard_map(
        per_device, mesh=mesh, in_specs=placed, out_specs=(P(), P("blk", None)), check_vma=False
    )
```
